32 devices in a mesh: wide: 8 (over y, x, core), narrow: 4 (over z).
Axes of the slice: x: 2, y: 2, z: 4, core: 2. Of those that a mesh axis runs over, the one named last changes fastest.
Arguments:
- tokens: bfloat16 [16384, 1024], P(('narrow', 'wide')), may hold values from -6 to 6
- hidden_patch: int32 [16384], P(('narrow', 'wide')), may hold values from 0 to 1, as said below
- segment_ids: int32 [16384], P(('narrow', 'wide')), may hold values from 0 to 1, as said below
- rel_ids: int32 [16384, 512], P(('narrow', 'wide')), may hold values from 0 to 31
- layout_ids: int32 [16384, 512], P(('narrow', 'wide')), may hold values from 0 to 63
- w_query: float32 [1024, 1024], P(('narrow', 'wide')), may hold values from -0.03125 to 0.03125
- w_key: float32 [1024, 1024], P(('narrow', 'wide')), may hold values from -0.1875 to 0.1875
- w_value: float32 [1024, 1024], P(('narrow', 'wide')), may hold values from -0.1875 to 0.1875
- w_out: float32 [1024, 1024], P(('narrow', 'wide')), may hold values from -1 to 1
- w_gate: float32 [1024, 2816], P(('narrow', 'wide')), may hold values from -0.1875 to 0.1875
- w_up: float32 [1024, 2816], P(('narrow', 'wide')), may hold values from -0.1875 to 0.1875
- w_down: float32 [2816, 1024], P(('narrow', 'wide')), may hold values from -0.109375 to 0.109375
- gain_attn: float32 [1024], P(('narrow', 'wide')), may hold values from 0.5 to 1.5
- gain_ffn: float32 [1024], P(('narrow', 'wide')), may hold values from 0.5 to 1.5
- mask_embed: float32 [1024], P(('narrow', 'wide')), may hold values from -6 to 6
- rel_table: float32 [512], P(('narrow', 'wide')), may hold values from -3 to 3
- layout_table: float32 [1024], P(('narrow', 'wide')), may hold values from -3 to 3
- cotangent: bfloat16 [16384, 1024], P(('narrow', 'wide')), may hold values from -6 to 6
Outputs:
- output: bfloat16 [16384, 1024], P(('narrow', 'wide'))
- tokens_grad: float32 [16384, 1024], P(('narrow', 'wide'))
- w_query_grad: float32 [1024, 1024], P(('narrow', 'wide'))
- w_key_grad: float32 [1024, 1024], P(('narrow', 'wide'))
- w_value_grad: float32 [1024, 1024], P(('narrow', 'wide'))
- w_out_grad: float32 [1024, 1024], P(('narrow', 'wide'))
- w_gate_grad: float32 [1024, 2816], P(('narrow', 'wide'))
- w_up_grad: float32 [1024, 2816], P(('narrow', 'wide'))
- w_down_grad: float32 [2816, 1024], P(('narrow', 'wide'))
- gain_attn_grad: float32 [1024], P(('narrow', 'wide'))
- gain_ffn_grad: float32 [1024], P(('narrow', 'wide'))
- mask_embed_grad: float32 [1024], P(('narrow', 'wide'))
- rel_table_grad: float32 [512], P(('narrow', 'wide'))
- layout_table_grad: float32 [1024], P(('narrow', 'wide'))
The draws below stay inside these ranges and needn't reach their ends.
Inputs may be any that keep to these rules, and one draw needn't show every extreme that they name: `hidden_patch`: each page is 512 consecutive rows; its first 256 rows are text and never hidden; of its last 256 rows exactly 192 are hidden. `segment_ids`: constant over each aligned run of 128 rows; 0 at the first row of each device's 512 rows; from run to run it rises by 0 or 1, and only where a page begins or in the middle of a page's text, so that each segment holds text rows. `rel_ids`: column j is the j-th row of the query row's own device. `layout_ids`: column j is the j-th row of the query row's own device.
All inputs are finite; a program needn't handle non-finite values.
Results may differ from the reference program's by a relative error of at most 0.014.
The reference program's roundings to bfloat16 on the way count: a program that leaves them out, or rounds other values in their place, can miss the bound.
Values may be sent and summed in bfloat16 or wider, within the bound.
No kernel may reach another device: no remote copies, remote signals or barrier semaphores. Data moves between devices by JAX's collectives and lax.ppermute only.
A program may use at most 256 MiB of HBM per device.

```python
import jax
import jax.numpy as jnp
from jax import lax

D = 1024
H = 16
HD = 64
FF = 2816
NB_REL = 32
NB_LAY = 64
PAGE = 512
TEXT = 256
PATCHES = 256
HIDE = 192
PAGES_DEV = 1
TOK_DEV = 512
TOKENS = 16384


def draw_hidden_patch(key, part):
    key = jax.random.fold_in(key, 11)
    pages = TOKENS // PAGE
    page_keys = jax.random.split(key, pages)
    orders = jax.vmap(lambda k: jax.random.permutation(k, PATCHES))(page_keys)
    hidden = (orders < HIDE).astype(jnp.int32)
    text_rows = jnp.zeros((pages, TEXT), jnp.int32)
    return jnp.concatenate([text_rows, hidden], axis=1).reshape(TOKENS).astype(jnp.int32)


def draw_segment_ids(key, part):
    key = jax.random.fold_in(key, 23)
    groups = TOKENS // TOK_DEV
    runs_dev = PAGES_DEV * 4
    begins = jax.random.randint(key, (groups, runs_dev), 0, 2).astype(jnp.int32)
    run_index = jnp.arange(runs_dev, dtype=jnp.int32)[None, :]
    allowed = (run_index % 4 == 0) | (run_index % 4 == 1)
    first_group = jnp.arange(groups, dtype=jnp.int32)[:, None] == 0
    forced = (run_index == 0) | first_group & allowed
    begins = jnp.where(allowed, jnp.where(forced, 1, begins), 0).astype(jnp.int32)
    numbers = jnp.cumsum(begins, axis=1) - 1
    return jnp.repeat(numbers, PAGE // 4, axis=1).reshape(TOKENS).astype(jnp.int32)


def place_ends(drawn, key, smallest, high):
    index_at = [jax.random.randint(jax.random.fold_in(key, axis), (), 0, length) for axis, length in enumerate(drawn.shape)]
    widest = drawn.shape.index(max(drawn.shape))
    beside = index_at[:widest] + [(index_at[widest] + 1) % drawn.shape[widest]] + index_at[widest + 1:]
    return drawn.at[tuple(index_at)].set(smallest).at[tuple(beside)].set(high)


def shard_levels(key, shape, shards, low, high):
    loudness, own = 1.0, jax.random.fold_in(key, 6)
    for dim, shards_of in shards:
        heights = jnp.exp(jax.random.uniform(jax.random.fold_in(own, dim), (shards_of,), jnp.float32, low / len(shards), high / len(shards)))
        loudness = loudness * jnp.repeat(heights, shape[dim] // shards_of).reshape([-1 if axis == dim else 1 for axis in range(len(shape))])
    return loudness


def bell_draw(own_key, extent, width, limit, cuts=(), kind=jnp.bfloat16):
    entries = width * jax.random.normal(own_key, extent, jnp.float32)
    if cuts:
        entries = entries * shard_levels(own_key, extent, cuts, -0.22, 0.18)
    return jnp.clip(entries, -limit, limit).astype(kind)


def setup_inputs(seed: int = 0) -> dict:
    key_list = jax.random.split(jax.random.key(seed), 19)
    tokens = bell_draw(key_list[0], (TOKENS, D), 1.0, 6.0, ((0, 32),))
    hidden_patch = draw_hidden_patch(jax.random.fold_in(key_list[18], 71), 0)
    segment_ids = draw_segment_ids(jax.random.fold_in(key_list[18], 71), 0)
    rel_ids = place_ends(jax.random.randint(key_list[3], (TOKENS, TOK_DEV), 0, NB_REL), jax.random.fold_in(key_list[3], 1), 0, NB_REL - 1).astype(jnp.int32)
    layout_ids = place_ends(jax.random.randint(key_list[4], (TOKENS, TOK_DEV), 0, NB_LAY), jax.random.fold_in(key_list[4], 1), 0, NB_LAY - 1).astype(jnp.int32)
    w_query = bell_draw(key_list[5], (D, D), (32 * D) ** -0.5, 0.03125, ((0, 32),), jnp.float32)
    w_key = bell_draw(key_list[6], (D, D), D ** -0.5, 0.1875, ((0, 32),), jnp.float32)
    w_value = bell_draw(key_list[7], (D, D), D ** -0.5, 0.1875, ((0, 32),), jnp.float32)
    w_out = bell_draw(key_list[8], (D, D), (D // 32) ** -0.5, 1.0, ((0, 32),), jnp.float32)
    w_gate = bell_draw(key_list[9], (D, FF), D ** -0.5, 0.1875, ((0, 32),), jnp.float32)
    w_up = bell_draw(key_list[10], (D, FF), D ** -0.5, 0.1875, ((0, 32),), jnp.float32)
    w_down = bell_draw(key_list[11], (FF, D), FF ** -0.5, 0.109375, ((0, 32),), jnp.float32)
    gain_attn = jnp.clip(1.0 + 0.1 * jax.random.normal(key_list[12], (D,), jnp.float32), 0.5, 1.5)
    gain_ffn = jnp.clip(1.0 + 0.1 * jax.random.normal(key_list[13], (D,), jnp.float32), 0.5, 1.5)
    mask_embed = bell_draw(key_list[14], (D,), 1.0, 6.0, ((0, 32),), jnp.float32)
    rel_table = bell_draw(key_list[15], (NB_REL * H,), 0.5, 3.0, ((0, 32),), jnp.float32)
    layout_table = bell_draw(key_list[16], (NB_LAY * H,), 0.5, 3.0, ((0, 32),), jnp.float32)
    cotangent = bell_draw(key_list[17], (TOKENS, D), 1.0, 6.0, ((0, 32),))
    return {"tokens": tokens, "hidden_patch": hidden_patch, "segment_ids": segment_ids, "rel_ids": rel_ids, "layout_ids": layout_ids, "w_query": w_query, "w_key": w_key, "w_value": w_value, "w_out": w_out, "w_gate": w_gate, "w_up": w_up, "w_down": w_down, "gain_attn": gain_attn, "gain_ffn": gain_ffn, "mask_embed": mask_embed, "rel_table": rel_table, "layout_table": layout_table, "cotangent": cotangent}


@jax.custom_vjp
def low(v):
    return lax.optimization_barrier(v.astype(jnp.bfloat16)).astype(jnp.float32)

@jax.custom_vjp
def low_back(v):
    return v

def low_keep(v):
    return (low(v), None)

def low_pass(kept, grad):
    return (grad,)

def back_keep(v):
    return (v, None)

def back_low(kept, grad):
    return (low(grad),)
low.defvjp(low_keep, low_pass)
low_back.defvjp(back_keep, back_low)
eps_norm = 1e-06
neg_large = -1e+30

def normalize(v):
    return v * lax.rsqrt(lax.optimization_barrier(jnp.mean(v * v, axis=-1, keepdims=True)) + eps_norm)

def matmul(left, right):
    return jnp.dot(left, right, precision=lax.Precision.HIGHEST, preferred_element_type=jnp.float32)

def device_layer(pieces, params):
    rows_in, hidden_rows, segment_rows, rel_rows, layout_rows = pieces
    lowered = [low(param) for param in params]
    query_weight, key_weight, value_weight, out_weight = (lowered[0], lowered[1], lowered[2], lowered[3])
    gate_weight, up_weight, down_weight = (lowered[4], lowered[5], lowered[6])
    attn_gain, ffn_gain, embed_row, rel_bias, layout_bias = (lowered[7], lowered[8], lowered[9], lowered[10], lowered[11])
    row_count = rows_in.shape[0]
    embedded = jnp.where(hidden_rows[:, None] == 1, embed_row[None, :], rows_in)
    attn_input = low(normalize(embedded) * attn_gain)
    queries = low_back(low(matmul(attn_input, query_weight))).reshape(row_count, H, HD)
    key_rows = low_back(low(matmul(attn_input, key_weight))).reshape(row_count, H, HD)
    value_rows = low_back(low(matmul(attn_input, value_weight))).reshape(row_count, H, HD)
    bias_sum = rel_bias.reshape(NB_REL, H)[rel_rows] + layout_bias.reshape(NB_LAY, H)[layout_rows]
    raw_scores = jnp.einsum('ihd,jhd->ihj', queries, key_rows, precision=lax.Precision.HIGHEST) + jnp.swapaxes(bias_sum, 1, 2)
    scores = low_back(raw_scores)
    valid_keys = (segment_rows[:, None] == segment_rows[None, :]) & (hidden_rows[None, :] == 0)
    masked = jnp.where(valid_keys[:, None, :], scores, neg_large)
    row_max = lax.optimization_barrier(jnp.max(masked, axis=-1, keepdims=True))
    exponent = jnp.exp(masked - row_max)
    probs = exponent / lax.optimization_barrier(jnp.sum(exponent, axis=-1, keepdims=True))
    attended = jnp.einsum('ihj,jhd->ihd', low(probs), value_rows, precision=lax.Precision.HIGHEST)
    attended = low_back(low(attended)).reshape(row_count, H * HD)
    residual = embedded + low_back(matmul(attended, out_weight))
    ffn_input = low(normalize(residual) * ffn_gain)
    gate_proj = low_back(matmul(ffn_input, gate_weight))
    up_proj = low_back(matmul(ffn_input, up_weight))
    activated = low(jax.nn.gelu(gate_proj, approximate=True) * up_proj)
    return residual + low_back(matmul(activated, down_weight))

def reference(tokens, hidden_patch, segment_ids, rel_ids, layout_ids, w_query, w_key, w_value, w_out, w_gate, w_up, w_down, gain_attn, gain_ffn, mask_embed, rel_table, layout_table, cotangent):
    groups = tokens.shape[0] // TOK_DEV
    hidden_groups = hidden_patch.reshape(groups, TOK_DEV)
    segment_groups = segment_ids.reshape(groups, TOK_DEV)
    rel_groups = rel_ids.reshape(groups, TOK_DEV, TOK_DEV)
    layout_groups = layout_ids.reshape(groups, TOK_DEV, TOK_DEV)
    inputs = tokens.astype(jnp.float32).reshape(groups, TOK_DEV, D)

    def forward(rows_all, *params):

        def one_group(pieces):
            return device_layer(pieces, params)
        stacked = lax.map(jax.checkpoint(one_group), (rows_all, hidden_groups, segment_groups, rel_groups, layout_groups))
        return stacked.reshape(groups * TOK_DEV, D)
    result, pull = jax.vjp(forward, inputs, w_query, w_key, w_value, w_out, w_gate, w_up, w_down, gain_attn, gain_ffn, mask_embed, rel_table, layout_table)
    grads = pull(cotangent.astype(jnp.float32))
    return (result.astype(jnp.bfloat16), grads[0].reshape(groups * TOK_DEV, D), grads[1], grads[2], grads[3], grads[4], grads[5], grads[6], grads[7], grads[8], grads[9], grads[10], grads[11], grads[12])
```

```python
import jax
import jax.numpy as jnp
from jax import lax
from jax.sharding import PartitionSpec as P

H = 16
HD = 64


eps_norm = 1e-06
neg_large = -1e30


def normalize(v):
    return v * lax.rsqrt(jnp.mean(v * v, axis=-1, keepdims=True) + eps_norm)


def shift_narrow(x, step, count):
    return lax.ppermute(x, "narrow", [(i, (i + step) % count) for i in range(count)])


def flip_wide(x, bits, count):
    return lax.ppermute(x, "wide", [(i, i ^ bits) for i in range(count)])


def gather_blocks(x, narrow, wide):
    column = jnp.stack([x] + [shift_narrow(x, s, narrow) for s in range(1, narrow)])
    plane = jnp.stack([column] + [flip_wide(column, 2 * b, wide) for b in range(1, wide // 2)])
    return jnp.stack([plane, flip_wide(plane, 1, wide)])


def gather_rows(x, narrow, wide):
    blocks = gather_blocks(x, narrow, wide).reshape((narrow * wide,) + x.shape)
    z, w = jnp.meshgrid(jnp.arange(narrow), jnp.arange(wide), indexing="ij")
    flip = w ^ lax.axis_index("wide")
    shift = (lax.axis_index("narrow") - z) % narrow
    order = ((flip & 1) * (wide // 2) + (flip >> 1)) * narrow + shift
    return blocks[order.reshape(-1)]


def scatter_rows(parts, narrow, wide):
    core, chip, shift = jnp.meshgrid(
        jnp.arange(2), jnp.arange(wide // 2), jnp.arange(narrow), indexing="ij"
    )
    w = (chip * 2 + core) ^ lax.axis_index("wide")
    z = (lax.axis_index("narrow") + shift) % narrow
    parts = parts[(z * wide + w).reshape(-1)].reshape(
        (2, wide // 2, narrow) + parts.shape[1:]
    )
    low, high = jnp.bfloat16, jnp.float32
    mine = parts[0].astype(high) + flip_wide(parts[1], 1, wide).astype(high)
    mine = mine.astype(low)
    total = mine[0].astype(high)
    for b in range(1, wide // 2):
        total = total + flip_wide(mine[b], 2 * b, wide).astype(high)
    mine = total.astype(low)
    total = mine[0].astype(high)
    for s in range(1, narrow):
        total = total + shift_narrow(mine[s], s, narrow).astype(high)
    return total


def collect(stored, narrow, wide):
    lowered = [param.astype(jnp.bfloat16) for param in stored]
    small = jnp.concatenate(lowered[7:])[None]
    small = gather_rows(small, narrow, wide)[:, 0]
    sizes = [param.shape[0] for param in stored[7:]]
    pieces, at = [], 0
    for size in sizes:
        pieces.append(small[:, at : at + size].reshape(-1))
        at += size
    return [
        gather_rows(param, narrow, wide).reshape(-1, param.shape[1]) for param in lowered[:7]
    ] + pieces


def reduce_grads(parts, narrow, wide):
    count = narrow * wide
    small = jnp.concatenate([part.reshape(count, -1) for part in parts[7:]], axis=1)
    sizes = [part.shape[0] // count for part in parts[7:]]
    big = [
        scatter_rows(part.astype(jnp.bfloat16).reshape(count, -1, part.shape[1]), narrow, wide)
        for part in parts[:7]
    ]
    small = scatter_rows(small.astype(jnp.bfloat16)[:, None], narrow, wide)[0]
    pieces, at = [], 0
    for size in sizes:
        pieces.append(small[at : at + size])
        at += size
    return big + pieces


def local(
    tokens,
    hidden_patch,
    segment_ids,
    rel_ids,
    layout_ids,
    w_query,
    w_key,
    w_value,
    w_out,
    w_gate,
    w_up,
    w_down,
    gain_attn,
    gain_ffn,
    mask_embed,
    rel_table,
    layout_table,
    cotangent,
):
    stored = (
        w_query,
        w_key,
        w_value,
        w_out,
        w_gate,
        w_up,
        w_down,
        gain_attn,
        gain_ffn,
        mask_embed,
        rel_table,
        layout_table,
    )
    narrow, wide = lax.axis_size("narrow"), lax.axis_size("wide")
    gathered = collect(stored, narrow, wide)
    row_count = tokens.shape[0]
    block = min(512, row_count)
    sub_rows = min(128, block)
    starts = jnp.arange(row_count // block, dtype=jnp.int32) * block
    offsets = jnp.arange(block // sub_rows, dtype=jnp.int32) * sub_rows
    hidden_rows = hidden_patch == 1
    visible_keys = jnp.logical_not(hidden_rows)

    def one_hot(start, offset, rel_count, lay_count):
        rel_part = lax.dynamic_slice_in_dim(rel_ids, start + offset, sub_rows, 0)
        lay_part = lax.dynamic_slice_in_dim(layout_ids, start + offset, sub_rows, 0)
        rel_hot = (
            rel_part[:, :, None] == jnp.arange(rel_count, dtype=jnp.int32)[None, None, :]
        ).astype(jnp.bfloat16)
        lay_hot = (
            lay_part[:, :, None] == jnp.arange(lay_count, dtype=jnp.int32)[None, None, :]
        ).astype(jnp.bfloat16)
        return (rel_hot, lay_hot)

    def block_scores(start, queries, key_rows, rel_rows, lay_rows):

        def piece(offset):
            rel_hot, lay_hot = one_hot(start, offset, rel_rows.shape[0], lay_rows.shape[0])
            return jnp.einsum(
                "ijb,bh->ihj", rel_hot, rel_rows, preferred_element_type=jnp.float32
            ) + jnp.einsum("ijb,bh->ihj", lay_hot, lay_rows, preferred_element_type=jnp.float32)

        bias_sum = lax.map(piece, offsets).reshape(block, H, row_count)
        raw_scores = (
            jnp.einsum("ihd,jhd->ihj", queries, key_rows, preferred_element_type=jnp.float32)
            + bias_sum
        )
        valid_keys = (segment_ids[:, None] == segment_ids[None, :]) & visible_keys[None, :]
        return (jnp.where(valid_keys[:, None, :], raw_scores, neg_large), queries)

    query_weight, key_weight, value_weight, out_weight, gate_weight, up_weight, down_weight = (
        gathered[:7]
    )
    attn_gain = gathered[7].astype(jnp.float32)
    ffn_gain = gathered[8].astype(jnp.float32)
    embed_row = gathered[9].astype(jnp.float32)
    rel_rows = gathered[10].reshape(-1, H)
    lay_rows = gathered[11].reshape(-1, H)
    embedded = jnp.where(hidden_rows[:, None], embed_row[None, :], tokens.astype(jnp.float32))
    normed_attn = normalize(embedded)
    attn_input = (normed_attn * attn_gain).astype(jnp.bfloat16)
    queries = (
        jnp.dot(attn_input, query_weight, preferred_element_type=jnp.float32)
        .astype(jnp.bfloat16)
        .reshape(row_count, H, HD)
    )
    key_rows = (
        jnp.dot(attn_input, key_weight, preferred_element_type=jnp.float32)
        .astype(jnp.bfloat16)
        .reshape(row_count, H, HD)
    )
    value_rows = (
        jnp.dot(attn_input, value_weight, preferred_element_type=jnp.float32)
        .astype(jnp.bfloat16)
        .reshape(row_count, H, HD)
    )

    def forward_block(start):
        masked, query_part = block_scores(start, queries, key_rows, rel_rows, lay_rows)
        row_max = jnp.max(masked, axis=-1, keepdims=True)
        exponent = jnp.exp(masked - row_max)
        total = jnp.sum(exponent, axis=-1, keepdims=True)
        probs = (exponent / total).astype(jnp.bfloat16)
        attended = jnp.einsum(
            "ihj,jhd->ihd", probs, value_rows, preferred_element_type=jnp.float32
        ).astype(jnp.bfloat16)
        return (attended, (row_max + jnp.log(total))[:, :, 0])

    attended, log_total = lax.map(forward_block, starts)
    attended = attended.reshape(row_count, H * HD)
    residual = embedded + jnp.dot(attended, out_weight, preferred_element_type=jnp.float32)
    normed_ffn = normalize(residual)
    ffn_input = (normed_ffn * ffn_gain).astype(jnp.bfloat16)
    gate_proj = jnp.dot(ffn_input, gate_weight, preferred_element_type=jnp.float32)
    up_proj = jnp.dot(ffn_input, up_weight, preferred_element_type=jnp.float32)
    activated = (jax.nn.gelu(gate_proj, approximate=True) * up_proj).astype(jnp.bfloat16)
    result = residual + jnp.dot(activated, down_weight, preferred_element_type=jnp.float32)
    second = gathered
    query_weight, key_weight, value_weight, out_weight, gate_weight, up_weight, down_weight = (
        second[:7]
    )
    rel_rows = second[10].reshape(-1, H)
    lay_rows = second[11].reshape(-1, H)
    down_part = jnp.einsum("tf,td->fd", activated, cotangent, preferred_element_type=jnp.float32)
    act_grad = jnp.einsum("td,fd->tf", cotangent, down_weight, preferred_element_type=jnp.float32)
    _, gelu_pull = jax.vjp(lambda a, b: jax.nn.gelu(a, approximate=True) * b, gate_proj, up_proj)
    gate_back, up_back = gelu_pull(act_grad)
    gate_back = gate_back.astype(jnp.bfloat16)
    up_back = up_back.astype(jnp.bfloat16)
    gate_part = jnp.einsum("td,tf->df", ffn_input, gate_back, preferred_element_type=jnp.float32)
    up_part = jnp.einsum("td,tf->df", ffn_input, up_back, preferred_element_type=jnp.float32)
    ffn_in_grad = jnp.einsum(
        "tf,df->td", gate_back, gate_weight, preferred_element_type=jnp.float32
    ) + jnp.einsum("tf,df->td", up_back, up_weight, preferred_element_type=jnp.float32)
    ffn_gain_part = jnp.sum(ffn_in_grad * normed_ffn, axis=0)
    _, ffn_norm_pull = jax.vjp(normalize, residual)
    residual_grad = cotangent.astype(jnp.float32) + ffn_norm_pull(ffn_in_grad * ffn_gain)[0]
    residual_low = residual_grad.astype(jnp.bfloat16)
    out_part = jnp.einsum("tk,td->kd", attended, residual_low, preferred_element_type=jnp.float32)
    head_grad = (
        jnp.einsum("td,kd->tk", residual_low, out_weight, preferred_element_type=jnp.float32)
        .astype(jnp.bfloat16)
        .reshape(row_count, H, HD)
    )

    def backward_block(carry, inputs):
        key_grad, value_grad, rel_grad, lay_grad = carry
        start, log_part = inputs
        masked, query_part = block_scores(start, queries, key_rows, rel_rows, lay_rows)
        probs = jnp.exp(masked - log_part[:, :, None])
        probs_low = probs.astype(jnp.bfloat16)
        prob_grad = jnp.einsum(
            "ihd,jhd->ihj", head_grad, value_rows, preferred_element_type=jnp.float32
        )
        center = jnp.sum(probs * prob_grad, axis=-1, keepdims=True)
        score_grad = (probs * (prob_grad - center)).astype(jnp.bfloat16)
        query_grad = jnp.einsum(
            "ihj,jhd->ihd", score_grad, key_rows, preferred_element_type=jnp.float32
        ).astype(jnp.bfloat16)
        key_grad = key_grad + jnp.einsum(
            "ihj,ihd->jhd", score_grad, query_part, preferred_element_type=jnp.float32
        )
        value_grad = value_grad + jnp.einsum(
            "ihj,ihd->jhd", probs_low, head_grad, preferred_element_type=jnp.float32
        )
        score_parts = score_grad.reshape(block // sub_rows, sub_rows, H, row_count)

        def table_piece(pieces):
            offset, grad_piece = pieces
            rel_hot, lay_hot = one_hot(start, offset, rel_rows.shape[0], lay_rows.shape[0])
            return (
                jnp.einsum("ijb,ihj->bh", rel_hot, grad_piece, preferred_element_type=jnp.float32),
                jnp.einsum("ijb,ihj->bh", lay_hot, grad_piece, preferred_element_type=jnp.float32),
            )

        rel_steps, lay_steps = lax.map(table_piece, (offsets, score_parts))
        return (
            (
                key_grad,
                value_grad,
                rel_grad + jnp.sum(rel_steps, axis=0),
                lay_grad + jnp.sum(lay_steps, axis=0),
            ),
            query_grad,
        )

    zeros_rows = jnp.zeros((row_count, H, HD), jnp.float32)
    initial = (
        zeros_rows,
        zeros_rows,
        jnp.zeros(rel_rows.shape, jnp.float32),
        jnp.zeros(lay_rows.shape, jnp.float32),
    )
    (key_grad, value_grad, rel_grad, lay_grad), query_grad = lax.scan(
        backward_block, initial, (starts, log_total)
    )
    query_low = query_grad.reshape(row_count, H * HD)
    key_low = key_grad.astype(jnp.bfloat16).reshape(row_count, H * HD)
    value_low = value_grad.astype(jnp.bfloat16).reshape(row_count, H * HD)
    query_part_w = jnp.einsum(
        "td,tk->dk", attn_input, query_low, preferred_element_type=jnp.float32
    )
    key_part_w = jnp.einsum("td,tk->dk", attn_input, key_low, preferred_element_type=jnp.float32)
    value_part_w = jnp.einsum(
        "td,tk->dk", attn_input, value_low, preferred_element_type=jnp.float32
    )
    attn_in_grad = (
        jnp.einsum("tk,dk->td", query_low, query_weight, preferred_element_type=jnp.float32)
        + jnp.einsum("tk,dk->td", key_low, key_weight, preferred_element_type=jnp.float32)
        + jnp.einsum("tk,dk->td", value_low, value_weight, preferred_element_type=jnp.float32)
    )
    attn_gain_part = jnp.sum(attn_in_grad * normed_attn, axis=0)
    _, attn_norm_pull = jax.vjp(normalize, embedded)
    embedded_grad = residual_grad + attn_norm_pull(attn_in_grad * attn_gain)[0]
    tokens_grad = jnp.where(hidden_rows[:, None], 0.0, embedded_grad)
    embed_part = jnp.sum(jnp.where(hidden_rows[:, None], embedded_grad, 0.0), axis=0)
    sums = reduce_grads(
        [
            query_part_w,
            key_part_w,
            value_part_w,
            out_part,
            gate_part,
            up_part,
            down_part,
            attn_gain_part,
            ffn_gain_part,
            embed_part,
            rel_grad.reshape(-1),
            lay_grad.reshape(-1),
        ],
        narrow,
        wide,
    )
    return (
        result.astype(jnp.bfloat16),
        tokens_grad,
        sums[0],
        sums[1],
        sums[2],
        sums[3],
        sums[4],
        sums[5],
        sums[6],
        sums[7],
        sums[8],
        sums[9],
        sums[10],
        sums[11],
    )


def solution(mesh):
    return jax.shard_map(
        local,
        mesh=mesh,
        in_specs=(
            P(("narrow", "wide"), None),
            P(("narrow", "wide")),
            P(("narrow", "wide")),
            P(("narrow", "wide"), None),
            P(("narrow", "wide"), None),
            P(("narrow", "wide"), None),
            P(("narrow", "wide"), None),
            P(("narrow", "wide"), None),
            P(("narrow", "wide"), None),
            P(("narrow", "wide"), None),
            P(("narrow", "wide"), None),
            P(("narrow", "wide"), None),
            P(("narrow", "wide")),
            P(("narrow", "wide")),
            P(("narrow", "wide")),
            P(("narrow", "wide")),
            P(("narrow", "wide")),
            P(("narrow", "wide"), None),
        ),
        out_specs=(
            P(("narrow", "wide"), None),
            P(("narrow", "wide"), None),
            P(("narrow", "wide"), None),
            P(("narrow", "wide"), None),
            P(("narrow", "wide"), None),
            P(("narrow", "wide"), None),
            P(("narrow", "wide"), None),
            P(("narrow", "wide"), None),
            P(("narrow", "wide"), None),
            P(("narrow", "wide")),
            P(("narrow", "wide")),
            P(("narrow", "wide")),
            P(("narrow", "wide")),
            P(("narrow", "wide")),
        ),
        check_vma=False,
    )
```

```python
import functools
import math

import jax
import jax.numpy as jnp
from jax import lax
from jax.experimental import pallas as pl
from jax.experimental.pallas import tpu as pltpu
from jax.sharding import PartitionSpec as P

H = 16
HD = 64
PAIRS = H // 2
NB_REL = 32
NB_LAY = 64
NB = NB_REL + NB_LAY
HIDE = 192
SPLIT = 1536
FF_STEP = 256

eps_norm = 1e-06
neg_large = -1e30
f32 = jnp.float32
bf16 = jnp.bfloat16

NN = (((1,), (0,)), ((), ()))
NT = (((1,), (1,)), ((), ()))
TN = (((0,), (0,)), ((), ()))


def dot(a, b, dims=NN):
    return lax.dot_general(a, b, dims, preferred_element_type=f32)


def params(mib=56):
    return pltpu.CompilerParams(vmem_limit_bytes=mib * 1024 * 1024)


def cost(flops, nbytes):
    return pl.CostEstimate(flops=int(flops), bytes_accessed=int(nbytes), transcendentals=0)


VM = pl.BlockSpec(memory_space=pltpu.VMEM)
SM = pl.BlockSpec(memory_space=pltpu.SMEM)
ANY = pl.BlockSpec(memory_space=pl.ANY)


def shift_narrow(x, step, count):
    return lax.ppermute(x, "narrow", [(i, (i + step) % count) for i in range(count)])


def flip_wide(x, bits, count):
    return lax.ppermute(x, "wide", [(i, i ^ bits) for i in range(count)])


def gather_blocks(x, narrow, wide):
    column = jnp.stack([x] + [shift_narrow(x, s, narrow) for s in range(1, narrow)])
    plane = jnp.stack([column] + [flip_wide(column, 2 * b, wide) for b in range(1, wide // 2)])
    return jnp.stack([plane, flip_wide(plane, 1, wide)])


def ordered(blocks, narrow, wide):
    flat = blocks.reshape((narrow * wide,) + blocks.shape[3:])
    z, w = jnp.meshgrid(jnp.arange(narrow), jnp.arange(wide), indexing="ij")
    flip = w ^ lax.axis_index("wide")
    shift = (lax.axis_index("narrow") - z) % narrow
    order = ((flip & 1) * (wide // 2) + (flip >> 1)) * narrow + shift
    return flat[order.reshape(-1)]


def scatter_blocks(parts, narrow, wide):
    mine = parts[0].astype(f32) + flip_wide(parts[1], 1, wide).astype(f32)
    return scatter_chips(mine.astype(bf16), narrow, wide)


def scatter_chips(mine, narrow, wide):
    total = mine[0].astype(f32)
    for b in range(1, wide // 2):
        total = total + flip_wide(mine[b], 2 * b, wide).astype(f32)
    return scatter_narrow(total.astype(bf16), narrow)


def scatter_narrow(mine, narrow):
    z0 = lax.axis_index("narrow")
    total = lax.dynamic_index_in_dim(mine, z0, 0, False).astype(f32)
    for s in range(1, narrow):
        sent = lax.dynamic_index_in_dim(mine, (z0 + s) % narrow, 0, False)
        total = total + shift_narrow(sent, s, narrow).astype(f32)
    return total


def block_rows(where, narrow, wide, index):
    core, rest = divmod(index, wide // 2 * narrow)
    chip, shift = divmod(rest, narrow)
    z = lax.rem(where[0] - shift + narrow, narrow)
    w = jnp.bitwise_xor(where[1], 2 * chip + core)
    return z, w, (core, chip, shift)


def load_rows(where, src, low, rows, lanes, dst, sem, narrow, wide):
    for index in range(narrow * wide):
        z, w, at = block_rows(where, narrow, wide, index)
        row = pl.multiple_of((z * wide + w) * rows, rows)
        pltpu.make_async_copy(
            src.at[at[0], at[1], at[2], pl.ds(low, rows), lanes],
            dst.at[pl.ds(row, rows), :],
            sem,
        ).start()


def wait_all(ref, sem):
    pltpu.make_async_copy(ref, ref, sem).wait()


def store_rows(where, src, dst, low, rows, sem, narrow, wide):
    for index in range(narrow * wide):
        z, w = divmod(index, wide)
        flip = jnp.bitwise_xor(where[1], w)
        row = (z * wide + w) * rows
        pltpu.make_async_copy(
            src.at[pl.ds(row, rows), :],
            dst.at[jnp.bitwise_and(flip, 1), lax.shift_right_logical(flip, 1), z, pl.ds(low, rows)],
            sem,
        ).start()


def prepare_kernel(hidden_ref, segment_ref, rel_ref, lay_ref, pick_ref, rel_out, lay_out):
    count = hidden_ref.shape[1]
    keys = pick_ref.shape[0]
    seen = hidden_ref[...] == 0
    before = lax.broadcasted_iota(jnp.int32, (count, count), 0)
    after = lax.broadcasted_iota(jnp.int32, (count, count), 1)
    upper = jnp.where(before <= after, 1.0, 0.0).astype(bf16)
    seen_rows = jnp.broadcast_to(jnp.where(seen, 1.0, 0.0), (16, count)).astype(bf16)
    rank = dot(seen_rows, upper)[0:1].astype(jnp.int32) - 1
    rank = jnp.where(seen, rank, -1)
    number = lax.broadcasted_iota(jnp.int32, (keys, count), 0)
    pick = jnp.where(number == rank, 1.0, 0.0).astype(bf16)
    pick_ref[...] = pick
    segment = jnp.broadcast_to(segment_ref[...].astype(f32), (16, count)).astype(bf16)
    key_segment = dot(pick, segment, NT)[:, 0:1]
    valid = key_segment == segment_ref[...].astype(f32)
    rel = dot(pick, rel_ref[...].astype(f32).astype(bf16), NT).astype(jnp.int32)
    lay = dot(pick, lay_ref[...].astype(f32).astype(bf16), NT).astype(jnp.int32)
    rel_out[...] = jnp.where(valid, rel, NB)
    lay_out[...] = lay + NB_REL


def bias_kernel(table_ref, rel_ref, lay_ref, out_ref):
    keys, count = rel_ref.shape
    groups = keys // 8
    pair = pl.program_id(0)
    tables = [
        jnp.broadcast_to(table_ref[pl.ds(2 * pair + side, 1), :], (keys, 128)) for side in range(2)
    ]
    for c in range(count // 128):
        lanes = slice(c * 128, c * 128 + 128)
        for side in range(2):
            found = jnp.take_along_axis(tables[side], rel_ref[:, lanes], axis=1)
            found = found + jnp.take_along_axis(tables[side], lay_ref[:, lanes], axis=1)
            out_ref[0, :, side * 8 : side * 8 + 8, lanes] = found.reshape(groups, 8, 128)


def embed(tokens_ref, hidden_ref, mask_ref):
    return jnp.where(hidden_ref[...] == 1.0, mask_ref[...], tokens_ref[...].astype(f32))


def inverse_rms(v):
    return lax.rsqrt(jnp.mean(v * v, axis=-1, keepdims=True) + eps_norm)


def project_kernel(
    narrow, wide, where, tokens_ref, hidden_ref, mask_ref, gain_ref, pick_ref, blocks_ref,
    input_ref, query_ref, key_ref, value_ref, weights, sems,
):
    width = tokens_ref.shape[1]
    rows = width // (narrow * wide)
    for n in range(3):
        load_rows(where, blocks_ref, n * rows, rows, slice(None), weights.at[n], sems.at[n], narrow, wide)
    embedded = embed(tokens_ref, hidden_ref, mask_ref)
    attn_input = (embedded * inverse_rms(embedded) * gain_ref[...]).astype(bf16)
    input_ref[...] = attn_input
    seen = dot(pick_ref[...], attn_input).astype(bf16)
    wait_all(weights.at[0], sems.at[0])
    query_ref[...] = dot(attn_input, weights[0]).astype(bf16)
    wait_all(weights.at[1], sems.at[1])
    key_ref[...] = dot(seen, weights[1]).astype(bf16)
    wait_all(weights.at[2], sems.at[2])
    value_ref[...] = dot(seen, weights[2]).astype(bf16)


def by_side(x):
    keys = x.shape[0]
    wide = x.astype(f32).reshape(keys // 8, 8, 128)
    left = lax.broadcasted_iota(jnp.int32, wide.shape, 2) < HD
    both = jnp.concatenate([jnp.where(left, wide, 0.0), jnp.where(left, 0.0, wide)], axis=1)
    return both.astype(bf16).reshape(keys * 2, 128)


def own_side(x):
    x = x.reshape(x.shape[0] // 16, 16, 128)
    left = lax.broadcasted_iota(jnp.int32, (x.shape[0], 8, 128), 2) < HD
    return jnp.where(left, x[:, 0:8], x[:, 8:16]).reshape(x.shape[0] * 8, 128)


def per_side(x, fold, spread):
    return jnp.concatenate(
        [
            jnp.broadcast_to(fold(x[side * 8 : side * 8 + 8], axis=0, keepdims=True), (8, spread))
            for side in range(2)
        ],
        axis=0,
    )[None]


def attend_kernel(query_ref, key_ref, value_ref, bias_ref, attended_ref, probs_ref):
    count = query_ref.shape[0]
    keys = key_ref.shape[0]
    scores = dot(by_side(key_ref[...]), query_ref[...], NT).reshape(keys // 8, 16, count)
    scores = scores + bias_ref[0]
    top = per_side(jnp.max(scores, axis=0), jnp.max, count)
    exponent = jnp.exp(scores - top)
    total = per_side(jnp.sum(exponent, axis=0), jnp.sum, count)
    probs = (exponent * (1.0 / total)).astype(bf16)
    probs_ref[0] = probs
    attended = dot(by_side(value_ref[...]), probs.reshape(keys * 2, count), TN)
    attended_ref[...] = attended.astype(bf16)


def residual_kernel(
    narrow, wide, where, attended_ref, tokens_ref, hidden_ref, mask_ref, gain_ref, blocks_ref,
    residual_ref, input_ref, weight, sem,
):
    rows = weight.shape[0] // (narrow * wide)
    load_rows(where, blocks_ref, 0, rows, slice(None), weight, sem, narrow, wide)
    embedded = embed(tokens_ref, hidden_ref, mask_ref)
    wait_all(weight, sem)
    residual = embedded + dot(attended_ref[...], weight[...], TN)
    residual_ref[...] = residual
    input_ref[...] = (residual * inverse_rms(residual) * gain_ref[...]).astype(bf16)


def gelu_parts(v):
    scale = math.sqrt(2.0 / math.pi)
    square = v * v
    bend = jnp.tanh(scale * v * (1.0 + 0.044715 * square))
    half = 0.5 * (1.0 + bend)
    slope = half + 0.5 * v * (1.0 - bend * bend) * (scale * (1.0 + 3 * 0.044715 * square))
    return v * half, slope


def ffn_kernel(
    narrow, wide, first, where, input_ref, cot_ref, blocks_ref, down_ref, *refs
):
    if first:
        acc_in = None
        grads_ref, active_ref, acc_ref, weights, grads, turned, sems = refs
    else:
        acc_in, grads_ref, active_ref, acc_ref, weights, grads, turned, sems = refs
    width = input_ref.shape[1]
    rows = width // (narrow * wide)
    steps = active_ref.shape[1] // FF_STEP
    for n in range(2):
        load_rows(where, blocks_ref, n * rows, rows, slice(None), weights.at[n], sems.at[n], narrow, wide)
    turned[...] = input_ref[...].T
    if first:
        acc_ref[...] = jnp.zeros_like(acc_ref)
    else:
        acc_ref[...] = acc_in[...]
    for n in range(2):
        wait_all(weights.at[n], sems.at[n])

    def step(n, _):
        lanes = pl.ds(pl.multiple_of(n * FF_STEP, FF_STEP), FF_STEP)
        x = input_ref[...]
        gate_weight = weights[0, :, lanes]
        up_weight = weights[1, :, lanes]
        gate = dot(x, gate_weight)
        up = dot(x, up_weight)
        act_grad = dot(cot_ref[...], down_ref[lanes, :], NT)
        gelu, slope = gelu_parts(gate)
        active_ref[:, lanes] = (gelu * up).astype(bf16)
        gate_back = (act_grad * up * slope).astype(bf16)
        up_back = (act_grad * gelu).astype(bf16)
        grads[0, :, lanes] = dot(turned[...], gate_back).astype(bf16)
        grads[1, :, lanes] = dot(turned[...], up_back).astype(bf16)
        acc_ref[...] += dot(gate_back, gate_weight, NT) + dot(up_back, up_weight, NT)
        return 0

    lax.fori_loop(0, steps, step, 0)
    for n in range(2):
        store_rows(where, grads.at[n], grads_ref, n * rows, rows, sems.at[n], narrow, wide)
    for n in range(2):
        wait_all(grads.at[n], sems.at[n])


def down_kernel(where, left_ref, right_ref, cot_ref, residual_ref, down_ref, out_ref, grads_ref):
    hidden = left_ref.shape[1]
    total = residual_ref[...] + dot(left_ref[...], down_ref[0:hidden, :])
    total = total + dot(right_ref[...], down_ref[hidden:, :])
    out_ref[...] = total.astype(bf16)
    cot = cot_ref[...]
    grads_ref[0:hidden, :] = dot(left_ref[...], cot, TN).astype(bf16)
    grads_ref[hidden:, :] = dot(right_ref[...], cot, TN).astype(bf16)


def turn_kernel(
    narrow, wide, where, residual_ref, ffn_ref, cot_ref, attended_ref, gain_ref, blocks_ref,
    grad_ref, head_ref, gain_out, grads_ref, weight, grads, sems,
):
    rows = weight.shape[0] // (narrow * wide)
    load_rows(where, blocks_ref, 0, rows, slice(None), weight, sems.at[0], narrow, wide)
    residual = residual_ref[...]
    inverse = inverse_rms(residual)
    normed = residual * inverse
    ffn_grad = ffn_ref[...]
    gain_out[...] = jnp.sum(ffn_grad * normed, axis=0, keepdims=True)
    scaled = ffn_grad * gain_ref[...]
    center = jnp.mean(scaled * normed, axis=-1, keepdims=True)
    grad = cot_ref[...].astype(f32) + (scaled - normed * center) * inverse
    grad_ref[...] = grad
    low = grad.astype(bf16)
    grads[...] = dot(attended_ref[...], low).astype(bf16)
    store_rows(where, grads, grads_ref, 0, rows, sems.at[1], narrow, wide)
    wait_all(weight, sems.at[0])
    head_ref[...] = dot(weight[...], low, NT).astype(bf16)
    wait_all(grads, sems.at[1])


def attend_back_kernel(
    query_ref, key_ref, value_ref, head_ref, probs_ref, query_out, key_out, value_out, scores_ref
):
    count = query_ref.shape[0]
    keys = key_ref.shape[0]
    low = probs_ref[0]
    head = head_ref[...]
    probs = low.astype(f32)
    prob_grad = dot(by_side(value_ref[...]), head).reshape(keys // 8, 16, count)
    center = per_side(jnp.sum(probs * prob_grad, axis=0), jnp.sum, count)
    score_grad = (probs * (prob_grad - center)).astype(bf16)
    scores_ref[0] = score_grad
    score_grad = score_grad.reshape(keys * 2, count)
    query_grad = dot(by_side(key_ref[...]), score_grad, TN)
    query_out[...] = query_grad.T.astype(bf16)
    key_out[...] = own_side(dot(score_grad, query_ref[...])).astype(bf16)
    value_out[...] = own_side(dot(low.reshape(keys * 2, count), head, NT)).astype(bf16)


def table_kernel(scores_ref, rel_ref, lay_ref, out_ref):
    keys, count = rel_ref.shape
    out_ref[...] = jnp.zeros_like(out_ref)

    def step(g, _):
        rows = pl.ds(pl.multiple_of(g * 8, 8), 8)
        hot = []
        for ids, low, high in ((rel_ref[rows, :], 0, NB_REL), (lay_ref[rows, :], NB_REL, NB)):
            for b in range(low, high, 2):
                pair = [jnp.where(ids == b + n, 1.0, 0.0) for n in range(2)]
                hot.append(jnp.concatenate(pair, axis=0).astype(bf16))
        hot = jnp.concatenate(hot, axis=0)
        grads = scores_ref[:, pl.ds(g, 1)].reshape(H * 8, count)
        out_ref[...] += dot(grads, hot, NT)
        return 0

    lax.fori_loop(0, keys // 8, step, 0)


def project_back_kernel(
    narrow, wide, where, input_ref, pick_ref, query_ref, key_ref, value_ref, tokens_ref, hidden_ref,
    mask_ref, gain_ref, residual_ref, blocks_ref,
    tokens_out, gain_out, embed_out, grads_ref, weights, grads, turned, sems,
):
    width = tokens_ref.shape[1]
    rows = width // (narrow * wide)
    for n in range(3):
        load_rows(where, blocks_ref, n * rows, rows, slice(None), weights.at[n], sems.at[n], narrow, wide)
    turned[...] = input_ref[...].T
    pick = pick_ref[...]
    spread = [query_ref[...]] + [
        dot(pick, ref[...], TN).astype(bf16) for ref in (key_ref, value_ref)
    ]
    for n in range(3):
        grads[n] = dot(turned[...], spread[n]).astype(bf16)
        store_rows(where, grads.at[n], grads_ref, n * rows, rows, sems.at[3 + n], narrow, wide)
    attn_grad = None
    for n in range(3):
        wait_all(weights.at[n], sems.at[n])
        term = dot(spread[n], weights[n], NT)
        attn_grad = term if n == 0 else attn_grad + term
    embedded = embed(tokens_ref, hidden_ref, mask_ref)
    inverse = inverse_rms(embedded)
    normed = embedded * inverse
    gain_out[...] = jnp.sum(attn_grad * normed, axis=0, keepdims=True)
    scaled = attn_grad * gain_ref[...]
    center = jnp.mean(scaled * normed, axis=-1, keepdims=True)
    grad = residual_ref[...] + (scaled - normed * center) * inverse
    concealed = hidden_ref[...] == 1.0
    tokens_out[...] = jnp.where(concealed, 0.0, grad)
    embed_out[...] = jnp.sum(jnp.where(concealed, grad, 0.0), axis=0, keepdims=True)
    for n in range(3):
        wait_all(grads.at[n], sems.at[3 + n])


def shape(dims, kind):
    return jax.ShapeDtypeStruct(tuple(dims), kind)


def local(
    tokens, hidden_patch, segment_ids, rel_ids, layout_ids, w_query, w_key, w_value, w_out, w_gate,
    w_up, w_down, gain_attn, gain_ffn, mask_embed, rel_table, layout_table, cotangent,
):
    narrow, wide = lax.axis_size("narrow"), lax.axis_size("wide")
    devices = narrow * wide
    count, width = tokens.shape
    keys = count - HIDE
    ff = w_gate.shape[1]
    rows = w_query.shape[0]
    where = jnp.stack([lax.axis_index("narrow"), lax.axis_index("wide")]).astype(jnp.int32)
    core = lax.axis_index("wide") % 2

    small = jnp.concatenate(
        [p.astype(bf16) for p in (gain_attn, gain_ffn, mask_embed, rel_table, layout_table)]
    )[None]
    small = ordered(gather_blocks(small, narrow, wide), narrow, wide)[:, 0].astype(f32)
    pieces, at = [], 0
    for p in (gain_attn, gain_ffn, mask_embed, rel_table, layout_table):
        pieces.append(small[:, at : at + p.shape[0]].reshape(-1))
        at += p.shape[0]
    attn_gain, ffn_gain, embed_row = [p[None] for p in pieces[:3]]
    table = jnp.concatenate([pieces[3].reshape(NB_REL, H), pieces[4].reshape(NB_LAY, H)])
    table = jnp.concatenate([table.T, jnp.full((H, 128 - NB), neg_large, f32)], axis=1)

    def as_blocks(x):
        full = gather_blocks(x, narrow, wide)
        return full

    qkv_blocks = as_blocks(jnp.concatenate([w_query, w_key, w_value]).astype(bf16))
    out_blocks = as_blocks(w_out.astype(bf16))
    down_low = ordered(as_blocks(w_down.astype(bf16)), narrow, wide).reshape(ff, width)
    gu_low = jnp.concatenate([w_gate, w_up]).astype(bf16)
    gu_blocks = [as_blocks(gu_low[:, :SPLIT]), as_blocks(gu_low[:, SPLIT:])]

    hidden_column = hidden_patch.astype(f32)[:, None]
    pick, rel_index, lay_index = pl.pallas_call(
        prepare_kernel,
        out_shape=(
            shape((keys, count), bf16), shape((keys, count), jnp.int32), shape((keys, count), jnp.int32),
        ),
        compiler_params=params(),
        cost_estimate=cost(2e9, 4e6),
    )(hidden_patch[None], segment_ids[None], rel_ids, layout_ids)

    groups = keys // 8
    whole = pl.BlockSpec((keys, count), lambda p: (0, 0))
    bias = pl.pallas_call(
        bias_kernel,
        grid=(PAIRS,),
        in_specs=[pl.BlockSpec((H, 128), lambda p: (0, 0)), whole, whole],
        out_specs=pl.BlockSpec((1, groups, 16, count), lambda p: (p, 0, 0, 0)),
        out_shape=shape((PAIRS, groups, 16, count), f32),
        compiler_params=params(),
        cost_estimate=cost(1e10, 40e6),
    )(table, rel_index, lay_index)

    attn_input, query, key, value = pl.pallas_call(
        functools.partial(project_kernel, narrow, wide),
        in_specs=[SM] + [VM] * 5 + [ANY],
        out_specs=[VM] * 4,
        out_shape=(
            shape((count, width), bf16), shape((count, width), bf16), shape((keys, width), bf16),
            shape((keys, width), bf16),
        ),
        scratch_shapes=[pltpu.VMEM((3, width, width), bf16), pltpu.SemaphoreType.DMA((3,))],
        compiler_params=params(),
        cost_estimate=cost(3.2e9, 10e6),
    )(where, tokens, hidden_column, embed_row, attn_gain, pick, qkv_blocks)

    row_block = pl.BlockSpec((count, 128), lambda p: (0, p))
    key_block = pl.BlockSpec((keys, 128), lambda p: (0, p))
    turn_block = pl.BlockSpec((128, count), lambda p: (p, 0))
    score_block = pl.BlockSpec((1, groups, 16, count), lambda p: (p, 0, 0, 0))
    attended, probs = pl.pallas_call(
        attend_kernel,
        grid=(PAIRS,),
        in_specs=[row_block, key_block, key_block, score_block],
        out_specs=[turn_block, score_block],
        out_shape=(shape((width, count), bf16), shape((PAIRS, groups, 16, count), bf16)),
        compiler_params=params(),
        cost_estimate=cost(1e10, 18e6),
    )(query, key, value, bias)

    residual, ffn_input = pl.pallas_call(
        functools.partial(residual_kernel, narrow, wide),
        in_specs=[SM] + [VM] * 5 + [ANY],
        out_specs=[VM] * 2,
        out_shape=(shape((count, width), f32), shape((count, width), bf16)),
        scratch_shapes=[pltpu.VMEM((width, width), bf16), pltpu.SemaphoreType.DMA],
        compiler_params=params(),
        cost_estimate=cost(1.1e9, 8e6),
    )(where, attended, tokens, hidden_column, embed_row, ffn_gain, out_blocks)

    block_dims = (2, wide // 2, narrow)
    acc, active, gu_grads = None, [], []
    for part, size in enumerate((SPLIT, ff - SPLIT)):
        first = part == 0
        down_spec = pl.BlockSpec((size, width), lambda *_: (0, 0))
        call = pl.pallas_call(
            functools.partial(ffn_kernel, narrow, wide, first),
            in_specs=[SM, VM, VM, ANY, VM] + ([] if first else [VM]),
            out_specs=[ANY, VM, VM],
            out_shape=(
                shape(block_dims + (2 * rows, size), bf16),
                shape((count, size), bf16),
                shape((count, width), f32),
            ),
            scratch_shapes=[
                pltpu.VMEM((2, width, size), bf16),
                pltpu.VMEM((2, width, size), bf16),
                pltpu.VMEM((width, count), bf16),
                pltpu.SemaphoreType.DMA((2,)),
            ],
            compiler_params=params(60),
            cost_estimate=cost(14 * count * width * size, 8 * width * size),
        )
        down_part = down_low[part * SPLIT : part * SPLIT + size]
        extra = () if first else (acc,)
        grads, act, acc = call(where, ffn_input, cotangent, gu_blocks[part], down_part, *extra)
        active.append(act)
        gu_grads.append(grads)

    residual_grad, head, ffn_gain_part, out_grads = pl.pallas_call(
        functools.partial(turn_kernel, narrow, wide),
        in_specs=[SM] + [VM] * 5 + [ANY],
        out_specs=[VM, VM, VM, ANY],
        out_shape=(
            shape((count, width), f32), shape((width, count), bf16), shape((1, width), f32),
            shape(block_dims + (rows, width), bf16),
        ),
        scratch_shapes=[
            pltpu.VMEM((width, width), bf16), pltpu.VMEM((width, width), bf16),
            pltpu.SemaphoreType.DMA((2,)),
        ],
        compiler_params=params(),
        cost_estimate=cost(2.2e9, 14e6),
    )(where, residual, acc, cotangent, attended, ffn_gain, out_blocks)

    output, down_grads = pl.pallas_call(
        down_kernel,
        in_specs=[SM] + [VM] * 5,
        out_specs=[VM, VM],
        out_shape=(shape((count, width), bf16), shape((ff, width), bf16)),
        compiler_params=params(60),
        cost_estimate=cost(4 * count * width * ff, 16e6),
    )(where, active[0], active[1], cotangent, residual, down_low)

    query_grad, key_grad, value_grad, score_grads = pl.pallas_call(
        attend_back_kernel,
        grid=(PAIRS,),
        in_specs=[row_block, key_block, key_block, turn_block, score_block],
        out_specs=[row_block, key_block, key_block, score_block],
        out_shape=(
            shape((count, width), bf16), shape((keys, width), bf16), shape((keys, width), bf16),
            shape((PAIRS, groups, 16, count), bf16),
        ),
        compiler_params=params(),
        cost_estimate=cost(2e10, 18e6),
    )(query, key, value, head, probs)

    tokens_grad, attn_gain_part, embed_part, qkv_grads = pl.pallas_call(
        functools.partial(project_back_kernel, narrow, wide),
        in_specs=[SM] + [VM] * 10 + [ANY],
        out_specs=[VM, VM, VM, ANY],
        out_shape=(
            shape((count, width), f32), shape((1, width), f32), shape((1, width), f32),
            shape(block_dims + (3 * rows, width), bf16),
        ),
        scratch_shapes=[
            pltpu.VMEM((3, width, width), bf16), pltpu.VMEM((3, width, width), bf16),
            pltpu.VMEM((width, count), bf16), pltpu.SemaphoreType.DMA((6,)),
        ],
        compiler_params=params(),
        cost_estimate=cost(6.5e9, 20e6),
    )(
        where, attn_input, pick, query_grad, key_grad, value_grad, tokens, hidden_column, embed_row,
        attn_gain, residual_grad, qkv_blocks,
    )

    table_grads = pl.pallas_call(
        table_kernel,
        out_shape=shape((H * 8, NB * 8), f32),
        compiler_params=params(),
        cost_estimate=cost(8e9, 8e6),
    )(score_grads, rel_index, lay_index)
    table_grads = jnp.einsum("hjbj->bh", table_grads.reshape(H, 8, NB, 8))

    gu_sums = [scatter_blocks(g, narrow, wide) for g in gu_grads]
    gu_sum = jnp.concatenate(gu_sums, axis=1)
    out_sum = scatter_blocks(out_grads, narrow, wide)
    order_z, order_w = jnp.meshgrid(jnp.arange(narrow), jnp.arange(wide), indexing="ij")
    del order_z, order_w
    core_flip, chip_flip, z = jnp.meshgrid(
        jnp.arange(2), jnp.arange(wide // 2), jnp.arange(narrow), indexing="ij"
    )
    owner = z * wide + ((chip_flip * 2 + core_flip) ^ lax.axis_index("wide"))

    def flipped(parts):
        parts = parts.reshape((devices, -1) + parts.shape[1:])
        return parts[owner.reshape(-1)].reshape(block_dims + parts.shape[1:])

    down_sum = scatter_blocks(flipped(down_grads), narrow, wide)
    qkv_sum = scatter_blocks(qkv_grads, narrow, wide)
    vectors = (attn_gain_part, ffn_gain_part, embed_part, table_grads[:NB_REL], table_grads[NB_REL:])
    vectors = jnp.concatenate([v.reshape(devices, -1) for v in vectors], axis=1)
    small_sum = scatter_blocks(flipped(vectors.astype(bf16)), narrow, wide)[0]
    sizes = [p.shape[0] for p in (gain_attn, gain_ffn, mask_embed, rel_table, layout_table)]
    small_out, at = [], 0
    for size in sizes:
        small_out.append(small_sum[at : at + size])
        at += size
    return (
        output, tokens_grad, qkv_sum[:rows], qkv_sum[rows : 2 * rows], qkv_sum[2 * rows :], out_sum,
        gu_sum[:rows], gu_sum[rows:], down_sum, *small_out,
    )


def solution(mesh):
    both = P(("narrow", "wide"))
    table = P(("narrow", "wide"), None)
    return jax.shard_map(
        local,
        mesh=mesh,
        in_specs=(table, both, both) + (table,) * 9 + (both,) * 5 + (table,),
        out_specs=(table,) * 9 + (both,) * 5,
        check_vma=False,
    )
```

```python
import functools
import math

import jax
import jax.numpy as jnp
from jax import lax
from jax.experimental import pallas as pl
from jax.experimental.pallas import tpu as pltpu
from jax.sharding import PartitionSpec as P

H = 16
HD = 64
PAIRS = H // 2
NB_REL = 32
NB_LAY = 64
NB = NB_REL + NB_LAY
HIDE = 192
SPLIT = 1536
FF_STEP = 256

eps_norm = 1e-06
neg_large = -1e30
f32 = jnp.float32
bf16 = jnp.bfloat16

NN = (((1,), (0,)), ((), ()))
NT = (((1,), (1,)), ((), ()))
TN = (((0,), (0,)), ((), ()))


def dot(a, b, dims=NN):
    return lax.dot_general(a, b, dims, preferred_element_type=f32)


def params(mib=56):
    return pltpu.CompilerParams(vmem_limit_bytes=mib * 1024 * 1024)


def cost(flops, nbytes):
    return pl.CostEstimate(flops=int(flops), bytes_accessed=int(nbytes), transcendentals=0)


VM = pl.BlockSpec(memory_space=pltpu.VMEM)
SM = pl.BlockSpec(memory_space=pltpu.SMEM)
ANY = pl.BlockSpec(memory_space=pl.ANY)


def shift_narrow(x, step, count):
    return lax.ppermute(x, "narrow", [(i, (i + step) % count) for i in range(count)])


def flip_wide(x, bits, count):
    return lax.ppermute(x, "wide", [(i, i ^ bits) for i in range(count)])


class Steps:
    def __init__(self):
        self.last = ()

    def enter(self, *values):
        out = lax.optimization_barrier(tuple(values) + self.last)
        return out[: len(values)] if len(values) > 1 else out[0]

    def leave(self, *values):
        self.last = tuple(values)


class Gather:
    def __init__(self, narrow, wide, x):
        self.narrow, self.wide, self.x = narrow, wide, x
        self.pieces = []

    def start(self, steps):
        x = steps.enter(self.x)
        self.x = x
        self.sent = [shift_narrow(x, s, self.narrow) for s in range(1, self.narrow)]

    def plane(self, steps):
        sent = steps.enter(*self.sent)
        steps.leave(sent[0])
        column = jnp.stack([self.x] + list(sent))
        self.column = column
        self.pieces = [(column, 0, 0, 0)]
        self.near = [flip_wide(column, 2, self.wide), flip_wide(column, 4, self.wide)]
        self.first = [(flip_wide(column, 1, self.wide), 1, 0, 0)]

    def forward(self, steps):
        x, y = steps.enter(*self.near)
        steps.leave(x)
        half = self.narrow // 2
        self.far = [flip_wide(x[:half], 4, self.wide), flip_wide(y[half:], 2, self.wide)]
        self.pieces += [(x, 0, 1, 0), (y, 0, 2, 0)]
        self.first += [
            (flip_wide(x, 1, self.wide), 1, 1, 0), (flip_wide(y, 1, self.wide), 1, 2, 0)
        ]

    def cores(self, steps):
        left, right = steps.enter(*self.far)
        steps.leave(left)
        half = self.narrow // 2
        self.pieces += [(left, 0, 3, 0), (right, 0, 3, half)]
        self.first += [
            (flip_wide(left, 1, self.wide), 1, 3, 0), (flip_wide(right, 1, self.wide), 1, 3, half)
        ]

    def finish(self, steps):
        arrays = steps.enter(*[p[0] for p in self.first])
        steps.leave(arrays[-1])
        return self.pieces + [(a,) + p[1:] for a, p in zip(arrays, self.first)]


class PlainGather(Gather):
    def plane(self, steps):
        sent = steps.enter(*self.sent)
        steps.leave(sent[0])
        column = jnp.stack([self.x] + list(sent))
        found = {0: column}
        bit = 2
        while bit < self.wide:
            for at in list(found):
                found[at ^ bit] = flip_wide(found[at], bit, self.wide)
            bit *= 2
        self.pieces = [(v, 0, k // 2, 0) for k, v in found.items()]

    def forward(self, steps):
        pass

    def cores(self, steps):
        self.first = [(flip_wide(v, 1, self.wide), 1, k, 0) for v, _, k, _ in self.pieces]


def ordered(pieces, narrow, wide):
    table = [None] * (narrow * wide)
    for array, core, chip, low in pieces:
        for s in range(array.shape[0]):
            table[(core * (wide // 2) + chip) * narrow + low + s] = array[s]
    flat = jnp.stack(table)
    z, w = jnp.meshgrid(jnp.arange(narrow), jnp.arange(wide), indexing="ij")
    flip = w ^ lax.axis_index("wide")
    shift = (lax.axis_index("narrow") - z) % narrow
    order = ((flip & 1) * (wide // 2) + (flip >> 1)) * narrow + shift
    return flat[order.reshape(-1)]


class Scatter:
    def __init__(self, narrow, wide, keep, send):
        self.narrow, self.wide, self.keep = narrow, wide, keep
        self.sent = flip_wide(send, 1, wide)

    def plane(self, steps):
        sent = steps.enter(self.sent)
        mine = (self.keep.astype(f32) + sent.astype(f32)).astype(bf16)
        steps.leave(mine)
        half = self.narrow // 2
        self.mine = mine
        self.far = [
            flip_wide(mine[3, :half], 2, self.wide), flip_wide(mine[3, half:], 4, self.wide)
        ]

    def forward(self, steps):
        left, right = steps.enter(*self.far)
        half = self.narrow // 2
        mine = self.mine
        y = jnp.concatenate(
            [(mine[2, :half].astype(f32) + left.astype(f32)).astype(bf16), mine[2, half:]]
        )
        x = jnp.concatenate(
            [mine[1, :half], (mine[1, half:].astype(f32) + right.astype(f32)).astype(bf16)]
        )
        steps.leave(x, y)
        self.near = [flip_wide(x, 2, self.wide), flip_wide(y, 4, self.wide)]

    def column(self, steps):
        x, y = steps.enter(*self.near)
        total = self.mine[0].astype(f32) + x.astype(f32) + y.astype(f32)
        self.spread(steps, total.astype(bf16))

    def spread(self, steps, mine):
        steps.leave(mine)
        z = lax.axis_index("narrow")
        self.own = lax.dynamic_index_in_dim(mine, z, 0, False)
        self.sent = [
            shift_narrow(
                lax.dynamic_index_in_dim(mine, (z + s) % self.narrow, 0, False), s, self.narrow
            )
            for s in range(1, self.narrow)
        ]

    def finish(self, steps):
        sent = steps.enter(*self.sent)
        total = self.own.astype(f32)
        for s in sent:
            total = total + s.astype(f32)
        steps.leave(total)
        return total


class PlainScatter(Scatter):
    def plane(self, steps):
        sent = steps.enter(self.sent)
        mine = self.keep.astype(f32) + sent.astype(f32)
        bit = self.wide // 2
        while bit > 1:
            half = mine.shape[0] // 2
            low = mine.astype(bf16)
            mine = low[:half].astype(f32) + flip_wide(low[half:], bit, self.wide).astype(f32)
            bit //= 2
        self.total = mine[0].astype(bf16)

    def forward(self, steps):
        pass

    def column(self, steps):
        self.spread(steps, self.total)


def piece_arrays(pieces):
    return [p[0] for p in pieces]


def piece_places(pieces):
    return [p[1:] + (p[0].shape[0],) for p in pieces]


def load_rows(where, sources, places, index, rows, dst, sem, narrow, wide):
    if places is None:
        pltpu.make_async_copy(sources[0].at[index], dst, sem).start()
        return
    for src, (core, chip, first, length) in zip(sources, places):
        w = jnp.bitwise_xor(where[1], 2 * chip + core)
        for n in range(length):
            z = lax.rem(where[0] - first - n + narrow, narrow)
            row = pl.multiple_of((z * wide + w) * rows, rows)
            pltpu.make_async_copy(
                src.at[n, pl.ds(index * rows, rows)], dst.at[pl.ds(row, rows), :], sem
            ).start()


def load_pairs(where, sources, places, dst, sem, narrow, wide):
    if places is None:
        pltpu.make_async_copy(sources[0].at[0], dst, sem).start()
        return
    for src, (core, chip, first, length) in zip(sources, places):
        rows, lanes = src.shape[1:]
        c = jnp.bitwise_xor(lax.shift_right_logical(where[1], 1), chip)
        lane = pl.multiple_of(jnp.bitwise_xor(jnp.bitwise_and(where[1], 1), core) * lanes, lanes)
        for n in range(length):
            z = lax.rem(where[0] - first - n + narrow, narrow)
            row = pl.multiple_of((z * (wide // 2) + c) * rows, rows)
            pltpu.make_async_copy(
                src.at[n], dst.at[pl.ds(row, rows), pl.ds(lane, lanes)], sem
            ).start()


def wait_all(ref, sem):
    pltpu.make_async_copy(ref, ref, sem).wait()


def store_rows(where, src, out, index, rows, sem, narrow, wide):
    if len(out) == 1:
        pltpu.make_async_copy(src, out[0].at[index], sem).start()
        return
    core = jnp.bitwise_and(where[1], 1)
    chip = lax.shift_right_logical(where[1], 1)
    for z in range(narrow):
        for c in range(wide // 2):
            flip = jnp.bitwise_xor(chip, c)
            for dst, side in zip(out, (core, 1 - core)):
                row = pl.multiple_of((z * wide + 2 * c + side) * rows, rows)
                pltpu.make_async_copy(
                    src.at[pl.ds(row, rows), :], dst.at[flip, z, pl.ds(index * rows, rows)], sem
                ).start()


def store_pairs(where, src, out, sem, narrow, wide):
    if len(out) == 1:
        pltpu.make_async_copy(src, out[0].at[0], sem).start()
        return
    core = jnp.bitwise_and(where[1], 1)
    chip = lax.shift_right_logical(where[1], 1)
    rows, lanes = out[0].shape[2:]
    for z in range(narrow):
        for c in range(wide // 2):
            flip = jnp.bitwise_xor(chip, c)
            for dst, side in zip(out, (core, 1 - core)):
                lane = pl.multiple_of(side * lanes, lanes)
                pltpu.make_async_copy(
                    src.at[pl.ds((z * (wide // 2) + c) * rows, rows), pl.ds(lane, lanes)],
                    dst.at[flip, z],
                    sem,
                ).start()


def prepare_kernel(hidden_ref, segment_ref, rel_ref, lay_ref, pick_ref, rel_out, lay_out):
    count = hidden_ref.shape[1]
    keys = pick_ref.shape[0]
    seen = hidden_ref[...] == 0
    before = lax.broadcasted_iota(jnp.int32, (count, count), 0)
    after = lax.broadcasted_iota(jnp.int32, (count, count), 1)
    upper = jnp.where(before <= after, 1.0, 0.0).astype(bf16)
    seen_rows = jnp.broadcast_to(jnp.where(seen, 1.0, 0.0), (16, count)).astype(bf16)
    rank = dot(seen_rows, upper)[0:1].astype(jnp.int32) - 1
    rank = jnp.where(seen, rank, -1)
    number = lax.broadcasted_iota(jnp.int32, (keys, count), 0)
    pick = jnp.where(number == rank, 1.0, 0.0).astype(bf16)
    pick_ref[...] = pick
    segment = jnp.broadcast_to(segment_ref[...].astype(f32), (16, count)).astype(bf16)
    key_segment = dot(pick, segment, NT)[:, 0:1]
    valid = key_segment == segment_ref[...].astype(f32)
    rel = dot(pick, rel_ref[...].astype(f32).astype(bf16), NT).astype(jnp.int32)
    lay = dot(pick, lay_ref[...].astype(f32).astype(bf16), NT).astype(jnp.int32)
    rel_out[...] = jnp.where(valid, rel, NB)
    lay_out[...] = lay + NB_REL


def bias_kernel(table_ref, rel_ref, lay_ref, out_ref):
    keys, count = rel_ref.shape
    groups = keys // 8
    pair = pl.program_id(0)
    tables = [
        jnp.broadcast_to(table_ref[pl.ds(2 * pair + side, 1), :], (keys, 128)) for side in range(2)
    ]
    for c in range(count // 128):
        lanes = slice(c * 128, c * 128 + 128)
        for side in range(2):
            found = jnp.take_along_axis(tables[side], rel_ref[:, lanes], axis=1)
            found = found + jnp.take_along_axis(tables[side], lay_ref[:, lanes], axis=1)
            out_ref[0, :, side * 8 : side * 8 + 8, lanes] = found.reshape(groups, 8, 128)


def embed(tokens_ref, hidden_ref, mask_ref):
    return jnp.where(hidden_ref[...] == 1.0, mask_ref[...], tokens_ref[...].astype(f32))


def inverse_rms(v):
    return lax.rsqrt(jnp.mean(v * v, axis=-1, keepdims=True) + eps_norm)


def project_kernel(
    narrow, wide, places, where, tokens_ref, hidden_ref, mask_ref, gain_ref, pick_ref, *refs
):
    sources = refs[:-6]
    input_ref, query_ref, key_ref, value_ref, weights, sems = refs[-6:]
    width = tokens_ref.shape[1]
    rows = width // (narrow * wide)
    for n in range(3):
        load_rows(where, sources, places, n, rows, weights.at[n], sems.at[n], narrow, wide)
    embedded = embed(tokens_ref, hidden_ref, mask_ref)
    attn_input = (embedded * inverse_rms(embedded) * gain_ref[...]).astype(bf16)
    input_ref[...] = attn_input
    seen = dot(pick_ref[...], attn_input).astype(bf16)
    wait_all(weights.at[0], sems.at[0])
    query_ref[...] = dot(attn_input, weights[0]).astype(bf16)
    wait_all(weights.at[1], sems.at[1])
    key_ref[...] = dot(seen, weights[1]).astype(bf16)
    wait_all(weights.at[2], sems.at[2])
    value_ref[...] = dot(seen, weights[2]).astype(bf16)


def by_side(x):
    keys = x.shape[0]
    wide = x.astype(f32).reshape(keys // 8, 8, 128)
    left = lax.broadcasted_iota(jnp.int32, wide.shape, 2) < HD
    both = jnp.concatenate([jnp.where(left, wide, 0.0), jnp.where(left, 0.0, wide)], axis=1)
    return both.astype(bf16).reshape(keys * 2, 128)


def own_side(x):
    x = x.reshape(x.shape[0] // 16, 16, 128)
    left = lax.broadcasted_iota(jnp.int32, (x.shape[0], 8, 128), 2) < HD
    return jnp.where(left, x[:, 0:8], x[:, 8:16]).reshape(x.shape[0] * 8, 128)


def per_side(x, fold, spread):
    return jnp.concatenate(
        [
            jnp.broadcast_to(fold(x[side * 8 : side * 8 + 8], axis=0, keepdims=True), (8, spread))
            for side in range(2)
        ],
        axis=0,
    )[None]


def attend_kernel(query_ref, key_ref, value_ref, bias_ref, attended_ref, probs_ref):
    count = query_ref.shape[0]
    keys = key_ref.shape[0]
    scores = dot(by_side(key_ref[...]), query_ref[...], NT).reshape(keys // 8, 16, count)
    scores = scores + bias_ref[0]
    top = per_side(jnp.max(scores, axis=0), jnp.max, count)
    exponent = jnp.exp(scores - top)
    total = per_side(jnp.sum(exponent, axis=0), jnp.sum, count)
    probs = (exponent * (1.0 / total)).astype(bf16)
    probs_ref[0] = probs
    attended = dot(by_side(value_ref[...]), probs.reshape(keys * 2, count), TN)
    attended_ref[...] = attended.astype(bf16)


def residual_kernel(
    narrow, wide, places, where, attended_ref, tokens_ref, hidden_ref, mask_ref, gain_ref, *refs
):
    sources = refs[:-4]
    residual_ref, input_ref, weight, sem = refs[-4:]
    rows = weight.shape[0] // (narrow * wide)
    load_rows(where, sources, places, 0, rows, weight, sem, narrow, wide)
    embedded = embed(tokens_ref, hidden_ref, mask_ref)
    wait_all(weight, sem)
    residual = embedded + dot(attended_ref[...], weight[...], TN)
    residual_ref[...] = residual
    input_ref[...] = (residual * inverse_rms(residual) * gain_ref[...]).astype(bf16)


def gelu_parts(v):
    scale = math.sqrt(2.0 / math.pi)
    square = v * v
    bend = jnp.tanh(scale * v * (1.0 + 0.044715 * square))
    half = 0.5 * (1.0 + bend)
    slope = half + 0.5 * v * (1.0 - bend * bend) * (scale * (1.0 + 3 * 0.044715 * square))
    return v * half, slope


def ffn_kernel(narrow, wide, low, counts, places, down_places, where, input_ref, cot_ref, *refs):
    sources, refs = refs[: counts[0]], refs[counts[0] :]
    down_sources, refs = refs[: counts[1]], refs[counts[1] :]
    acc_in, refs = (None, refs) if low == 0 else (refs[0], refs[1:])
    out, refs = refs[: counts[2]], refs[counts[2] :]
    active_ref, acc_ref, weights, down_ref, grads, turned, sems = refs
    width = input_ref.shape[1]
    rows = width // (narrow * wide)
    steps = active_ref.shape[1] // FF_STEP
    for n in range(2):
        load_rows(where, sources, places, n, rows, weights.at[n], sems.at[n], narrow, wide)
    load_pairs(where, down_sources, down_places, down_ref, sems.at[2], narrow, wide)
    turned[...] = input_ref[...].T
    if low == 0:
        acc_ref[...] = jnp.zeros_like(acc_ref)
    else:
        acc_ref[...] = acc_in[...]
    for n in range(2):
        wait_all(weights.at[n], sems.at[n])
    wait_all(down_ref, sems.at[2])

    def step(n, _):
        lanes = pl.ds(pl.multiple_of(n * FF_STEP, FF_STEP), FF_STEP)
        x = input_ref[...]
        gate_weight = weights[0, :, lanes]
        up_weight = weights[1, :, lanes]
        gate = dot(x, gate_weight)
        up = dot(x, up_weight)
        hidden = pl.ds(pl.multiple_of(low + n * FF_STEP, FF_STEP), FF_STEP)
        act_grad = dot(cot_ref[...], down_ref[hidden, :], NT)
        gelu, slope = gelu_parts(gate)
        active_ref[:, lanes] = (gelu * up).astype(bf16)
        gate_back = (act_grad * up * slope).astype(bf16)
        up_back = (act_grad * gelu).astype(bf16)
        grads[0, :, lanes] = dot(turned[...], gate_back).astype(bf16)
        grads[1, :, lanes] = dot(turned[...], up_back).astype(bf16)
        acc_ref[...] += dot(gate_back, gate_weight, NT) + dot(up_back, up_weight, NT)
        return 0

    lax.fori_loop(0, steps, step, 0)
    for n in range(2):
        store_rows(where, grads.at[n], out, n, rows, sems.at[n], narrow, wide)
    for n in range(2):
        wait_all(grads.at[n], sems.at[n])


def down_kernel(narrow, wide, places, count, where, left_ref, right_ref, cot_ref, residual_ref, *refs):
    sources, refs = refs[:count], refs[count:]
    output_ref, refs = refs[0], refs[1:]
    out, (weight, grads, sems) = refs[:-3], refs[-3:]
    load_pairs(where, sources, places, weight, sems.at[0], narrow, wide)
    hidden = left_ref.shape[1]
    cot = cot_ref[...]
    grads[0:hidden, :] = dot(left_ref[...], cot, TN).astype(bf16)
    grads[hidden:, :] = dot(right_ref[...], cot, TN).astype(bf16)
    store_pairs(where, grads, out, sems.at[1], narrow, wide)
    wait_all(weight, sems.at[0])
    total = residual_ref[...] + dot(left_ref[...], weight[0:hidden, :])
    total = total + dot(right_ref[...], weight[hidden:, :])
    output_ref[...] = total.astype(bf16)
    wait_all(grads, sems.at[1])


def turn_kernel(
    narrow, wide, places, count, where, residual_ref, ffn_ref, cot_ref, attended_ref, gain_ref, *refs
):
    sources, refs = refs[:count], refs[count:]
    grad_ref, head_ref, gain_out = refs[:3]
    out, (weight, grads, sems) = refs[3:-3], refs[-3:]
    rows = weight.shape[0] // (narrow * wide)
    load_rows(where, sources, places, 0, rows, weight, sems.at[0], narrow, wide)
    residual = residual_ref[...]
    inverse = inverse_rms(residual)
    normed = residual * inverse
    ffn_grad = ffn_ref[...]
    gain_out[...] = jnp.sum(ffn_grad * normed, axis=0, keepdims=True)
    scaled = ffn_grad * gain_ref[...]
    center = jnp.mean(scaled * normed, axis=-1, keepdims=True)
    grad = cot_ref[...].astype(f32) + (scaled - normed * center) * inverse
    grad_ref[...] = grad
    low = grad.astype(bf16)
    grads[...] = dot(attended_ref[...], low).astype(bf16)
    store_rows(where, grads, out, 0, rows, sems.at[1], narrow, wide)
    wait_all(weight, sems.at[0])
    head_ref[...] = dot(weight[...], low, NT).astype(bf16)
    wait_all(grads, sems.at[1])


def attend_back_kernel(
    query_ref, key_ref, value_ref, head_ref, probs_ref, query_out, key_out, value_out, scores_ref
):
    count = query_ref.shape[0]
    keys = key_ref.shape[0]
    low = probs_ref[0]
    head = head_ref[...]
    probs = low.astype(f32)
    prob_grad = dot(by_side(value_ref[...]), head).reshape(keys // 8, 16, count)
    center = per_side(jnp.sum(probs * prob_grad, axis=0), jnp.sum, count)
    score_grad = (probs * (prob_grad - center)).astype(bf16)
    scores_ref[0] = score_grad
    score_grad = score_grad.reshape(keys * 2, count)
    query_grad = dot(by_side(key_ref[...]), score_grad, TN)
    query_out[...] = query_grad.T.astype(bf16)
    key_out[...] = own_side(dot(score_grad, query_ref[...])).astype(bf16)
    value_out[...] = own_side(dot(low.reshape(keys * 2, count), head, NT)).astype(bf16)


def table_kernel(scores_ref, rel_ref, lay_ref, out_ref):
    keys, count = rel_ref.shape
    out_ref[...] = jnp.zeros_like(out_ref)

    def step(g, _):
        rows = pl.ds(pl.multiple_of(g * 8, 8), 8)
        hot = []
        for ids, low, high in ((rel_ref[rows, :], 0, NB_REL), (lay_ref[rows, :], NB_REL, NB)):
            for b in range(low, high, 2):
                pair = [jnp.where(ids == b + n, 1.0, 0.0) for n in range(2)]
                hot.append(jnp.concatenate(pair, axis=0).astype(bf16))
        hot = jnp.concatenate(hot, axis=0)
        grads = scores_ref[:, pl.ds(g, 1)].reshape(H * 8, count)
        out_ref[...] += dot(grads, hot, NT)
        return 0

    lax.fori_loop(0, keys // 8, step, 0)


def project_back_kernel(
    narrow, wide, places, count, where, input_ref, pick_ref, query_ref, key_ref, value_ref,
    tokens_ref, hidden_ref, mask_ref, gain_ref, residual_ref, *refs
):
    sources, refs = refs[:count], refs[count:]
    tokens_out, gain_out, embed_out = refs[:3]
    out, (weights, grads, turned, sems) = refs[3:-4], refs[-4:]
    width = tokens_ref.shape[1]
    rows = width // (narrow * wide)
    for n in range(3):
        load_rows(where, sources, places, n, rows, weights.at[n], sems.at[n], narrow, wide)
    turned[...] = input_ref[...].T
    pick = pick_ref[...]
    spread = [query_ref[...]] + [
        dot(pick, ref[...], TN).astype(bf16) for ref in (key_ref, value_ref)
    ]
    for n in range(3):
        grads[n] = dot(turned[...], spread[n]).astype(bf16)
        store_rows(where, grads.at[n], out, n, rows, sems.at[3 + n], narrow, wide)
    attn_grad = None
    for n in range(3):
        wait_all(weights.at[n], sems.at[n])
        term = dot(spread[n], weights[n], NT)
        attn_grad = term if n == 0 else attn_grad + term
    embedded = embed(tokens_ref, hidden_ref, mask_ref)
    inverse = inverse_rms(embedded)
    normed = embedded * inverse
    gain_out[...] = jnp.sum(attn_grad * normed, axis=0, keepdims=True)
    scaled = attn_grad * gain_ref[...]
    center = jnp.mean(scaled * normed, axis=-1, keepdims=True)
    grad = residual_ref[...] + (scaled - normed * center) * inverse
    concealed = hidden_ref[...] == 1.0
    tokens_out[...] = jnp.where(concealed, 0.0, grad)
    embed_out[...] = jnp.sum(jnp.where(concealed, grad, 0.0), axis=0, keepdims=True)
    for n in range(3):
        wait_all(grads.at[n], sems.at[3 + n])


def shape(dims, kind):
    return jax.ShapeDtypeStruct(tuple(dims), kind)


def local(
    tokens, hidden_patch, segment_ids, rel_ids, layout_ids, w_query, w_key, w_value, w_out, w_gate,
    w_up, w_down, gain_attn, gain_ffn, mask_embed, rel_table, layout_table, cotangent,
):
    narrow, wide = lax.axis_size("narrow"), lax.axis_size("wide")
    devices = narrow * wide
    count, width = tokens.shape
    keys = count - HIDE
    ff = w_gate.shape[1]
    rows = w_query.shape[0]
    where = jnp.stack([lax.axis_index("narrow"), lax.axis_index("wide")]).astype(jnp.int32)
    core = lax.axis_index("wide") % 2

    fine = narrow % 2 == 0 and wide == 8 and rows % 16 == 0 and w_down.shape[0] % 8 == 0
    gather, scatter = (Gather, Scatter) if fine else (PlainGather, PlainScatter)
    steps = Steps()

    def sources_of(pieces, number):
        if fine:
            return piece_arrays(pieces), piece_places(pieces)
        full = ordered(pieces, narrow, wide)
        full = full.reshape((devices, number, -1) + full.shape[2:])
        return [jnp.swapaxes(full, 0, 1).reshape(number, -1, full.shape[-1])], None

    chip_flip, z_index = jnp.meshgrid(jnp.arange(wide // 2), jnp.arange(narrow), indexing="ij")

    def sides(parts):
        flip = (chip_flip * 2) ^ lax.axis_index("wide")
        return [parts[z_index * wide + (flip ^ side)] for side in range(2)]

    def blocks_of(grads, number):
        if fine:
            return grads
        parts = grads[0].reshape(number, devices, -1, grads[0].shape[-1])
        return sides(jnp.swapaxes(parts, 0, 1).reshape(devices, -1, parts.shape[-1]))

    def block_shapes(number, block_rows, lanes):
        if fine:
            return [shape((wide // 2, narrow, number * block_rows, lanes), bf16)] * 2
        return [shape((number, devices * block_rows, lanes), bf16)]

    def call(kernel, in_specs, outs, scratch, flops, *args, mib=56):
        return pl.pallas_call(
            kernel,
            in_specs=in_specs,
            out_specs=[o[0] for o in outs],
            out_shape=[o[1] for o in outs],
            scratch_shapes=scratch,
            compiler_params=params(mib),
            cost_estimate=cost(flops, 0),
        )(*args)

    def vm(dims, kind):
        return (VM, shape(dims, kind))

    def anys(shapes):
        return [(ANY, x) for x in shapes]

    smalls = (gain_attn, gain_ffn, mask_embed, rel_table, layout_table)
    small = gather(narrow, wide, jnp.concatenate([p.astype(bf16) for p in smalls])[None])
    qkv = gather(narrow, wide, jnp.concatenate([w_query, w_key, w_value]).astype(bf16))
    out = gather(narrow, wide, w_out.astype(bf16))
    gu_low = jnp.concatenate([w_gate, w_up]).astype(bf16)
    gu = [gather(narrow, wide, gu_low[:, :SPLIT]), gather(narrow, wide, gu_low[:, SPLIT:])]
    down_low = w_down.astype(bf16)
    if fine:
        half = width // 2
        mine = lax.dynamic_slice_in_dim(down_low, core * half, half, 1)
        other = flip_wide(lax.dynamic_slice_in_dim(down_low, (1 - core) * half, half, 1), 1, wide)
        down_low = jnp.where(
            core == 0, jnp.concatenate([mine, other]), jnp.concatenate([other, mine])
        )
    down = gather(narrow, wide, down_low)

    hidden_column = hidden_patch.astype(f32)[:, None]
    pick, rel_index, lay_index = pl.pallas_call(
        prepare_kernel,
        out_shape=(
            shape((keys, count), bf16), shape((keys, count), jnp.int32), shape((keys, count), jnp.int32),
        ),
        compiler_params=params(),
        cost_estimate=cost(0, 0),
    )(hidden_patch[None], segment_ids[None], rel_ids, layout_ids)

    small.start(steps)
    qkv.start(steps)
    small.plane(steps)
    small.forward(steps)
    small.cores(steps)
    qkv.plane(steps)
    down.start(steps)
    found = ordered(small.finish(steps), narrow, wide)[:, 0].astype(f32)
    pieces, at = [], 0
    for p in smalls:
        pieces.append(found[:, at : at + p.shape[0]].reshape(-1))
        at += p.shape[0]
    attn_gain, ffn_gain, embed_row = [p[None] for p in pieces[:3]]
    table = jnp.concatenate([pieces[3].reshape(NB_REL, H), pieces[4].reshape(NB_LAY, H)])
    table = jnp.concatenate([table.T, jnp.full((H, 128 - NB), neg_large, f32)], axis=1)

    groups = keys // 8
    whole = pl.BlockSpec((keys, count), lambda p: (0, 0))
    table = steps.enter(table)
    bias = pl.pallas_call(
        bias_kernel,
        grid=(PAIRS,),
        in_specs=[pl.BlockSpec((H, 128), lambda p: (0, 0)), whole, whole],
        out_specs=pl.BlockSpec((1, groups, 16, count), lambda p: (p, 0, 0, 0)),
        out_shape=shape((PAIRS, groups, 16, count), f32),
        compiler_params=params(),
        cost_estimate=cost(0, 0),
    )(table, rel_index, lay_index)
    steps.leave(bias)

    qkv.forward(steps)
    down.plane(steps)
    gu[0].start(steps)
    out.start(steps)
    qkv.cores(steps)
    qkv_sources, qkv_places = sources_of(qkv.finish(steps), 3)
    place = steps.enter(where)
    attn_input, query, key, value = call(
        functools.partial(project_kernel, narrow, wide, qkv_places),
        [SM] + [VM] * 5 + [ANY] * len(qkv_sources),
        [vm((count, width), bf16), vm((count, width), bf16), vm((keys, width), bf16), vm((keys, width), bf16)],
        [pltpu.VMEM((3, width, width), bf16), pltpu.SemaphoreType.DMA((3,))],
        0, place, tokens, hidden_column, embed_row, attn_gain, pick, *qkv_sources,
    )
    steps.leave(query)
    down.forward(steps)
    out.plane(steps)
    gu[0].plane(steps)
    gu[1].start(steps)

    row_block = pl.BlockSpec((count, 128), lambda p: (0, p))
    key_block = pl.BlockSpec((keys, 128), lambda p: (0, p))
    turn_block = pl.BlockSpec((128, count), lambda p: (p, 0))
    score_block = pl.BlockSpec((1, groups, 16, count), lambda p: (p, 0, 0, 0))
    query_here = steps.enter(query)
    attended, probs = pl.pallas_call(
        attend_kernel,
        grid=(PAIRS,),
        in_specs=[row_block, key_block, key_block, score_block],
        out_specs=[turn_block, score_block],
        out_shape=(shape((width, count), bf16), shape((PAIRS, groups, 16, count), bf16)),
        compiler_params=params(),
        cost_estimate=cost(0, 0),
    )(query_here, key, value, bias)
    steps.leave(attended)
    down.cores(steps)
    out.forward(steps)
    gu[0].forward(steps)
    gu[1].plane(steps)
    out.cores(steps)
    gu[0].cores(steps)
    out_sources, out_places = sources_of(out.finish(steps), 1)
    place = steps.enter(where)
    residual, ffn_input = call(
        functools.partial(residual_kernel, narrow, wide, out_places),
        [SM] + [VM] * 5 + [ANY] * len(out_sources),
        [vm((count, width), f32), vm((count, width), bf16)],
        [pltpu.VMEM((width, width), bf16), pltpu.SemaphoreType.DMA],
        0, place, attended, tokens, hidden_column, embed_row, ffn_gain, *out_sources,
    )
    steps.leave(residual)
    gu[1].forward(steps)
    down_sources, down_places = sources_of(down.finish(steps), 1)

    acc, active, gu_sums = None, [], []
    for part, size in enumerate((SPLIT, ff - SPLIT)):
        if part == 1:
            gu[1].cores(steps)
        sources, places = sources_of(gu[part].finish(steps), 2)
        if part == 1:
            gu_sums[0].plane(steps)
        shapes = block_shapes(2, rows, size)
        place = steps.enter(where)
        extra = () if part == 0 else (acc,)
        results = call(
            functools.partial(
                ffn_kernel, narrow, wide, part * SPLIT,
                (len(sources), len(down_sources), len(shapes)), places, down_places,
            ),
            [SM, VM, VM] + [ANY] * (len(sources) + len(down_sources)) + [VM] * len(extra),
            anys(shapes) + [vm((count, size), bf16), vm((count, width), f32)],
            [
                pltpu.VMEM((2, width, size), bf16), pltpu.VMEM((ff, width), bf16),
                pltpu.VMEM((2, width, size), bf16), pltpu.VMEM((width, count), bf16),
                pltpu.SemaphoreType.DMA((3,)),
            ],
            0, place, ffn_input, cotangent, *sources, *down_sources, *extra, mib=60,
        )
        act, acc = results[-2:]
        active.append(act)
        steps.leave(acc)
        gu_sums.append(scatter(narrow, wide, *blocks_of(results[:-2], 2)))

    shapes = block_shapes(1, rows, width)
    place = steps.enter(where)
    residual_grad, head, ffn_gain_part, *out_grads = call(
        functools.partial(turn_kernel, narrow, wide, out_places, len(out_sources)),
        [SM] + [VM] * 5 + [ANY] * len(out_sources),
        [vm((count, width), f32), vm((width, count), bf16), vm((1, width), f32)] + anys(shapes),
        [
            pltpu.VMEM((width, width), bf16), pltpu.VMEM((width, width), bf16),
            pltpu.SemaphoreType.DMA((2,)),
        ],
        0, place, residual, acc, cotangent, attended, ffn_gain, *out_sources,
    )
    steps.leave(head)
    out_sum = scatter(narrow, wide, *blocks_of(out_grads, 1))
    gu_sums[0].forward(steps)
    gu_sums[1].plane(steps)

    query_here = steps.enter(query)
    query_grad, key_grad, value_grad, score_grads = pl.pallas_call(
        attend_back_kernel,
        grid=(PAIRS,),
        in_specs=[row_block, key_block, key_block, turn_block, score_block],
        out_specs=[row_block, key_block, key_block, score_block],
        out_shape=(
            shape((count, width), bf16), shape((keys, width), bf16), shape((keys, width), bf16),
            shape((PAIRS, groups, 16, count), bf16),
        ),
        compiler_params=params(),
        cost_estimate=cost(0, 0),
    )(query_here, key, value, head, probs)
    steps.leave(query_grad)
    gu_sums[0].column(steps)
    gu_sums[1].forward(steps)
    out_sum.plane(steps)

    shapes = block_shapes(3, rows, width)
    place = steps.enter(where)
    tokens_grad, attn_gain_part, embed_part, *qkv_grads = call(
        functools.partial(project_back_kernel, narrow, wide, qkv_places, len(qkv_sources)),
        [SM] + [VM] * 10 + [ANY] * len(qkv_sources),
        [vm((count, width), f32), vm((1, width), f32), vm((1, width), f32)] + anys(shapes),
        [
            pltpu.VMEM((3, width, width), bf16), pltpu.VMEM((3, width, width), bf16),
            pltpu.VMEM((width, count), bf16), pltpu.SemaphoreType.DMA((6,)),
        ],
        0, place, attn_input, pick, query_grad, key_grad, value_grad, tokens, hidden_column, embed_row,
        attn_gain, residual_grad, *qkv_sources,
    )
    steps.leave(tokens_grad)
    qkv_sum = scatter(narrow, wide, *blocks_of(qkv_grads, 3))
    gu_sums[1].column(steps)
    out_sum.forward(steps)
    qkv_sum.plane(steps)
    gu_first = gu_sums[0].finish(steps)

    if fine:
        shapes = [shape((wide // 2, narrow, 2 * w_down.shape[0], width // 2), bf16)] * 2
    else:
        shapes = [shape((1, ff, width), bf16)]
    place = steps.enter(where)
    output, *down_grads = call(
        functools.partial(down_kernel, narrow, wide, down_places, len(down_sources)),
        [SM] + [VM] * 4 + [ANY] * len(down_sources),
        [vm((count, width), bf16)] + anys(shapes),
        [pltpu.VMEM((ff, width), bf16), pltpu.VMEM((ff, width), bf16), pltpu.SemaphoreType.DMA((2,))],
        0, place, active[0], active[1], cotangent, residual, *down_sources, mib=60,
    )
    steps.leave(output)
    down_sum = scatter(narrow, wide, *blocks_of(down_grads, 1))
    qkv_sum.forward(steps)
    out_sum.column(steps)
    down_sum.plane(steps)
    gu_second = gu_sums[1].finish(steps)

    scores_here = steps.enter(score_grads)
    table_grads = pl.pallas_call(
        table_kernel,
        out_shape=shape((H * 8, NB * 8), f32),
        compiler_params=params(),
        cost_estimate=cost(0, 0),
    )(scores_here, rel_index, lay_index)
    steps.leave(table_grads)
    qkv_sum.column(steps)
    down_sum.forward(steps)
    table_grads = jnp.einsum("hjbj->bh", table_grads.reshape(H, 8, NB, 8))
    vectors = (attn_gain_part, ffn_gain_part, embed_part, table_grads[:NB_REL], table_grads[NB_REL:])
    vectors = jnp.concatenate([v.reshape(devices, -1) for v in vectors], axis=1).astype(bf16)
    small_sum = scatter(narrow, wide, *sides(vectors[:, None]))
    small_sum.plane(steps)
    out_total = out_sum.finish(steps)
    down_sum.column(steps)
    small_sum.forward(steps)
    qkv_total = qkv_sum.finish(steps)
    small_sum.column(steps)
    down_total = down_sum.finish(steps)
    if fine:
        rows_here = w_down.shape[0]
        mine = lax.dynamic_slice_in_dim(down_total, core * rows_here, rows_here, 0)
        other = lax.dynamic_slice_in_dim(down_total, (1 - core) * rows_here, rows_here, 0)
        other = flip_wide(other, 1, wide)
        down_total = jnp.where(
            core == 0, jnp.concatenate([mine, other], 1), jnp.concatenate([other, mine], 1)
        )
    small_total = small_sum.finish(steps)[0]
    small_out, at = [], 0
    for p in smalls:
        small_out.append(small_total[at : at + p.shape[0]])
        at += p.shape[0]
    gu_total = jnp.concatenate([gu_first, gu_second], axis=1)
    return (
        output, tokens_grad, qkv_total[:rows], qkv_total[rows : 2 * rows], qkv_total[2 * rows :],
        out_total, gu_total[:rows], gu_total[rows:], down_total, *small_out,
    )


def solution(mesh):
    both = P(("narrow", "wide"))
    table = P(("narrow", "wide"), None)
    return jax.shard_map(
        local,
        mesh=mesh,
        in_specs=(table, both, both) + (table,) * 9 + (both,) * 5 + (table,),
        out_specs=(table,) * 9 + (both,) * 5,
        check_vma=False,
    )
```

```python
import functools
import math

import jax
import jax.numpy as jnp
from jax import lax
from jax.experimental import pallas as pl
from jax.experimental.pallas import tpu as pltpu
from jax.sharding import PartitionSpec as P

H = 16
HD = 64
PAIRS = H // 2
NB_REL = 32
NB_LAY = 64
NB = NB_REL + NB_LAY
HIDE = 192
PARTS = (2048, 768)
FF_STEP = 1024

eps_norm = 1e-06
neg_large = -1e30
f32 = jnp.float32
bf16 = jnp.bfloat16

NN = (((1,), (0,)), ((), ()))
NT = (((1,), (1,)), ((), ()))
TN = (((0,), (0,)), ((), ()))


def dot(a, b, dims=NN):
    return lax.dot_general(a, b, dims, preferred_element_type=f32)


def params(mib=56):
    return pltpu.CompilerParams(vmem_limit_bytes=mib * 1024 * 1024)


def cost(us):
    return pl.CostEstimate(flops=int(us * 1.5e9), bytes_accessed=0, transcendentals=0)


VM = pl.BlockSpec(memory_space=pltpu.VMEM)
SM = pl.BlockSpec(memory_space=pltpu.SMEM)
ANY = pl.BlockSpec(memory_space=pl.ANY)


def shift_narrow(x, step, count):
    return lax.ppermute(x, "narrow", [(i, (i + step) % count) for i in range(count)])


def flip_wide(x, bits, count):
    return lax.ppermute(x, "wide", [(i, i ^ bits) for i in range(count)])


class Steps:
    def __init__(self):
        self.last = ()

    def enter(self, *values):
        out = lax.optimization_barrier(tuple(values) + self.last)
        return out[: len(values)] if len(values) > 1 else out[0]

    def leave(self, *values):
        self.last = tuple(values)


class Columns:
    def __init__(self, narrow, x):
        self.narrow, self.x = narrow, x

    def start(self, steps):
        x = steps.enter(self.x)
        self.sent = [x] + [shift_narrow(x, s, self.narrow) for s in range(1, self.narrow)]

    def finish(self, steps, bounds=None):
        sent = steps.enter(*self.sent)
        if bounds is None:
            columns = [jnp.stack(sent)]
        else:
            columns = [
                jnp.stack([x[:, low:high] for x in sent])
                for low, high in zip(bounds[:-1], bounds[1:])
            ]
        steps.leave(*columns)
        return columns


class Gather:
    def __init__(self, wide, first=2, second=4, direct=False):
        self.wide, self.bits, self.direct = wide, (first, second), direct

    def add(self, array, chip):
        self.pieces.append((array, 0, chip))
        self.crossed.append((flip_wide(array, 1, self.wide), 1, chip))

    def plane(self, steps, column):
        column = steps.enter(column)
        steps.leave(column)
        self.near = [flip_wide(column, bit, self.wide) for bit in self.bits]
        if self.direct:
            self.far = flip_wide(column, 6, self.wide)
        self.pieces, self.crossed = [], []
        self.add(column, 0)

    def forward(self, steps):
        near, other = steps.enter(*self.near)
        steps.leave(near)
        if not self.direct:
            self.far = flip_wide(near, self.bits[1], self.wide)
        self.add(near, self.bits[0] // 2)
        self.add(other, self.bits[1] // 2)

    def arrive(self, steps):
        far = steps.enter(self.far)
        steps.leave(far)
        self.add(far, 3)

    def finish(self, steps):
        arrays = steps.enter(*[p[0] for p in self.crossed])
        steps.leave(arrays[-1])
        return self.pieces + [(a,) + p[1:] for a, p in zip(arrays, self.crossed)]


class PlainGather(Gather):
    def plane(self, steps, column):
        column = steps.enter(column)
        steps.leave(column)
        found = {0: column}
        bit = 2
        while bit < self.wide:
            for at in list(found):
                found[at ^ bit] = flip_wide(found[at], bit, self.wide)
            bit *= 2
        self.pieces, self.crossed = [], []
        for at, array in found.items():
            self.add(array, at // 2)

    def forward(self, steps):
        pass

    def arrive(self, steps):
        pass


def ordered(pieces, narrow, wide):
    table = [None] * wide
    for array, core, chip in pieces:
        table[2 * chip + core] = array
    order = jnp.arange(wide) ^ lax.axis_index("wide")
    shift = (lax.axis_index("narrow") - jnp.arange(narrow)) % narrow
    full = jnp.stack(table, axis=1)[shift[:, None], order[None]]
    return full.reshape((narrow * wide,) + full.shape[2:])


class Scatter:
    def __init__(self, narrow, wide, keep, send, first=2, second=4):
        self.narrow, self.wide, self.keep, self.bits = narrow, wide, keep, (first, second)
        self.sent = flip_wide(send, 1, wide)

    def plane(self, steps):
        sent = steps.enter(self.sent)
        mine = [
            (self.keep[n].astype(f32) + sent[n].astype(f32)).astype(bf16) for n in range(self.wide // 2)
        ]
        steps.leave(*mine)
        self.mine = mine
        second = self.bits[1]
        self.far = flip_wide(mine[3], second, self.wide)
        self.straight = flip_wide(mine[second // 2], second, self.wide)

    def forward(self, steps, both=False):
        if both:
            far, self.straight = steps.enter(self.far, self.straight)
        else:
            far = steps.enter(self.far)
        first = self.bits[0]
        both = (self.mine[first // 2].astype(f32) + far.astype(f32)).astype(bf16)
        steps.leave(both)
        self.near = flip_wide(both, first, self.wide)

    def column(self, steps):
        straight, near = steps.enter(self.straight, self.near)
        total = self.mine[0].astype(f32) + straight.astype(f32) + near.astype(f32)
        total = total.astype(bf16)
        steps.leave(total)
        return total


class Rows:
    def __init__(self, narrow, mine):
        z = lax.axis_index("narrow")
        self.own = lax.dynamic_index_in_dim(mine, z, 0, False)
        self.sent = [
            shift_narrow(lax.dynamic_index_in_dim(mine, (z + s) % narrow, 0, False), s, narrow)
            for s in range(1, narrow)
        ]

    def finish(self, steps):
        sent = steps.enter(*self.sent)
        total = self.own.astype(f32)
        for s in sent:
            total = total + s.astype(f32)
        steps.leave(total)
        return total


class PlainScatter(Scatter):
    def plane(self, steps):
        sent = steps.enter(self.sent)
        mine = self.keep.astype(f32) + sent.astype(f32)
        bit = self.wide // 2
        while bit > 1:
            half = mine.shape[0] // 2
            low = mine.astype(bf16)
            mine = low[:half].astype(f32) + flip_wide(low[half:], bit, self.wide).astype(f32)
            bit //= 2
        self.total = mine[0].astype(bf16)

    def forward(self, steps, both=False):
        pass

    def column(self, steps):
        return self.total


def piece_arrays(pieces):
    return [p[0] for p in pieces]


def piece_places(pieces):
    return [p[1:] for p in pieces]


def load_rows(where, sources, places, index, rows, dst, sem, narrow, wide):
    if places is None:
        pltpu.make_async_copy(sources[0].at[index], dst, sem).start()
        return
    for src, (core, chip) in zip(sources, places):
        w = jnp.bitwise_xor(where[1], 2 * chip + core)
        for n in range(narrow):
            z = lax.rem(where[0] - n + narrow, narrow)
            row = pl.multiple_of((z * wide + w) * rows, rows)
            pltpu.make_async_copy(
                src.at[n, pl.ds(index * rows, rows)], dst.at[pl.ds(row, rows), :], sem
            ).start()


def load_pairs(where, sources, places, dst, sem, narrow, wide):
    if places is None:
        pltpu.make_async_copy(sources[0].at[0], dst, sem).start()
        return
    for src, (core, chip) in zip(sources, places):
        rows, lanes = src.shape[1:]
        c = jnp.bitwise_xor(lax.shift_right_logical(where[1], 1), chip)
        lane = pl.multiple_of(jnp.bitwise_xor(jnp.bitwise_and(where[1], 1), core) * lanes, lanes)
        for n in range(narrow):
            z = lax.rem(where[0] - n + narrow, narrow)
            row = pl.multiple_of((z * (wide // 2) + c) * rows, rows)
            pltpu.make_async_copy(
                src.at[n], dst.at[pl.ds(row, rows), pl.ds(lane, lanes)], sem
            ).start()


def wait_all(ref, sem):
    pltpu.make_async_copy(ref, ref, sem).wait()


def store_rows(where, src, out, index, rows, sem, narrow, wide):
    if len(out) == 1:
        pltpu.make_async_copy(src, out[0].at[index], sem).start()
        return
    core = jnp.bitwise_and(where[1], 1)
    chip = lax.shift_right_logical(where[1], 1)
    for z in range(narrow):
        for c in range(wide // 2):
            flip = jnp.bitwise_xor(chip, c)
            for dst, side in zip(out, (core, 1 - core)):
                row = pl.multiple_of((z * wide + 2 * c + side) * rows, rows)
                pltpu.make_async_copy(
                    src.at[pl.ds(row, rows), :], dst.at[flip, z, pl.ds(index * rows, rows)], sem
                ).start()


def store_pairs(where, src, out, sem, narrow, wide):
    if len(out) == 1:
        pltpu.make_async_copy(src, out[0].at[0], sem).start()
        return
    core = jnp.bitwise_and(where[1], 1)
    chip = lax.shift_right_logical(where[1], 1)
    rows, lanes = out[0].shape[2:]
    for z in range(narrow):
        for c in range(wide // 2):
            flip = jnp.bitwise_xor(chip, c)
            for dst, side in zip(out, (core, 1 - core)):
                lane = pl.multiple_of(side * lanes, lanes)
                pltpu.make_async_copy(
                    src.at[pl.ds((z * (wide // 2) + c) * rows, rows), pl.ds(lane, lanes)],
                    dst.at[flip, z],
                    sem,
                ).start()


def prepare_kernel(hidden_ref, segment_ref, rel_ref, lay_ref, pick_ref, rel_out, lay_out):
    count = hidden_ref.shape[1]
    keys = pick_ref.shape[0]
    seen = hidden_ref[...] == 0
    before = lax.broadcasted_iota(jnp.int32, (count, count), 0)
    after = lax.broadcasted_iota(jnp.int32, (count, count), 1)
    upper = jnp.where(before <= after, 1.0, 0.0).astype(bf16)
    seen_rows = jnp.broadcast_to(jnp.where(seen, 1.0, 0.0), (16, count)).astype(bf16)
    rank = dot(seen_rows, upper)[0:1].astype(jnp.int32) - 1
    rank = jnp.where(seen, rank, -1)
    number = lax.broadcasted_iota(jnp.int32, (keys, count), 0)
    pick = jnp.where(number == rank, 1.0, 0.0).astype(bf16)
    pick_ref[...] = pick
    segment = jnp.broadcast_to(segment_ref[...].astype(f32), (16, count)).astype(bf16)
    key_segment = dot(pick, segment, NT)[:, 0:1]
    valid = key_segment == segment_ref[...].astype(f32)
    rel = dot(pick, rel_ref[...].astype(f32).astype(bf16), NT).astype(jnp.int32)
    lay = dot(pick, lay_ref[...].astype(f32).astype(bf16), NT).astype(jnp.int32)
    rel_out[...] = jnp.where(valid, rel, NB)
    lay_out[...] = lay + NB_REL


def bias_kernel(low, table_ref, rel_ref, lay_ref, *refs):
    out_ref = refs[-1]
    keys, count = rel_ref.shape
    groups = keys // 8
    pair = pl.program_id(0) + low
    tables = [
        jnp.broadcast_to(table_ref[pl.ds(2 * pair + side, 1), :], (keys, 128)) for side in range(2)
    ]
    for c in range(count // 128):
        lanes = slice(c * 128, c * 128 + 128)
        for side in range(2):
            found = jnp.take_along_axis(tables[side], rel_ref[:, lanes], axis=1)
            found = found + jnp.take_along_axis(tables[side], lay_ref[:, lanes], axis=1)
            out_ref[0, :, side * 8 : side * 8 + 8, lanes] = found.reshape(groups, 8, 128)


def embed(tokens_ref, hidden_ref, vectors_ref):
    return jnp.where(hidden_ref[...] == 1.0, vectors_ref[2:3, :], tokens_ref[...].astype(f32))


def inverse_rms(v):
    return lax.rsqrt(jnp.mean(v * v, axis=-1, keepdims=True) + eps_norm)


def pack_kernel(where, wide, lengths, *refs):
    query, key, value, out, gate, up, down, smalls = refs[:8]
    attn_ref, first_ref, second_ref = refs[8:11]
    rows = query.shape[0]
    for n, ref in enumerate((query, key, value, out)):
        attn_ref[n * rows : (n + 1) * rows, :] = ref[...].astype(bf16)
    own = where[0] * wide + where[1]
    row = lax.broadcasted_iota(jnp.int32, smalls.shape, 0)
    placed = jnp.zeros(smalls.shape, f32)
    for length in sorted(set(lengths)):
        moved = pltpu.roll(smalls[...], own * length, 1)
        for n, other in enumerate(lengths):
            if other == length:
                placed = jnp.where(row == n, moved, placed)
    attn_ref[4 * rows :, :] = placed.astype(bf16)
    size = first_ref.shape[1]
    for n, ref in enumerate((gate, up)):
        first_ref[n * rows : (n + 1) * rows, :] = ref[:, 0:size].astype(bf16)
        second_ref[n * rows : (n + 1) * rows, :] = ref[:, size:].astype(bf16)
    if len(refs) == 12:
        refs[11][...] = down[...].astype(bf16)
    else:
        half = down.shape[1] // 2
        core = jnp.bitwise_and(where[1], 1)
        for n, side in enumerate((core, 1 - core)):
            lanes = pl.ds(pl.multiple_of(side * half, half), half)
            refs[11 + n][...] = down[:, lanes].astype(bf16)


def project_kernel(narrow, wide, places, where, tokens_ref, hidden_ref, pick_ref, *refs):
    sources = refs[:-9]
    input_ref, query_ref, key_ref, value_ref, vectors_ref, table_ref, weights, smalls, sems = refs[-9:]
    width = tokens_ref.shape[1]
    rows = width // (narrow * wide)
    for n, src in enumerate(sources[1:] if places is None else sources):
        low = 0 if places is None else 4 * rows
        pltpu.make_async_copy(src.at[:, pl.ds(low, 16)], smalls.at[n], sems.at[3]).start()
    for n in range(3):
        load_rows(where, sources, places, n, rows, weights.at[n], sems.at[n], narrow, wide)
    wait_all(smalls, sems.at[3])
    vectors = jnp.sum(smalls[...].astype(f32).reshape((-1, 16, width)), axis=0)
    vectors_ref[...] = vectors[0:8]
    lane = lax.broadcasted_iota(jnp.int32, (H, width), 1)
    head = lax.broadcasted_iota(jnp.int32, (H, width), 0)
    entry = lax.broadcasted_iota(jnp.int32, (width, 128), 0) // H
    bucket = lax.broadcasted_iota(jnp.int32, (width, 128), 1)
    end = lax.broadcasted_iota(jnp.int32, (H, 128), 1)
    table = jnp.where(end >= NB, neg_large, 0.0)
    for n, first in ((3, 0), (4, NB_REL)):
        split = jnp.where(lane % H == head, vectors[n : n + 1], 0.0).astype(bf16)
        spot = jnp.where(entry + first == bucket, 1.0, 0.0).astype(bf16)
        table = table + dot(split, spot)
    table_ref[...] = table
    embedded = embed(tokens_ref, hidden_ref, vectors_ref)
    attn_input = (embedded * inverse_rms(embedded) * vectors_ref[0:1, :]).astype(bf16)
    input_ref[...] = attn_input
    seen = dot(pick_ref[...], attn_input).astype(bf16)
    wait_all(weights.at[0], sems.at[0])
    query_ref[...] = dot(attn_input, weights[0]).astype(bf16)
    wait_all(weights.at[1], sems.at[1])
    key_ref[...] = dot(seen, weights[1]).astype(bf16)
    wait_all(weights.at[2], sems.at[2])
    value_ref[...] = dot(seen, weights[2]).astype(bf16)


def by_side(x):
    keys = x.shape[0]
    wide = x.astype(f32).reshape(keys // 8, 8, 128)
    left = lax.broadcasted_iota(jnp.int32, wide.shape, 2) < HD
    both = jnp.concatenate([jnp.where(left, wide, 0.0), jnp.where(left, 0.0, wide)], axis=1)
    return both.astype(bf16).reshape(keys * 2, 128)


def own_side(x):
    x = x.reshape(x.shape[0] // 16, 16, 128)
    left = lax.broadcasted_iota(jnp.int32, (x.shape[0], 8, 128), 2) < HD
    return jnp.where(left, x[:, 0:8], x[:, 8:16]).reshape(x.shape[0] * 8, 128)


def per_side(x, fold, spread):
    return jnp.concatenate(
        [
            jnp.broadcast_to(fold(x[side * 8 : side * 8 + 8], axis=0, keepdims=True), (8, spread))
            for side in range(2)
        ],
        axis=0,
    )[None]


def attend_kernel(query_ref, key_ref, value_ref, bias_ref, attended_ref, probs_ref):
    count = query_ref.shape[0]
    keys = key_ref.shape[0]
    scores = dot(by_side(key_ref[...]), query_ref[...], NT).reshape(keys // 8, 16, count)
    scores = scores + bias_ref[0]
    top = per_side(jnp.max(scores, axis=0), jnp.max, count)
    exponent = jnp.exp(scores - top)
    total = per_side(jnp.sum(exponent, axis=0), jnp.sum, count)
    probs = (exponent * (1.0 / total)).astype(bf16)
    probs_ref[0] = probs
    attended = dot(by_side(value_ref[...]), probs.reshape(keys * 2, count), TN)
    attended_ref[...] = attended.astype(bf16)


def residual_kernel(
    narrow, wide, places, where, attended_ref, tokens_ref, hidden_ref, vectors_ref, *refs
):
    sources = refs[:-4]
    residual_ref, input_ref, weight, sem = refs[-4:]
    rows = weight.shape[0] // (narrow * wide)
    load_rows(where, sources, places, 3, rows, weight, sem, narrow, wide)
    embedded = embed(tokens_ref, hidden_ref, vectors_ref)
    wait_all(weight, sem)
    residual = embedded + dot(attended_ref[...], weight[...], TN)
    residual_ref[...] = residual
    input_ref[...] = (residual * inverse_rms(residual) * vectors_ref[1:2, :]).astype(bf16)


def gelu_parts(v):
    scale = math.sqrt(2.0 / math.pi)
    square = v * v
    bend = jnp.tanh(scale * v * (1.0 + 0.044715 * square))
    half = 0.5 * (1.0 + bend)
    slope = half + 0.5 * v * (1.0 - bend * bend) * (scale * (1.0 + 3 * 0.044715 * square))
    return v * half, slope


def ffn_kernel(narrow, wide, low, counts, places, down_places, where, input_ref, cot_ref, *refs):
    sources, refs = refs[: counts[0]], refs[counts[0] :]
    down_sources, refs = refs[: counts[1]], refs[counts[1] :]
    acc_in, refs = (None, refs) if low == 0 else (refs[0], refs[1:])
    out, refs = refs[: counts[2]], refs[counts[2] :]
    active_ref, acc_ref, weights, down_ref, grads, turned, sems = refs
    width = input_ref.shape[1]
    rows = width // (narrow * wide)
    size = active_ref.shape[1]
    for n in range(2):
        load_rows(where, sources, places, n, rows, weights.at[n], sems.at[n], narrow, wide)
    load_pairs(where, down_sources, down_places, down_ref, sems.at[2], narrow, wide)
    x = input_ref[...]
    turned[...] = x.T
    steps = [slice(at, min(at + FF_STEP, size)) for at in range(0, size, FF_STEP)]
    acc = None if acc_in is None else acc_in[...]
    for at, lanes in enumerate(steps):
        if at == 0:
            wait_all(weights.at[0], sems.at[0])
        gate = dot(x, weights[0, :, lanes])
        gelu, slope = gelu_parts(gate)
        if at == 0:
            wait_all(weights.at[1], sems.at[1])
        up = dot(x, weights[1, :, lanes])
        active_ref[:, lanes] = (gelu * up).astype(bf16)
        if at == 0:
            wait_all(down_ref, sems.at[2])
        act_grad = dot(cot_ref[...], down_ref[low + lanes.start : low + lanes.stop, :], NT)
        up_back = (act_grad * gelu).astype(bf16)
        gate_back = (act_grad * up * slope).astype(bf16)
        last = at == len(steps) - 1
        for n, back in ((1, up_back), (0, gate_back)):
            grads[n, :, lanes] = dot(turned[...], back).astype(bf16)
            if last:
                store_rows(where, grads.at[n], out, n, rows, sems.at[n], narrow, wide)
        for n, back in ((1, up_back), (0, gate_back)):
            term = dot(back, weights[n, :, lanes], NT)
            acc = term if acc is None else acc + term
    acc_ref[...] = acc
    for n in range(2):
        wait_all(grads.at[n], sems.at[n])


def turn_kernel(narrow, wide, places, down_places, counts, where, *refs):
    residual_ref, ffn_ref, cot_ref, attended_ref, vectors_ref = refs[:5]
    actives, refs = refs[5 : 5 + len(PARTS)], refs[5 + len(PARTS) :]
    sources, down_sources, refs = refs[: counts[0]], refs[counts[0] : counts[0] + counts[1]], refs[sum(counts) :]
    grad_ref, head_ref, gain_out, output_ref = refs[:4]
    weight, grads, down, down_grads, sems = refs[-5:]
    out, down_out = refs[4:-5][: len(refs[4:-5]) // 2], refs[4:-5][len(refs[4:-5]) // 2 :]
    rows = weight.shape[0] // (narrow * wide)
    load_rows(where, sources, places, 3, rows, weight, sems.at[0], narrow, wide)
    load_pairs(where, down_sources, down_places, down, sems.at[2], narrow, wide)
    cot = cot_ref[...]
    residual = residual_ref[...]
    inverse = inverse_rms(residual)
    normed = residual * inverse
    ffn_grad = ffn_ref[...]
    gain_out[...] = jnp.sum(ffn_grad * normed, axis=0, keepdims=True)
    scaled = ffn_grad * vectors_ref[1:2, :]
    center = jnp.mean(scaled * normed, axis=-1, keepdims=True)
    grad = cot.astype(f32) + (scaled - normed * center) * inverse
    grad_ref[...] = grad
    low = grad.astype(bf16)
    grads[...] = dot(attended_ref[...], low).astype(bf16)
    store_rows(where, grads, out, 0, rows, sems.at[1], narrow, wide)
    at = 0
    for ref in actives:
        down_grads[at : at + ref.shape[1], :] = dot(ref[...], cot, TN).astype(bf16)
        at += ref.shape[1]
    store_pairs(where, down_grads, down_out, sems.at[3], narrow, wide)
    wait_all(weight, sems.at[0])
    head_ref[...] = dot(weight[...], low, NT).astype(bf16)
    wait_all(down, sems.at[2])
    total = residual
    at = 0
    for ref in actives:
        total = total + dot(ref[...], down[at : at + ref.shape[1], :])
        at += ref.shape[1]
    output_ref[...] = total.astype(bf16)
    wait_all(grads, sems.at[1])
    wait_all(down_grads, sems.at[3])


def attend_back_kernel(
    query_ref, key_ref, value_ref, head_ref, probs_ref, query_out, key_out, value_out, scores_ref
):
    count = query_ref.shape[0]
    keys = key_ref.shape[0]
    low = probs_ref[0]
    head = head_ref[...]
    probs = low.astype(f32)
    prob_grad = dot(by_side(value_ref[...]), head).reshape(keys // 8, 16, count)
    center = per_side(jnp.sum(probs * prob_grad, axis=0), jnp.sum, count)
    score_grad = (probs * (prob_grad - center)).astype(bf16)
    scores_ref[0] = score_grad
    score_grad = score_grad.reshape(keys * 2, count)
    query_grad = dot(by_side(key_ref[...]), score_grad, TN)
    query_out[...] = query_grad.T.astype(bf16)
    key_out[...] = own_side(dot(score_grad, query_ref[...])).astype(bf16)
    value_out[...] = own_side(dot(low.reshape(keys * 2, count), head, NT)).astype(bf16)


def table_kernel(scores_ref, rel_ref, lay_ref, out_ref, total):
    keys, count = rel_ref.shape
    total[...] = jnp.zeros_like(total)

    def step(g, _):
        rows = pl.ds(pl.multiple_of(g * 8, 8), 8)
        hot = []
        for ids, low, high in ((rel_ref[rows, :], 0, NB_REL), (lay_ref[rows, :], NB_REL, NB)):
            for b in range(low, high, 2):
                pair = [jnp.where(ids == b + n, 1.0, 0.0) for n in range(2)]
                hot.append(jnp.concatenate(pair, axis=0).astype(bf16))
        hot = jnp.concatenate(hot, axis=0)
        grads = scores_ref[:, pl.ds(g, 1)].reshape(H * 8, count)
        total[...] += dot(hot, grads, NT)
        return 0

    lax.fori_loop(0, keys // 8, step, 0)
    row = lax.broadcasted_iota(jnp.int32, total.shape, 0) % 8
    lane = lax.broadcasted_iota(jnp.int32, total.shape, 1) % 8
    own = jnp.where(row == lane, total[...], 0.0)
    own = jnp.sum(own.reshape(NB, 8, H * 8), axis=1)
    fold = lax.broadcasted_iota(jnp.int32, (H * 8, 128), 0) // 8
    fold = jnp.where(fold == lax.broadcasted_iota(jnp.int32, (H * 8, 128), 1), 1.0, 0.0)
    out_ref[...] = jnp.dot(own, fold, precision=lax.Precision.HIGHEST, preferred_element_type=f32)


def spread_rows(pick_ref, ref):
    return dot(pick_ref[...], ref[...], TN).astype(bf16)


def project_grads_kernel(
    narrow, wide, where, input_ref, pick_ref, query_ref, key_ref, value_ref, key_out, value_out, *refs
):
    out, (grads, turned, sems) = refs[:-3], refs[-3:]
    rows = turned.shape[0] // (narrow * wide)
    turned[...] = input_ref[...].T
    key_out[...] = spread_rows(pick_ref, key_ref)
    value_out[...] = spread_rows(pick_ref, value_ref)
    for n, ref in enumerate((query_ref, key_out, value_out)):
        grads[n] = dot(turned[...], ref[...]).astype(bf16)
        store_rows(where, grads.at[n], out, n, rows, sems.at[n], narrow, wide)
    for n in range(3):
        wait_all(grads.at[n], sems.at[n])


def project_back_kernel(
    narrow, wide, places, count, where, query_ref, key_ref, value_ref, tokens_ref, hidden_ref,
    vectors_ref, residual_ref, *refs
):
    sources, refs = refs[:count], refs[count:]
    tokens_out, gain_out, embed_out, weights, sems = refs
    rows = weights.shape[1] // (narrow * wide)
    for n in range(3):
        load_rows(where, sources, places, n, rows, weights.at[n], sems.at[n], narrow, wide)
    embedded = embed(tokens_ref, hidden_ref, vectors_ref)
    inverse = inverse_rms(embedded)
    normed = embedded * inverse
    attn_grad = None
    for n, ref in enumerate((query_ref, key_ref, value_ref)):
        wait_all(weights.at[n], sems.at[n])
        term = dot(ref[...], weights[n], NT)
        attn_grad = term if n == 0 else attn_grad + term
    gain_out[...] = jnp.sum(attn_grad * normed, axis=0, keepdims=True)
    scaled = attn_grad * vectors_ref[0:1, :]
    center = jnp.mean(scaled * normed, axis=-1, keepdims=True)
    grad = residual_ref[...] + (scaled - normed * center) * inverse
    concealed = hidden_ref[...] == 1.0
    tokens_out[...] = jnp.where(concealed, 0.0, grad)
    embed_out[...] = jnp.sum(jnp.where(concealed, grad, 0.0), axis=0, keepdims=True)


def shape(dims, kind):
    return jax.ShapeDtypeStruct(tuple(dims), kind)


def local(
    tokens, hidden_patch, segment_ids, rel_ids, layout_ids, w_query, w_key, w_value, w_out, w_gate,
    w_up, w_down, gain_attn, gain_ffn, mask_embed, rel_table, layout_table, cotangent,
):
    narrow, wide = lax.axis_size("narrow"), lax.axis_size("wide")
    devices = narrow * wide
    count, width = tokens.shape
    keys = count - HIDE
    ff = w_gate.shape[1]
    rows = w_query.shape[0]
    where = jnp.stack([lax.axis_index("narrow"), lax.axis_index("wide")]).astype(jnp.int32)
    core = lax.axis_index("wide") % 2

    fine = narrow % 2 == 0 and wide == 8 and rows % 16 == 0 and w_down.shape[0] % 8 == 0
    gather, scatter = (Gather, Scatter) if fine else (PlainGather, PlainScatter)
    steps = Steps()

    def sources_of(pieces, low_rows):
        if fine:
            return piece_arrays(pieces), piece_places(pieces)
        full = ordered(pieces, narrow, wide)
        full = full.reshape((devices, full.shape[1] // low_rows, -1) + full.shape[2:])
        return [jnp.swapaxes(full, 0, 1).reshape(full.shape[1], -1, full.shape[-1])], None

    chip_flip, z_index = jnp.meshgrid(jnp.arange(wide // 2), jnp.arange(narrow), indexing="ij")

    def sides(parts):
        flip = (chip_flip * 2) ^ lax.axis_index("wide")
        return [parts[z_index * wide + (flip ^ side)] for side in range(2)]

    def blocks_of(grads, number):
        if fine:
            return grads
        parts = grads[0].reshape(number, devices, -1, grads[0].shape[-1])
        return sides(jnp.swapaxes(parts, 0, 1).reshape(devices, -1, parts.shape[-1]))

    def block_shapes(number, block_rows, lanes):
        if fine:
            return [shape((wide // 2, narrow, number * block_rows, lanes), bf16)] * 2
        return [shape((number, devices * block_rows, lanes), bf16)]

    def call(kernel, in_specs, outs, scratch, us, *args, mib=56):
        return pl.pallas_call(
            kernel,
            in_specs=in_specs,
            out_specs=[o[0] for o in outs],
            out_shape=[o[1] for o in outs],
            scratch_shapes=scratch,
            compiler_params=params(mib),
            cost_estimate=cost(us),
        )(*args)

    def vm(dims, kind):
        return (VM, shape(dims, kind))

    def anys(shapes):
        return [(ANY, x) for x in shapes]

    smalls = (gain_attn, gain_ffn, mask_embed, rel_table, layout_table)
    lengths = tuple(p.shape[0] for p in smalls)
    small = jnp.stack([jnp.pad(p, (0, width - p.shape[0])) for p in smalls])
    small = jnp.pad(small, ((0, 16 - len(smalls)), (0, 0)))
    bounds = [0, PARTS[0], ff]
    half = width // 2
    down_shapes = [(w_down.shape[0], half)] * 2 if fine else [w_down.shape]
    attn_low, first_low, second_low, *down_low = pl.pallas_call(
        lambda where_ref, *refs: pack_kernel(where_ref, wide, lengths, *refs),
        in_specs=[SM] + [VM] * 8,
        out_shape=[
            shape(dims, bf16)
            for dims in [(4 * rows + 16, width), (2 * rows, PARTS[0]), (2 * rows, PARTS[1])] + down_shapes
        ],
        compiler_params=params(),
        cost_estimate=cost(0),
    )(where, w_query, w_key, w_value, w_out, w_gate, w_up, w_down, small)
    attn_column = Columns(narrow, attn_low)
    attn = gather(wide)
    gu_columns = [Columns(narrow, first_low), Columns(narrow, second_low)]
    gu = [gather(wide, 4, 2), gather(wide, direct=True)]
    if fine:
        mine, other = down_low
        other = flip_wide(other, 1, wide)
        down_low = jnp.where(
            core == 0, jnp.concatenate([mine, other]), jnp.concatenate([other, mine])
        )
    else:
        down_low = down_low[0]
    down_column = Columns(narrow, down_low)
    down = gather(wide, 4, 2)

    hidden_column = hidden_patch.astype(f32)[:, None]
    attn_column.start(steps)
    steps.leave(attn_low)
    hidden_row = steps.enter(hidden_patch[None])
    pick, rel_index, lay_index = pl.pallas_call(
        prepare_kernel,
        out_shape=(
            shape((keys, count), bf16), shape((keys, count), jnp.int32), shape((keys, count), jnp.int32),
        ),
        compiler_params=params(),
        cost_estimate=cost(0),
    )(hidden_row, segment_ids[None], rel_ids, layout_ids)
    steps.leave(pick)

    column = attn_column.finish(steps)[0]
    attn.plane(steps, column)
    down_column.start(steps)
    down_stack = down_column.finish(steps)[0]
    gu_columns[0].start(steps)
    attn.forward(steps)
    down.plane(steps, down_stack)
    gu_stack = gu_columns[0].finish(steps)[0]
    gu_columns[1].start(steps)
    attn.arrive(steps)
    gu[0].plane(steps, gu_stack)
    attn_pieces = attn.finish(steps)

    groups = keys // 8
    whole = pl.BlockSpec((keys, count), lambda p: (0, 0))

    def bias_half(part, table, *given):
        low = part * (PAIRS // 2)
        out = pl.pallas_call(
            functools.partial(bias_kernel, low),
            grid=(PAIRS // 2,),
            in_specs=[pl.BlockSpec((H, 128), lambda p: (0, 0)), whole, whole] + [ANY] * len(given),
            out_specs=pl.BlockSpec((1, groups, 16, count), lambda p: (p + low, 0, 0, 0)),
            out_shape=shape((PAIRS, groups, 16, count), f32),
            input_output_aliases={3: 0} if given else {},
            compiler_params=params(),
            cost_estimate=cost(0),
        )(table, rel_index, lay_index, *given)
        steps.leave(out)
        return out

    if fine:
        attn_sources, attn_places = sources_of(attn_pieces, rows)
        start_sources = attn_sources
        small_dims = (wide, narrow, 16, width)
    else:
        attn_sources, attn_places = sources_of([(p[0][:, : 4 * rows],) + p[1:] for p in attn_pieces], rows)
        found = sum(p[0][:, 4 * rows :].astype(f32).sum(0) for p in attn_pieces)
        start_sources = attn_sources + [found.astype(bf16)[None]]
        small_dims = (1, 1, 16, width)
    place = steps.enter(where)
    attn_input, query, key, value, vectors, table = call(
        functools.partial(project_kernel, narrow, wide, attn_places),
        [SM] + [VM] * 3 + [ANY] * len(start_sources),
        [
            vm((count, width), bf16), vm((count, width), bf16), vm((keys, width), bf16),
            vm((keys, width), bf16), vm((8, width), f32), vm((H, 128), f32),
        ],
        [
            pltpu.VMEM((3, width, width), bf16), pltpu.VMEM(small_dims, bf16),
            pltpu.SemaphoreType.DMA((4,)),
        ],
        0, place, tokens, hidden_column, pick, *start_sources,
    )
    steps.leave(query)
    gu_stack = gu_columns[1].finish(steps)[0]
    bias = bias_half(0, steps.enter(table))
    down.forward(steps)
    bias = bias_half(1, steps.enter(table), bias)

    row_block = pl.BlockSpec((count, 128), lambda p: (0, p))
    key_block = pl.BlockSpec((keys, 128), lambda p: (0, p))
    turn_block = pl.BlockSpec((128, count), lambda p: (p, 0))
    score_block = pl.BlockSpec((1, groups, 16, count), lambda p: (p, 0, 0, 0))
    query_here = steps.enter(query)
    attended, probs = pl.pallas_call(
        attend_kernel,
        grid=(PAIRS,),
        in_specs=[row_block, key_block, key_block, score_block],
        out_specs=[turn_block, score_block],
        out_shape=(shape((width, count), bf16), shape((PAIRS, groups, 16, count), bf16)),
        compiler_params=params(),
        cost_estimate=cost(0),
    )(query_here, key, value, bias)
    steps.leave(attended)
    gu[0].forward(steps)
    down.arrive(steps)
    gu[1].plane(steps, gu_stack)
    place = steps.enter(where)
    residual, ffn_input = call(
        functools.partial(residual_kernel, narrow, wide, attn_places),
        [SM] + [VM] * 4 + [ANY] * len(attn_sources),
        [vm((count, width), f32), vm((count, width), bf16)],
        [pltpu.VMEM((width, width), bf16), pltpu.SemaphoreType.DMA],
        0, place, attended, tokens, hidden_column, vectors, *attn_sources,
    )
    steps.leave(residual)
    down_sources, down_places = sources_of(down.finish(steps), w_down.shape[0])
    gu[0].arrive(steps)

    acc, active, gu_sums = None, [], []
    for part, size in enumerate(PARTS):
        if part > 0:
            gu[part].forward(steps)
            gu[part].arrive(steps)
        sources, places = sources_of(gu[part].finish(steps), rows)
        shapes = block_shapes(2, rows, size)
        place = steps.enter(where)
        extra = () if part == 0 else (acc,)
        results = call(
            functools.partial(
                ffn_kernel, narrow, wide, bounds[part],
                (len(sources), len(down_sources), len(shapes)), places, down_places,
            ),
            [SM, VM, VM] + [ANY] * (len(sources) + len(down_sources)) + [VM] * len(extra),
            anys(shapes) + [vm((count, size), bf16), vm((count, width), f32)],
            [
                pltpu.VMEM((2, width, size), bf16), pltpu.VMEM((ff, width), bf16),
                pltpu.VMEM((2, width, size), bf16), pltpu.VMEM((width, count), bf16),
                pltpu.SemaphoreType.DMA((3,)),
            ],
            0 if part == 0 else 100, place, ffn_input, cotangent, *sources, *down_sources, *extra, mib=60,
        )
        act, acc = results[-2:]
        active.append(act)
        steps.leave(acc)
        turn = (2, 4) if part == 0 else (4, 2)
        gu_sums.append(scatter(narrow, wide, *blocks_of(results[:-2], 2), *turn))

    gu_sums[0].plane(steps)
    gu_sums[1].plane(steps)

    shapes = block_shapes(1, rows, width)
    if fine:
        down_grad_shapes = [shape((wide // 2, narrow, 2 * w_down.shape[0], half), bf16)] * 2
    else:
        down_grad_shapes = [shape((1, ff, width), bf16)]
    place = steps.enter(where)
    residual_grad, head, ffn_gain_part, output, *grads = call(
        functools.partial(
            turn_kernel, narrow, wide, attn_places, down_places, (len(attn_sources), len(down_sources))
        ),
        [SM] + [VM] * (5 + len(PARTS)) + [ANY] * (len(attn_sources) + len(down_sources)),
        [
            vm((count, width), f32), vm((width, count), bf16), vm((1, width), f32),
            vm((count, width), bf16),
        ] + anys(shapes + down_grad_shapes),
        [
            pltpu.VMEM((width, width), bf16), pltpu.VMEM((width, width), bf16),
            pltpu.VMEM((ff, width), bf16), pltpu.VMEM((ff, width), bf16),
            pltpu.SemaphoreType.DMA((4,)),
        ],
        100, place, residual, acc, cotangent, attended, vectors, *active, *attn_sources, *down_sources,
        mib=60,
    )
    steps.leave(head)
    out_grads, down_grads = grads[: len(shapes)], grads[len(shapes) :]
    out_sum = scatter(narrow, wide, *blocks_of(out_grads, 1), 4, 2)
    down_sum = scatter(narrow, wide, *blocks_of(down_grads, 1))
    gu_sums[1].forward(steps)
    gu_sums[0].forward(steps)

    query_here = steps.enter(query)
    query_grad, key_grad, value_grad, score_grads = pl.pallas_call(
        attend_back_kernel,
        grid=(PAIRS,),
        in_specs=[row_block, key_block, key_block, turn_block, score_block],
        out_specs=[row_block, key_block, key_block, score_block],
        out_shape=(
            shape((count, width), bf16), shape((keys, width), bf16), shape((keys, width), bf16),
            shape((PAIRS, groups, 16, count), bf16),
        ),
        compiler_params=params(),
        cost_estimate=cost(100),
    )(query_here, key, value, head, probs)
    steps.leave(query_grad)
    out_sum.plane(steps)
    down_sum.plane(steps)

    shapes = block_shapes(3, rows, width)
    place = steps.enter(where)
    key_wide, value_wide, *qkv_grads = call(
        functools.partial(project_grads_kernel, narrow, wide),
        [SM] + [VM] * 5,
        [vm((count, width), bf16), vm((count, width), bf16)] + anys(shapes),
        [
            pltpu.VMEM((3, width, width), bf16), pltpu.VMEM((width, count), bf16),
            pltpu.SemaphoreType.DMA((3,)),
        ],
        100, place, attn_input, pick, query_grad, key_grad, value_grad,
    )
    steps.leave(key_wide)
    qkv_sum = scatter(narrow, wide, *blocks_of(qkv_grads, 3))
    gu_totals = [part.column(steps) for part in reversed(gu_sums)][::-1]
    gu_rows = Rows(narrow, jnp.concatenate(gu_totals, axis=2))
    out_sum.forward(steps)

    place = steps.enter(where)
    tokens_grad, attn_gain_part, embed_part = call(
        functools.partial(project_back_kernel, narrow, wide, attn_places, len(attn_sources)),
        [SM] + [VM] * 7 + [ANY] * len(attn_sources),
        [vm((count, width), f32), vm((1, width), f32), vm((1, width), f32)],
        [pltpu.VMEM((3, width, width), bf16), pltpu.SemaphoreType.DMA((3,))],
        100, place, query_grad, key_wide, value_wide, tokens, hidden_column, vectors, residual_grad,
        *attn_sources,
    )
    steps.leave(tokens_grad)
    qkv_sum.plane(steps)
    down_sum.forward(steps, True)

    scores_here = steps.enter(score_grads)
    table_grads = pl.pallas_call(
        table_kernel,
        out_shape=shape((NB, 128), f32),
        scratch_shapes=[pltpu.VMEM((NB * 8, H * 8), f32)],
        compiler_params=params(),
        cost_estimate=cost(100),
    )(scores_here, rel_index, lay_index)
    steps.leave(table_grads)
    qkv_sum.forward(steps)
    down_rows = Rows(narrow, down_sum.column(steps))
    out_rows = Rows(narrow, out_sum.column(steps))
    table_grads = table_grads[:, :H]
    parts = (attn_gain_part, ffn_gain_part, embed_part, table_grads[:NB_REL], table_grads[NB_REL:])
    parts = jnp.concatenate([v.reshape(devices, -1) for v in parts], axis=1).astype(bf16)
    small_sum = scatter(narrow, wide, *sides(parts[:, None]), 4, 2)
    gu_total = gu_rows.finish(steps)
    small_sum.plane(steps)
    small_sum.forward(steps)
    qkv_rows = Rows(narrow, qkv_sum.column(steps))
    down_total = down_rows.finish(steps)
    out_total = out_rows.finish(steps)
    small_rows = Rows(narrow, small_sum.column(steps))
    qkv_total = qkv_rows.finish(steps)
    small_total = small_rows.finish(steps)[0]
    if fine:
        rows_here = w_down.shape[0]
        mine = lax.dynamic_slice_in_dim(down_total, core * rows_here, rows_here, 0)
        other = lax.dynamic_slice_in_dim(down_total, (1 - core) * rows_here, rows_here, 0)
        other = flip_wide(other, 1, wide)
        down_total = jnp.where(
            core == 0, jnp.concatenate([mine, other], 1), jnp.concatenate([other, mine], 1)
        )
    small_out, at = [], 0
    for p in smalls:
        small_out.append(small_total[at : at + p.shape[0]])
        at += p.shape[0]
    return (
        output, tokens_grad, qkv_total[:rows], qkv_total[rows : 2 * rows], qkv_total[2 * rows :],
        out_total, gu_total[:rows], gu_total[rows:], down_total, *small_out,
    )


def solution(mesh):
    both = P(("narrow", "wide"))
    table = P(("narrow", "wide"), None)
    return jax.shard_map(
        local,
        mesh=mesh,
        in_specs=(table, both, both) + (table,) * 9 + (both,) * 5 + (table,),
        out_specs=(table,) * 9 + (both,) * 5,
        check_vma=False,
    )
```

```python
import functools
import math

import jax
import jax.numpy as jnp
import numpy as np
from jax import lax
from jax.experimental import pallas as pl
from jax.experimental.pallas import tpu as pltpu
from jax.sharding import PartitionSpec as P

H = 16
HD = 64
PAIRS = H // 2
NB_REL = 32
NB_LAY = 64
NB = NB_REL + NB_LAY
HIDE = 192
PARTS = (2048, 768)
FF_STEP = 1024

eps_norm = 1e-06
neg_large = -1e30
f32 = jnp.float32
bf16 = jnp.bfloat16

NN = (((1,), (0,)), ((), ()))
NT = (((1,), (1,)), ((), ()))
TN = (((0,), (0,)), ((), ()))


def dot(a, b, dims=NN):
    return lax.dot_general(a, b, dims, preferred_element_type=f32)


def params(mib=56):
    return pltpu.CompilerParams(vmem_limit_bytes=mib * 1024 * 1024)


def cost(us):
    return pl.CostEstimate(flops=int(us * 1.5e9), bytes_accessed=0, transcendentals=0)


VM = pl.BlockSpec(memory_space=pltpu.VMEM)
SM = pl.BlockSpec(memory_space=pltpu.SMEM)
ANY = pl.BlockSpec(memory_space=pl.ANY)


def flip_narrow(x, bits, count):
    return lax.ppermute(x, "narrow", [(i, i ^ bits) for i in range(count)])


def narrow_order(count):
    order, bit = [0], count // 2
    while bit:
        order += [at ^ bit for at in order]
        bit //= 2
    return order


def flip_wide(x, bits, count):
    return lax.ppermute(x, "wide", [(i, i ^ bits) for i in range(count)])


class Steps:
    def __init__(self):
        self.last = ()

    def enter(self, *values):
        out = lax.optimization_barrier(tuple(values) + self.last)
        return out[: len(values)] if len(values) > 1 else out[0]

    def leave(self, *values):
        self.last = tuple(values)


class Columns:
    def __init__(self, narrow, x):
        self.narrow, self.stack, self.bit = narrow, x[None], narrow // 2

    def start(self, steps):
        stack = steps.enter(self.stack)
        self.stack, self.sent = stack, flip_narrow(stack, self.bit, self.narrow)

    def middle(self, steps):
        sent = steps.enter(self.sent)
        self.stack = jnp.concatenate([self.stack, sent])
        steps.leave(self.stack)
        self.bit //= 2
        if self.bit:
            self.sent = flip_narrow(self.stack, self.bit, self.narrow)

    def finish(self, steps):
        while self.bit:
            self.middle(steps)
        return self.stack

    def halves(self, steps):
        while self.bit > 1:
            self.middle(steps)
        sent = steps.enter(self.sent)
        steps.leave(sent)
        return self.stack, sent


class Gather:
    def __init__(self, wide, first=2, second=4, direct=False, split=False, halves=False):
        self.wide, self.bits, self.direct = wide, (first, second), direct
        self.split, self.halves = split, halves

    def add(self, array, chip, split=False):
        self.pieces.append((array, 0, chip, 0))
        half = array.shape[0] // 2
        for low in (0, half) if split else (0,):
            part = array[low : low + half] if split else array
            self.crossed.append((flip_wide(part, 1, self.wide), 1, chip, low))

    def plane(self, steps, column):
        column = steps.enter(column)
        steps.leave(column)
        self.near = [flip_wide(column, bit, self.wide) for bit in self.bits]
        if self.direct:
            self.far = [flip_wide(column, 6, self.wide)]
        self.pieces, self.crossed = [], []
        self.add(column, 0)

    def settle(self, steps, at):
        self.near[at] = steps.enter(self.near[at])
        steps.leave(self.near[at])

    def forward(self, steps):
        near, other = steps.enter(*self.near)
        steps.leave(near)
        if not self.direct:
            half = near.shape[0] // 2
            parts = [near[:half], near[half:]] if self.halves else [near]
            self.far = [flip_wide(part, self.bits[1], self.wide) for part in parts]
        self.add(near, self.bits[0] // 2)
        self.add(other, self.bits[1] // 2)

    def cross(self, steps):
        arrays = steps.enter(*[p[0] for p in self.crossed])
        steps.leave(arrays[-1])
        self.crossed = [(a,) + p[1:] for a, p in zip(arrays, self.crossed)]

    def arrive(self, steps):
        if self.halves:
            low = 0
            for far in steps.enter(*self.far):
                steps.leave(far)
                self.pieces.append((far, 0, 3, low))
                self.crossed.append((flip_wide(far, 1, self.wide), 1, 3, low))
                low += far.shape[0]
        else:
            far = steps.enter(self.far[0])
            steps.leave(far)
            self.add(far, 3, self.split)

    def finish(self, steps):
        arrays = steps.enter(*[p[0] for p in self.crossed])
        steps.leave(arrays[-1])
        return self.pieces + [(a,) + p[1:] for a, p in zip(arrays, self.crossed)]


class PlaneFirst:
    def __init__(self, narrow, wide, x):
        self.narrow, self.wide, self.x = narrow, wide, x

    def start(self, steps):
        x = steps.enter(self.x)
        self.x = x
        self.near = [flip_wide(x, bit, self.wide) for bit in (2, 4)]

    def forward(self, steps):
        self.near = steps.enter(*self.near)
        steps.leave(self.near[0])
        self.far = flip_wide(self.near[0], 4, self.wide)

    def arrive(self, steps):
        far = steps.enter(self.far)
        blocks = [self.x, *self.near, far]
        self.columns = [Columns(self.narrow, jnp.stack(blocks))]
        steps.leave(*[c.stack for c in self.columns])

    def columns_start(self, steps):
        for column in self.columns:
            column.start(steps)

    def columns_middle(self, steps):
        for column in self.columns:
            column.middle(steps)

    def cores(self, steps):
        halves = [column.halves(steps) for column in self.columns]
        self.pieces = [
            (part, 0, 2 * n, low) for n, pair in enumerate(halves)
            for part, low in zip(pair, (0, self.narrow // 2))
        ]
        self.crossed = [flip_wide(p[0], 1, self.wide) for p in self.pieces]

    def finish(self, steps):
        crossed = steps.enter(*self.crossed)
        steps.leave(*crossed)
        return self.pieces + [(a, 1) + p[2:] for a, p in zip(crossed, self.pieces)]


class SmallGather:
    def __init__(self, narrow, wide, x):
        self.narrow, self.wide, self.stack, self.bits = narrow, wide, x[None], []
        bit = 1
        while bit < narrow:
            self.bits.append((flip_narrow, bit, narrow))
            bit *= 2
        bit = 2
        while bit < wide:
            self.bits.append((flip_wide, bit, wide))
            bit *= 2

    def start(self, steps):
        self.stack = steps.enter(self.stack)
        self.send()

    def send(self):
        if self.bits:
            flip, bit, count = self.bits.pop(0)
            self.sent = flip(self.stack, bit, count)
        else:
            self.sent = None

    def middle(self, steps):
        self.stack = jnp.concatenate([self.stack, steps.enter(self.sent)])
        steps.leave(self.stack)
        self.send()
        if self.sent is None:
            self.crossed = flip_wide(self.stack, 1, self.wide)

    def finish(self, steps):
        while self.sent is not None:
            self.middle(steps)
        crossed = steps.enter(self.crossed)
        steps.leave(crossed)
        return [self.stack, crossed]


class PlainGather(Gather):
    def plane(self, steps, column):
        column = steps.enter(column)
        steps.leave(column)
        found = {0: column}
        bit = 2
        while bit < self.wide:
            for at in list(found):
                found[at ^ bit] = flip_wide(found[at], bit, self.wide)
            bit *= 2
        self.pieces, self.crossed = [], []
        for at, array in found.items():
            self.add(array, at // 2)

    def settle(self, steps, at):
        pass

    def cross(self, steps):
        pass

    def forward(self, steps):
        pass

    def arrive(self, steps):
        pass


def ordered(pieces, narrow, wide):
    table = [None] * wide
    for array, core, chip, _ in pieces:
        table[2 * chip + core] = array
    order = jnp.arange(wide) ^ lax.axis_index("wide")
    place = np.argsort(narrow_order(narrow))
    shift = jnp.asarray(place)[jnp.arange(narrow) ^ lax.axis_index("narrow")]
    full = jnp.stack(table, axis=1)[shift[:, None], order[None]]
    return full.reshape((narrow * wide,) + full.shape[2:])


class Scatter:
    def __init__(self, narrow, wide, keep, send, first=2, second=4, joined=False):
        self.narrow, self.wide, self.keep, self.bits = narrow, wide, keep, (first, second)
        self.joined = joined
        self.sent = flip_wide(send, 1, wide)

    def plane(self, steps):
        self.sent = steps.enter(self.sent)
        second = self.bits[1]
        mine = [self.chip(n).astype(bf16) for n in (3, second // 2)]
        if self.joined:
            mine = [jnp.stack(mine)]
        steps.leave(*mine)
        self.away = [flip_wide(part, second, self.wide) for part in mine]

    def chip(self, n):
        return self.keep[n].astype(f32) + self.sent[n].astype(f32)

    def settle(self, steps):
        self.away[1] = steps.enter(self.away[1])
        steps.leave(self.away[1])

    def forward(self, steps):
        if self.joined:
            self.away = list(steps.enter(self.away[0]))
        else:
            self.away[0] = steps.enter(self.away[0])
        first = self.bits[0]
        both = (self.chip(first // 2) + self.away[0].astype(f32)).astype(bf16)
        steps.leave(both)
        self.near = flip_wide(both, first, self.wide)

    def column(self, steps):
        if self.joined:
            near, straight = steps.enter(self.near), self.away[1]
        else:
            near, straight = steps.enter(self.near, self.away[1])
        total = self.chip(0) + straight.astype(f32) + near.astype(f32)
        total = total.astype(bf16)
        steps.leave(total)
        return total


class DirectScatter(Scatter):
    def plane(self, steps):
        sent = steps.enter(self.sent)
        mine = (self.keep.astype(f32) + sent.astype(f32)).astype(bf16)
        steps.leave(mine)
        self.mine = mine
        self.other = [flip_wide(mine[n], 2 * n, self.wide) for n in range(1, self.wide // 2)]

    def column(self, steps):
        other = steps.enter(*self.other)
        total = self.mine[0].astype(f32)
        for part in other:
            total = total + part.astype(f32)
        total = total.astype(bf16)
        steps.leave(total)
        return total


class Rows:
    def __init__(self, steps, narrow, mine):
        self.narrow, self.bit = narrow, 1
        z = lax.axis_index("narrow")
        self.mine = [lax.dynamic_index_in_dim(mine, z ^ n, 0, False) for n in range(narrow)]
        self.send()

    def send(self):
        away = jnp.stack([part for n, part in enumerate(self.mine) if n & 1])
        self.mine = [part for n, part in enumerate(self.mine) if not n & 1]
        self.sent = flip_narrow(away, self.bit, self.narrow)

    def middle(self, steps):
        sent = steps.enter(self.sent)
        self.mine = [part.astype(f32) + sent[n].astype(f32) for n, part in enumerate(self.mine)]
        self.bit *= 2
        if self.bit < self.narrow:
            self.mine = [part.astype(bf16) for part in self.mine]
            steps.leave(*self.mine)
            self.send()
        else:
            steps.leave(self.mine[0])

    def finish(self, steps):
        while self.bit < self.narrow:
            self.middle(steps)
        return self.mine[0]


class PlainScatter(Scatter):
    def plane(self, steps):
        sent = steps.enter(self.sent)
        mine = self.keep.astype(f32) + sent.astype(f32)
        bit = self.wide // 2
        while bit > 1:
            half = mine.shape[0] // 2
            low = mine.astype(bf16)
            mine = low[:half].astype(f32) + flip_wide(low[half:], bit, self.wide).astype(f32)
            bit //= 2
        self.total = mine[0].astype(bf16)

    def settle(self, steps):
        pass

    def forward(self, steps):
        pass

    def column(self, steps):
        return self.total


def piece_arrays(pieces):
    return [p[0] for p in pieces]


def piece_places(pieces):
    return [p[1:] for p in pieces]


def load_rows(where, sources, places, index, rows, dst, sem, narrow, wide):
    if places is None:
        pltpu.make_async_copy(sources[0].at[index], dst, sem).start()
        return
    for src, (core, chip, low) in zip(sources, places):
        w = jnp.bitwise_xor(where[1], 2 * chip + core)
        for n, flip in enumerate(narrow_order(narrow)[low : low + src.shape[0]]):
            z = jnp.bitwise_xor(where[0], flip)
            row = pl.multiple_of((z * wide + w) * rows, rows)
            pltpu.make_async_copy(
                src.at[n, pl.ds(index * rows, rows)], dst.at[pl.ds(row, rows), :], sem
            ).start()


def load_pairs(where, sources, places, dst, sem, narrow, wide):
    if places is None:
        pltpu.make_async_copy(sources[0].at[0], dst, sem).start()
        return
    for src, (core, chip, low) in zip(sources, places):
        rows, lanes = src.shape[2:]
        lane = pl.multiple_of(jnp.bitwise_xor(jnp.bitwise_and(where[1], 1), core) * lanes, lanes)
        for n, flip in enumerate(narrow_order(narrow)[low : low + src.shape[0]]):
            z = jnp.bitwise_xor(where[0], flip)
            for flip in range(src.shape[1]):
                c = jnp.bitwise_xor(lax.shift_right_logical(where[1], 1), chip + flip)
                row = pl.multiple_of((z * (wide // 2) + c) * rows, rows)
                pltpu.make_async_copy(
                    src.at[n, flip], dst.at[pl.ds(row, rows), pl.ds(lane, lanes)], sem
                ).start()


def wait_all(ref, sem):
    pltpu.make_async_copy(ref, ref, sem).wait()


def store_rows(where, src, out, index, rows, sem, narrow, wide):
    if len(out) == 1:
        pltpu.make_async_copy(src, out[0].at[index], sem).start()
        return
    core = jnp.bitwise_and(where[1], 1)
    chip = lax.shift_right_logical(where[1], 1)
    for z in range(narrow):
        for c in range(wide // 2):
            flip = jnp.bitwise_xor(chip, c)
            for dst, side in zip(out, (core, 1 - core)):
                row = pl.multiple_of((z * wide + 2 * c + side) * rows, rows)
                pltpu.make_async_copy(
                    src.at[pl.ds(row, rows), :], dst.at[flip, z, pl.ds(index * rows, rows)], sem
                ).start()


def store_pairs(where, src, out, sem, narrow, wide):
    if len(out) == 1:
        pltpu.make_async_copy(src, out[0].at[0], sem).start()
        return
    core = jnp.bitwise_and(where[1], 1)
    chip = lax.shift_right_logical(where[1], 1)
    rows, lanes = out[0].shape[2:]
    for z in range(narrow):
        for c in range(wide // 2):
            flip = jnp.bitwise_xor(chip, c)
            for dst, side in zip(out, (core, 1 - core)):
                lane = pl.multiple_of(side * lanes, lanes)
                pltpu.make_async_copy(
                    src.at[pl.ds((z * (wide // 2) + c) * rows, rows), pl.ds(lane, lanes)],
                    dst.at[flip, z],
                    sem,
                ).start()


def prepare_kernel(hidden_ref, segment_ref, rel_ref, lay_ref, pick_ref, rel_out, lay_out):
    count = hidden_ref.shape[1]
    keys = pick_ref.shape[0]
    seen = hidden_ref[...] == 0
    before = lax.broadcasted_iota(jnp.int32, (count, count), 0)
    after = lax.broadcasted_iota(jnp.int32, (count, count), 1)
    upper = jnp.where(before <= after, 1.0, 0.0).astype(bf16)
    seen_rows = jnp.broadcast_to(jnp.where(seen, 1.0, 0.0), (16, count)).astype(bf16)
    rank = dot(seen_rows, upper)[0:1].astype(jnp.int32) - 1
    rank = jnp.where(seen, rank, -1)
    number = lax.broadcasted_iota(jnp.int32, (keys, count), 0)
    pick = jnp.where(number == rank, 1.0, 0.0).astype(bf16)
    pick_ref[...] = pick
    segment = jnp.broadcast_to(segment_ref[...].astype(f32), (16, count)).astype(bf16)
    key_segment = dot(pick, segment, NT)[:, 0:1]
    valid = key_segment == segment_ref[...].astype(f32)
    rel = dot(pick, rel_ref[...].astype(f32).astype(bf16), NT).astype(jnp.int32)
    lay = dot(pick, lay_ref[...].astype(f32).astype(bf16), NT).astype(jnp.int32)
    rel_out[...] = jnp.where(valid, rel, NB)
    lay_out[...] = lay + NB_REL


def bias_kernel(low, table_ref, rel_ref, lay_ref, *refs):
    out_ref = refs[-1]
    keys, count = rel_ref.shape
    groups = keys // 8
    pair = pl.program_id(0) + low
    tables = [
        jnp.broadcast_to(table_ref[pl.ds(2 * pair + side, 1), :], (keys, 128)) for side in range(2)
    ]
    for c in range(count // 128):
        lanes = slice(c * 128, c * 128 + 128)
        for side in range(2):
            found = jnp.take_along_axis(tables[side], rel_ref[:, lanes], axis=1)
            found = found + jnp.take_along_axis(tables[side], lay_ref[:, lanes], axis=1)
            out_ref[0, :, side * 8 : side * 8 + 8, lanes] = found.reshape(groups, 8, 128)


def embed(tokens_ref, hidden_ref, vectors_ref):
    return jnp.where(hidden_ref[...] == 1.0, vectors_ref[2:3, :], tokens_ref[...].astype(f32))


def inverse_rms(v):
    return lax.rsqrt(jnp.mean(v * v, axis=-1, keepdims=True) + eps_norm)


def pack_kernel(where, wide, lengths, *refs):
    query, key, value, out, gate, up, down, smalls = refs[:8]
    attn_ref, small_ref, first_ref, second_ref = refs[8:12]
    rows = query.shape[0]
    for n, ref in enumerate((query, key, value, out)):
        attn_ref[n * rows : (n + 1) * rows, :] = ref[...].astype(bf16)
    own = where[0] * wide + where[1]
    dims = (8, smalls.shape[1])
    row = lax.broadcasted_iota(jnp.int32, dims, 0)
    lane = lax.broadcasted_iota(jnp.int32, dims, 1)
    spread = jnp.broadcast_to(smalls[...], dims)
    placed = jnp.zeros(dims, f32)
    at = 0
    for n, length in enumerate(lengths):
        part = jnp.where((row == n) & (lane >= at) & (lane < at + length), spread, 0.0)
        placed = placed + pltpu.roll(part, own * length + (dims[1] - at), 1)
        at += length
    small_ref[...] = placed.astype(bf16)
    size = first_ref.shape[1]
    for n, ref in enumerate((gate, up)):
        first_ref[n * rows : (n + 1) * rows, :] = ref[:, 0:size].astype(bf16)
        second_ref[n * rows : (n + 1) * rows, :] = ref[:, size:].astype(bf16)
    if len(refs) == 13:
        refs[12][...] = down[...].astype(bf16)
    else:
        half = down.shape[1] // 2
        core = jnp.bitwise_and(where[1], 1)
        for n, side in enumerate((core, 1 - core)):
            lanes = pl.ds(pl.multiple_of(side * half, half), half)
            refs[12 + n][...] = down[:, lanes].astype(bf16)


def unpack_kernel(left_ref, right_ref, vectors_ref, table_ref):
    width = vectors_ref.shape[1]
    vectors = jnp.sum(left_ref[...].astype(f32), axis=0) + jnp.sum(right_ref[...].astype(f32), axis=0)
    vectors_ref[...] = vectors
    lane = lax.broadcasted_iota(jnp.int32, (H, width), 1)
    head = lax.broadcasted_iota(jnp.int32, (H, width), 0)
    entry = lax.broadcasted_iota(jnp.int32, (width, 128), 0) // H
    bucket = lax.broadcasted_iota(jnp.int32, (width, 128), 1)
    end = lax.broadcasted_iota(jnp.int32, (H, 128), 1)
    table = jnp.where(end >= NB, neg_large, 0.0)
    for n, first in ((3, 0), (4, NB_REL)):
        split = jnp.where(lane % H == head, vectors[n : n + 1], 0.0).astype(bf16)
        spot = jnp.where(entry + first == bucket, 1.0, 0.0).astype(bf16)
        table = table + dot(split, spot)
    table_ref[...] = table


def project_kernel(narrow, wide, places, where, tokens_ref, hidden_ref, pick_ref, vectors_ref, *refs):
    sources = refs[:-6]
    input_ref, query_ref, key_ref, value_ref, weights, sems = refs[-6:]
    width = tokens_ref.shape[1]
    rows = width // (narrow * wide)
    for n in range(3):
        load_rows(where, sources, places, n, rows, weights.at[n], sems.at[n], narrow, wide)
    embedded = embed(tokens_ref, hidden_ref, vectors_ref)
    attn_input = (embedded * inverse_rms(embedded) * vectors_ref[0:1, :]).astype(bf16)
    input_ref[...] = attn_input
    seen = dot(pick_ref[...], attn_input).astype(bf16)
    wait_all(weights.at[0], sems.at[0])
    query_ref[...] = dot(attn_input, weights[0]).astype(bf16)
    wait_all(weights.at[1], sems.at[1])
    key_ref[...] = dot(seen, weights[1]).astype(bf16)
    wait_all(weights.at[2], sems.at[2])
    value_ref[...] = dot(seen, weights[2]).astype(bf16)


def by_side(x):
    keys = x.shape[0]
    wide = x.astype(f32).reshape(keys // 8, 8, 128)
    left = lax.broadcasted_iota(jnp.int32, wide.shape, 2) < HD
    both = jnp.concatenate([jnp.where(left, wide, 0.0), jnp.where(left, 0.0, wide)], axis=1)
    return both.astype(bf16).reshape(keys * 2, 128)


def own_side(x):
    x = x.reshape(x.shape[0] // 16, 16, 128)
    left = lax.broadcasted_iota(jnp.int32, (x.shape[0], 8, 128), 2) < HD
    return jnp.where(left, x[:, 0:8], x[:, 8:16]).reshape(x.shape[0] * 8, 128)


def per_side(x, fold, spread):
    return jnp.concatenate(
        [
            jnp.broadcast_to(fold(x[side * 8 : side * 8 + 8], axis=0, keepdims=True), (8, spread))
            for side in range(2)
        ],
        axis=0,
    )[None]


def attend_kernel(query_ref, key_ref, value_ref, bias_ref, attended_ref, probs_ref):
    count = query_ref.shape[0]
    keys = key_ref.shape[0]
    scores = dot(by_side(key_ref[...]), query_ref[...], NT).reshape(keys // 8, 16, count)
    scores = scores + bias_ref[0]
    top = per_side(jnp.max(scores, axis=0), jnp.max, count)
    exponent = jnp.exp(scores - top)
    total = per_side(jnp.sum(exponent, axis=0), jnp.sum, count)
    probs = (exponent * (1.0 / total)).astype(bf16)
    probs_ref[0] = probs
    attended = dot(by_side(value_ref[...]), probs.reshape(keys * 2, count), TN)
    attended_ref[...] = attended.astype(bf16)


def residual_kernel(
    narrow, wide, places, where, attended_ref, tokens_ref, hidden_ref, vectors_ref, *refs
):
    sources = refs[:-4]
    residual_ref, input_ref, weight, sem = refs[-4:]
    rows = weight.shape[0] // (narrow * wide)
    load_rows(where, sources, places, 3, rows, weight, sem, narrow, wide)
    embedded = embed(tokens_ref, hidden_ref, vectors_ref)
    wait_all(weight, sem)
    residual = embedded + dot(attended_ref[...], weight[...], TN)
    residual_ref[...] = residual
    input_ref[...] = (residual * inverse_rms(residual) * vectors_ref[1:2, :]).astype(bf16)


def gelu_parts(v):
    scale = math.sqrt(2.0 / math.pi)
    square = v * v
    bend = jnp.tanh(scale * v * (1.0 + 0.044715 * square))
    half = 0.5 * (1.0 + bend)
    slope = half + 0.5 * v * (1.0 - bend * bend) * (scale * (1.0 + 3 * 0.044715 * square))
    return v * half, slope


def ffn_kernel(narrow, wide, low, counts, places, down_places, where, input_ref, cot_ref, *refs):
    sources, refs = refs[: counts[0]], refs[counts[0] :]
    down_sources, refs = refs[: counts[1]], refs[counts[1] :]
    acc_in, refs = (None, refs) if low == 0 else (refs[0], refs[1:])
    out, refs = refs[: counts[2]], refs[counts[2] :]
    active_ref, acc_ref, weights, down_ref, grads, turned, sems = refs
    width = input_ref.shape[1]
    rows = width // (narrow * wide)
    size = active_ref.shape[1]
    for n in range(2):
        load_rows(where, sources, places, n, rows, weights.at[n], sems.at[n], narrow, wide)
    load_pairs(where, down_sources, down_places, down_ref, sems.at[2], narrow, wide)
    x = input_ref[...]
    turned[...] = x.T
    steps = [slice(at, min(at + FF_STEP, size)) for at in range(0, size, FF_STEP)]
    acc = None if acc_in is None else acc_in[...]
    for at, lanes in enumerate(steps):
        if at == 0:
            wait_all(weights.at[0], sems.at[0])
        gate = dot(x, weights[0, :, lanes])
        gelu, slope = gelu_parts(gate)
        if at == 0:
            wait_all(weights.at[1], sems.at[1])
        up = dot(x, weights[1, :, lanes])
        active_ref[:, lanes] = (gelu * up).astype(bf16)
        if at == 0:
            wait_all(down_ref, sems.at[2])
        act_grad = dot(cot_ref[...], down_ref[low + lanes.start : low + lanes.stop, :], NT)
        up_back = (act_grad * gelu).astype(bf16)
        gate_back = (act_grad * up * slope).astype(bf16)
        last = at == len(steps) - 1
        for n, back in ((1, up_back), (0, gate_back)):
            grads[n, :, lanes] = dot(turned[...], back).astype(bf16)
            if last:
                store_rows(where, grads.at[n], out, n, rows, sems.at[n], narrow, wide)
        for n, back in ((1, up_back), (0, gate_back)):
            term = dot(back, weights[n, :, lanes], NT)
            acc = term if acc is None else acc + term
    acc_ref[...] = acc
    for n in range(2):
        wait_all(grads.at[n], sems.at[n])


def turn_kernel(narrow, wide, places, down_places, counts, where, *refs):
    residual_ref, ffn_ref, cot_ref, attended_ref, vectors_ref = refs[:5]
    actives, refs = refs[5 : 5 + len(PARTS)], refs[5 + len(PARTS) :]
    sources, down_sources, refs = refs[: counts[0]], refs[counts[0] : counts[0] + counts[1]], refs[sum(counts) :]
    grad_ref, head_ref, gain_out, output_ref = refs[:4]
    weight, grads, down, down_grads, sems = refs[-5:]
    out, down_out = refs[4:-5][: len(refs[4:-5]) // 2], refs[4:-5][len(refs[4:-5]) // 2 :]
    rows = weight.shape[0] // (narrow * wide)
    load_rows(where, sources, places, 3, rows, weight, sems.at[0], narrow, wide)
    load_pairs(where, down_sources, down_places, down, sems.at[2], narrow, wide)
    cot = cot_ref[...]
    residual = residual_ref[...]
    inverse = inverse_rms(residual)
    normed = residual * inverse
    ffn_grad = ffn_ref[...]
    gain_out[...] = jnp.sum(ffn_grad * normed, axis=0, keepdims=True)
    scaled = ffn_grad * vectors_ref[1:2, :]
    center = jnp.mean(scaled * normed, axis=-1, keepdims=True)
    grad = cot.astype(f32) + (scaled - normed * center) * inverse
    grad_ref[...] = grad
    low = grad.astype(bf16)
    grads[...] = dot(attended_ref[...], low).astype(bf16)
    store_rows(where, grads, out, 0, rows, sems.at[1], narrow, wide)
    at = 0
    for ref in actives:
        down_grads[at : at + ref.shape[1], :] = dot(ref[...], cot, TN).astype(bf16)
        at += ref.shape[1]
    store_pairs(where, down_grads, down_out, sems.at[3], narrow, wide)
    wait_all(weight, sems.at[0])
    head_ref[...] = dot(weight[...], low, NT).astype(bf16)
    wait_all(down, sems.at[2])
    total = residual
    at = 0
    for ref in actives:
        total = total + dot(ref[...], down[at : at + ref.shape[1], :])
        at += ref.shape[1]
    output_ref[...] = total.astype(bf16)
    wait_all(grads, sems.at[1])
    wait_all(down_grads, sems.at[3])


def attend_back_kernel(
    query_ref, key_ref, value_ref, head_ref, probs_ref, query_out, key_out, value_out, scores_ref
):
    count = query_ref.shape[0]
    keys = key_ref.shape[0]
    low = probs_ref[0]
    head = head_ref[...]
    probs = low.astype(f32)
    prob_grad = dot(by_side(value_ref[...]), head).reshape(keys // 8, 16, count)
    center = per_side(jnp.sum(probs * prob_grad, axis=0), jnp.sum, count)
    score_grad = (probs * (prob_grad - center)).astype(bf16)
    scores_ref[0] = score_grad
    score_grad = score_grad.reshape(keys * 2, count)
    query_grad = dot(by_side(key_ref[...]), score_grad, TN)
    query_out[...] = query_grad.T.astype(bf16)
    key_out[...] = own_side(dot(score_grad, query_ref[...])).astype(bf16)
    value_out[...] = own_side(dot(low.reshape(keys * 2, count), head, NT)).astype(bf16)


def table_kernel(scores_ref, rel_ref, lay_ref, out_ref, total):
    keys, count = rel_ref.shape
    total[...] = jnp.zeros_like(total)

    def step(g, _):
        rows = pl.ds(pl.multiple_of(g * 8, 8), 8)
        hot = []
        for ids, low, high in ((rel_ref[rows, :], 0, NB_REL), (lay_ref[rows, :], NB_REL, NB)):
            for b in range(low, high, 2):
                pair = [jnp.where(ids == b + n, 1.0, 0.0) for n in range(2)]
                hot.append(jnp.concatenate(pair, axis=0).astype(bf16))
        hot = jnp.concatenate(hot, axis=0)
        grads = scores_ref[:, pl.ds(g, 1)].reshape(H * 8, count)
        total[...] += dot(hot, grads, NT)
        return 0

    lax.fori_loop(0, keys // 8, step, 0)
    row = lax.broadcasted_iota(jnp.int32, total.shape, 0) % 8
    lane = lax.broadcasted_iota(jnp.int32, total.shape, 1) % 8
    own = jnp.where(row == lane, total[...], 0.0)
    own = jnp.sum(own.reshape(NB, 8, H * 8), axis=1)
    fold = lax.broadcasted_iota(jnp.int32, (H * 8, 128), 0) // 8
    fold = jnp.where(fold == lax.broadcasted_iota(jnp.int32, (H * 8, 128), 1), 1.0, 0.0)
    out_ref[...] = jnp.dot(own, fold, precision=lax.Precision.HIGHEST, preferred_element_type=f32)


def spread_rows(pick_ref, ref):
    return dot(pick_ref[...], ref[...], TN).astype(bf16)


def project_grads_kernel(
    narrow, wide, where, input_ref, pick_ref, query_ref, key_ref, value_ref, key_out, value_out, *refs
):
    out, (grads, turned, sems) = refs[:-3], refs[-3:]
    rows = turned.shape[0] // (narrow * wide)
    turned[...] = input_ref[...].T
    key_out[...] = spread_rows(pick_ref, key_ref)
    value_out[...] = spread_rows(pick_ref, value_ref)
    for n, ref in enumerate((query_ref, key_out, value_out)):
        grads[n] = dot(turned[...], ref[...]).astype(bf16)
        store_rows(where, grads.at[n], out, n, rows, sems.at[n], narrow, wide)
    for n in range(3):
        wait_all(grads.at[n], sems.at[n])


def project_back_kernel(
    narrow, wide, places, count, where, query_ref, key_ref, value_ref, tokens_ref, hidden_ref,
    vectors_ref, residual_ref, *refs
):
    sources, refs = refs[:count], refs[count:]
    tokens_out, gain_out, embed_out, weights, sems = refs
    rows = weights.shape[1] // (narrow * wide)
    for n in range(3):
        load_rows(where, sources, places, n, rows, weights.at[n], sems.at[n], narrow, wide)
    embedded = embed(tokens_ref, hidden_ref, vectors_ref)
    inverse = inverse_rms(embedded)
    normed = embedded * inverse
    attn_grad = None
    for n, ref in enumerate((query_ref, key_ref, value_ref)):
        wait_all(weights.at[n], sems.at[n])
        term = dot(ref[...], weights[n], NT)
        attn_grad = term if n == 0 else attn_grad + term
    gain_out[...] = jnp.sum(attn_grad * normed, axis=0, keepdims=True)
    scaled = attn_grad * vectors_ref[0:1, :]
    center = jnp.mean(scaled * normed, axis=-1, keepdims=True)
    grad = residual_ref[...] + (scaled - normed * center) * inverse
    concealed = hidden_ref[...] == 1.0
    tokens_out[...] = jnp.where(concealed, 0.0, grad)
    embed_out[...] = jnp.sum(jnp.where(concealed, grad, 0.0), axis=0, keepdims=True)


def shape(dims, kind):
    return jax.ShapeDtypeStruct(tuple(dims), kind)


def local(
    tokens, hidden_patch, segment_ids, rel_ids, layout_ids, w_query, w_key, w_value, w_out, w_gate,
    w_up, w_down, gain_attn, gain_ffn, mask_embed, rel_table, layout_table, cotangent,
):
    narrow, wide = lax.axis_size("narrow"), lax.axis_size("wide")
    devices = narrow * wide
    count, width = tokens.shape
    keys = count - HIDE
    ff = w_gate.shape[1]
    rows = w_query.shape[0]
    where = jnp.stack([lax.axis_index("narrow"), lax.axis_index("wide")]).astype(jnp.int32)
    core = lax.axis_index("wide") % 2

    fine = narrow % 2 == 0 and wide == 8 and rows % 16 == 0 and w_down.shape[0] % 8 == 0
    gather, scatter = (Gather, Scatter) if fine else (PlainGather, PlainScatter)
    steps = Steps()

    def sources_of(pieces, low_rows):
        if fine:
            return piece_arrays(pieces), piece_places(pieces)
        full = ordered(pieces, narrow, wide)
        full = full.reshape((devices, full.shape[1] // low_rows, -1) + full.shape[2:])
        return [jnp.swapaxes(full, 0, 1).reshape(full.shape[1], -1, full.shape[-1])], None

    chip_flip, z_index = jnp.meshgrid(jnp.arange(wide // 2), jnp.arange(narrow), indexing="ij")

    def sides(parts):
        flip = (chip_flip * 2) ^ lax.axis_index("wide")
        return [parts[z_index * wide + (flip ^ side)] for side in range(2)]

    def blocks_of(grads, number):
        if fine:
            return grads
        parts = grads[0].reshape(number, devices, -1, grads[0].shape[-1])
        return sides(jnp.swapaxes(parts, 0, 1).reshape(devices, -1, parts.shape[-1]))

    def block_shapes(number, block_rows, lanes):
        if fine:
            return [shape((wide // 2, narrow, number * block_rows, lanes), bf16)] * 2
        return [shape((number, devices * block_rows, lanes), bf16)]

    def call(kernel, in_specs, outs, scratch, us, *args, mib=56):
        return pl.pallas_call(
            kernel,
            in_specs=in_specs,
            out_specs=[o[0] for o in outs],
            out_shape=[o[1] for o in outs],
            scratch_shapes=scratch,
            compiler_params=params(mib),
            cost_estimate=cost(us),
        )(*args)

    def vm(dims, kind):
        return (VM, shape(dims, kind))

    def anys(shapes):
        return [(ANY, x) for x in shapes]

    smalls = (gain_attn, gain_ffn, mask_embed, rel_table, layout_table)
    lengths = tuple(p.shape[0] for p in smalls)
    small = jnp.concatenate(smalls + (jnp.zeros(width - sum(lengths), f32),))[None]
    bounds = [0, PARTS[0], ff]
    half = width // 2
    down_shapes = [(w_down.shape[0], half)] * 2 if fine else [w_down.shape]
    attn_low, small_low, first_low, second_low, *down_low = pl.pallas_call(
        lambda where_ref, *refs: pack_kernel(where_ref, wide, lengths, *refs),
        in_specs=[SM] + [VM] * 8,
        out_shape=[
            shape(dims, bf16)
            for dims in [(4 * rows, width), (8, width), (2 * rows, PARTS[0]), (2 * rows, PARTS[1])] + down_shapes
        ],
        compiler_params=params(),
        cost_estimate=cost(0),
    )(where, w_query, w_key, w_value, w_out, w_gate, w_up, w_down, small)
    smalls_gather = SmallGather(narrow, wide, small_low)
    attn_column = Columns(narrow, attn_low)
    attn = gather(wide, split=True)
    gu_columns = [Columns(narrow, first_low), Columns(narrow, second_low)]
    gu = [gather(wide, 4, 2, halves=True), gather(wide, direct=True)]
    if fine:
        mine, other = down_low
        other = flip_wide(other, 1, wide)
        down_low = jnp.where(
            core == 0, jnp.concatenate([mine, other]), jnp.concatenate([other, mine])
        )
    else:
        down_low = down_low[0]
    down = PlaneFirst(narrow, wide, down_low) if fine else gather(wide)
    down_column = Columns(narrow, down_low)

    hidden_column = hidden_patch.astype(f32)[:, None]
    smalls_gather.start(steps)
    attn_column.start(steps)
    steps.leave(attn_low)
    hidden_row = steps.enter(hidden_patch[None])
    pick, rel_index, lay_index = pl.pallas_call(
        prepare_kernel,
        out_shape=(
            shape((keys, count), bf16), shape((keys, count), jnp.int32), shape((keys, count), jnp.int32),
        ),
        compiler_params=params(),
        cost_estimate=cost(0),
    )(hidden_row, segment_ids[None], rel_ids, layout_ids)
    steps.leave(pick)

    groups = keys // 8
    whole = pl.BlockSpec((keys, count), lambda p: (0, 0))

    def bias_half(part, table, *given):
        low = part * (PAIRS // 2)
        out = pl.pallas_call(
            functools.partial(bias_kernel, low),
            grid=(PAIRS // 2,),
            in_specs=[pl.BlockSpec((H, 128), lambda p: (0, 0)), whole, whole] + [ANY] * len(given),
            out_specs=pl.BlockSpec((1, groups, 16, count), lambda p: (p + low, 0, 0, 0)),
            out_shape=shape((PAIRS, groups, 16, count), f32),
            input_output_aliases={3: 0} if given else {},
            compiler_params=params(),
            cost_estimate=cost(0),
        )(table, rel_index, lay_index, *given)
        steps.leave(out)
        return out

    smalls_gather.middle(steps)
    if fine:
        down.start(steps)
        down.forward(steps)
    else:
        down_column.start(steps)
    smalls_gather.middle(steps)
    attn_column.middle(steps)
    if fine:
        down.arrive(steps)
    smalls_gather.middle(steps)
    attn.plane(steps, attn_column.finish(steps))
    vectors, table = pl.pallas_call(
        unpack_kernel,
        out_shape=(shape((8, width), f32), shape((H, 128), f32)),
        compiler_params=params(),
        cost_estimate=cost(0),
    )(*smalls_gather.finish(steps))
    gu_columns[0].start(steps)
    bias = bias_half(0, steps.enter(table))
    gu_columns[0].middle(steps)
    bias = bias_half(1, steps.enter(table), bias)
    gu_stack = gu_columns[0].finish(steps)
    attn.forward(steps)
    gu[0].plane(steps, gu_stack)
    if fine:
        down.columns_start(steps)
    attn.cross(steps)
    gu[0].settle(steps, 1)
    if fine:
        down.columns_middle(steps)
    attn.arrive(steps)
    attn_pieces = attn.finish(steps)
    attn_sources, attn_places = sources_of(attn_pieces, rows)
    place = steps.enter(where)
    attn_input, query, key, value = call(
        functools.partial(project_kernel, narrow, wide, attn_places),
        [SM] + [VM] * 4 + [ANY] * len(attn_sources),
        [vm((count, width), bf16), vm((count, width), bf16), vm((keys, width), bf16), vm((keys, width), bf16)],
        [pltpu.VMEM((3, width, width), bf16), pltpu.SemaphoreType.DMA((3,))],
        0, place, tokens, hidden_column, pick, vectors, *attn_sources,
    )
    steps.leave(query)
    gu[0].forward(steps)
    gu_columns[1].start(steps)

    row_block = pl.BlockSpec((count, 128), lambda p: (0, p))
    key_block = pl.BlockSpec((keys, 128), lambda p: (0, p))
    turn_block = pl.BlockSpec((128, count), lambda p: (p, 0))
    score_block = pl.BlockSpec((1, groups, 16, count), lambda p: (p, 0, 0, 0))
    query_here = steps.enter(query)
    attended, probs = pl.pallas_call(
        attend_kernel,
        grid=(PAIRS,),
        in_specs=[row_block, key_block, key_block, score_block],
        out_specs=[turn_block, score_block],
        out_shape=(shape((width, count), bf16), shape((PAIRS, groups, 16, count), bf16)),
        compiler_params=params(),
        cost_estimate=cost(0),
    )(query_here, key, value, bias)
    steps.leave(attended)
    place = steps.enter(where)
    residual, ffn_input = call(
        functools.partial(residual_kernel, narrow, wide, attn_places),
        [SM] + [VM] * 4 + [ANY] * len(attn_sources),
        [vm((count, width), f32), vm((count, width), bf16)],
        [pltpu.VMEM((width, width), bf16), pltpu.SemaphoreType.DMA],
        0, place, attended, tokens, hidden_column, vectors, *attn_sources,
    )
    steps.leave(residual)
    if fine:
        down.cores(steps)
    gu[0].arrive(steps)
    gu_columns[1].middle(steps)
    gu[1].plane(steps, gu_columns[1].finish(steps))
    if not fine:
        down.plane(steps, down_column.finish(steps))
    down_sources, down_places = sources_of(down.finish(steps), w_down.shape[0])

    acc, active, gu_sums = None, [], []
    for part, size in enumerate(PARTS):
        if part > 0:
            gu[part].forward(steps)
            gu[part].arrive(steps)
        sources, places = sources_of(gu[part].finish(steps), rows)
        shapes = block_shapes(2, rows, size)
        place = steps.enter(where)
        extra = () if part == 0 else (acc,)
        results = call(
            functools.partial(
                ffn_kernel, narrow, wide, bounds[part],
                (len(sources), len(down_sources), len(shapes)), places, down_places,
            ),
            [SM, VM, VM] + [ANY] * (len(sources) + len(down_sources)) + [VM] * len(extra),
            anys(shapes) + [vm((count, size), bf16), vm((count, width), f32)],
            [
                pltpu.VMEM((2, width, size), bf16), pltpu.VMEM((ff, width), bf16),
                pltpu.VMEM((2, width, size), bf16), pltpu.VMEM((width, count), bf16),
                pltpu.SemaphoreType.DMA((3,)),
            ],
            0 if part == 0 else 100, place, ffn_input, cotangent, *sources, *down_sources, *extra, mib=60,
        )
        act, acc = results[-2:]
        active.append(act)
        steps.leave(acc)
        turn = (2, 4) if part == 0 else (4, 2, True)
        gu_sums.append(scatter(narrow, wide, *blocks_of(results[:-2], 2), *turn))

    gu_sums[0].plane(steps)
    gu_sums[1].plane(steps)

    shapes = block_shapes(1, rows, width)
    if fine:
        down_grad_shapes = [shape((wide // 2, narrow, 2 * w_down.shape[0], half), bf16)] * 2
    else:
        down_grad_shapes = [shape((1, ff, width), bf16)]
    place = steps.enter(where)
    residual_grad, head, ffn_gain_part, output, *grads = call(
        functools.partial(
            turn_kernel, narrow, wide, attn_places, down_places, (len(attn_sources), len(down_sources))
        ),
        [SM] + [VM] * (5 + len(PARTS)) + [ANY] * (len(attn_sources) + len(down_sources)),
        [
            vm((count, width), f32), vm((width, count), bf16), vm((1, width), f32),
            vm((count, width), bf16),
        ] + anys(shapes + down_grad_shapes),
        [
            pltpu.VMEM((width, width), bf16), pltpu.VMEM((width, width), bf16),
            pltpu.VMEM((ff, width), bf16), pltpu.VMEM((ff, width), bf16),
            pltpu.SemaphoreType.DMA((4,)),
        ],
        100, place, residual, acc, cotangent, attended, vectors, *active, *attn_sources, *down_sources,
        mib=60,
    )
    steps.leave(head)
    out_grads, down_grads = grads[: len(shapes)], grads[len(shapes) :]
    out_sum = scatter(narrow, wide, *blocks_of(out_grads, 1), 4, 2, True)
    down_sum = scatter(narrow, wide, *blocks_of(down_grads, 1), joined=True)
    gu_sums[1].forward(steps)
    gu_sums[0].forward(steps)

    query_here = steps.enter(query)
    query_grad, key_grad, value_grad, score_grads = pl.pallas_call(
        attend_back_kernel,
        grid=(PAIRS,),
        in_specs=[row_block, key_block, key_block, turn_block, score_block],
        out_specs=[row_block, key_block, key_block, score_block],
        out_shape=(
            shape((count, width), bf16), shape((keys, width), bf16), shape((keys, width), bf16),
            shape((PAIRS, groups, 16, count), bf16),
        ),
        compiler_params=params(),
        cost_estimate=cost(100),
    )(query_here, key, value, head, probs)
    steps.leave(query_grad)
    out_sum.plane(steps)
    down_sum.plane(steps)

    shapes = block_shapes(3, rows, width)
    place = steps.enter(where)
    key_wide, value_wide, *qkv_grads = call(
        functools.partial(project_grads_kernel, narrow, wide),
        [SM] + [VM] * 5,
        [vm((count, width), bf16), vm((count, width), bf16)] + anys(shapes),
        [
            pltpu.VMEM((3, width, width), bf16), pltpu.VMEM((width, count), bf16),
            pltpu.SemaphoreType.DMA((3,)),
        ],
        100, place, attn_input, pick, query_grad, key_grad, value_grad,
    )
    steps.leave(key_wide)
    qkv_sum = scatter(narrow, wide, *blocks_of(qkv_grads, 3))
    gu_totals = [part.column(steps) for part in reversed(gu_sums)][::-1]
    gu_rows = Rows(steps, narrow, jnp.concatenate(gu_totals, axis=2))
    out_sum.forward(steps)

    place = steps.enter(where)
    tokens_grad, attn_gain_part, embed_part = call(
        functools.partial(project_back_kernel, narrow, wide, attn_places, len(attn_sources)),
        [SM] + [VM] * 7 + [ANY] * len(attn_sources),
        [vm((count, width), f32), vm((1, width), f32), vm((1, width), f32)],
        [pltpu.VMEM((3, width, width), bf16), pltpu.SemaphoreType.DMA((3,))],
        100, place, query_grad, key_wide, value_wide, tokens, hidden_column, vectors, residual_grad,
        *attn_sources,
    )
    steps.leave(tokens_grad)
    qkv_sum.plane(steps)
    down_sum.forward(steps)
    out_rows = Rows(steps, narrow, out_sum.column(steps))
    gu_rows.middle(steps)

    scores_here = steps.enter(score_grads)
    table_grads = pl.pallas_call(
        table_kernel,
        out_shape=shape((NB, 128), f32),
        scratch_shapes=[pltpu.VMEM((NB * 8, H * 8), f32)],
        compiler_params=params(),
        cost_estimate=cost(100),
    )(scores_here, rel_index, lay_index)
    steps.leave(table_grads)
    gu_total = gu_rows.finish(steps)
    out_rows.middle(steps)
    qkv_sum.forward(steps)
    down_rows = Rows(steps, narrow, down_sum.column(steps))
    table_grads = steps.enter(table_grads)[:, :H]
    parts = (attn_gain_part, ffn_gain_part, embed_part, table_grads[:NB_REL], table_grads[NB_REL:])
    parts = jnp.concatenate([v.reshape(devices, -1) for v in parts], axis=1).astype(bf16)
    small_sum = DirectScatter(narrow, wide, *sides(parts[:, None]))
    small_sum.plane(steps)
    qkv_sum.settle(steps)
    qkv_rows = Rows(steps, narrow, qkv_sum.column(steps))
    down_rows.middle(steps)
    small_rows = Rows(steps, narrow, small_sum.column(steps))
    out_total = out_rows.finish(steps)
    qkv_rows.middle(steps)
    small_rows.middle(steps)
    down_total = down_rows.finish(steps)
    if fine:
        rows_here = w_down.shape[0]
        mine = lax.dynamic_slice_in_dim(down_total, core * rows_here, rows_here, 0)
        other = lax.dynamic_slice_in_dim(down_total, (1 - core) * rows_here, rows_here, 0)
        other = flip_wide(other, 1, wide)
        down_total = jnp.where(
            core == 0, jnp.concatenate([mine, other], 1), jnp.concatenate([other, mine], 1)
        )
    qkv_total = qkv_rows.finish(steps)
    small_total = small_rows.finish(steps)[0]
    small_out, at = [], 0
    for p in smalls:
        small_out.append(small_total[at : at + p.shape[0]])
        at += p.shape[0]
    return (
        output, tokens_grad, qkv_total[:rows], qkv_total[rows : 2 * rows], qkv_total[2 * rows :],
        out_total, gu_total[:rows], gu_total[rows:], down_total, *small_out,
    )


def solution(mesh):
    both = P(("narrow", "wide"))
    table = P(("narrow", "wide"), None)
    return jax.shard_map(
        local,
        mesh=mesh,
        in_specs=(table, both, both) + (table,) * 9 + (both,) * 5 + (table,),
        out_specs=(table,) * 9 + (both,) * 5,
        check_vma=False,
    )
```

```python
import functools
import math

import jax
import jax.numpy as jnp
import numpy as np
from jax import lax
from jax.experimental import pallas as pl
from jax.experimental.pallas import tpu as pltpu
from jax.sharding import PartitionSpec as P

H = 16
HD = 64
PAIRS = H // 2
NB_REL = 32
NB_LAY = 64
NB = NB_REL + NB_LAY
HIDE = 192
PARTS = (2048, 768)
FFN_COST = (0, 100)
FF_STEP = 1024

eps_norm = 1e-06
neg_large = -1e30
f32 = jnp.float32
bf16 = jnp.bfloat16

NN = (((1,), (0,)), ((), ()))
NT = (((1,), (1,)), ((), ()))
TN = (((0,), (0,)), ((), ()))


def dot(a, b, dims=NN):
    return lax.dot_general(a, b, dims, preferred_element_type=f32)


def params(mib=56):
    return pltpu.CompilerParams(vmem_limit_bytes=mib * 1024 * 1024)


def cost(us):
    return pl.CostEstimate(flops=int(us * 1.5e9), bytes_accessed=0, transcendentals=0)


VM = pl.BlockSpec(memory_space=pltpu.VMEM)
SM = pl.BlockSpec(memory_space=pltpu.SMEM)
ANY = pl.BlockSpec(memory_space=pl.ANY)


def flip_narrow(x, bits, count):
    return lax.ppermute(x, "narrow", [(i, i ^ bits) for i in range(count)])


def narrow_order(count):
    order, bit = [0], count // 2
    while bit:
        order += [at ^ bit for at in order]
        bit //= 2
    return order


def flip_wide(x, bits, count):
    return lax.ppermute(x, "wide", [(i, i ^ bits) for i in range(count)])


class Steps:
    def __init__(self):
        self.last = ()

    def enter(self, *values):
        out = lax.optimization_barrier(tuple(values) + self.last)
        return out[: len(values)] if len(values) > 1 else out[0]

    def leave(self, *values):
        self.last = tuple(values)


class Columns:
    def __init__(self, narrow, x):
        self.narrow, self.stack, self.bit = narrow, x[None], narrow // 2

    def start(self, steps):
        stack = steps.enter(self.stack)
        self.stack, self.sent = stack, flip_narrow(stack, self.bit, self.narrow)

    def middle(self, steps):
        sent = steps.enter(self.sent)
        self.stack = jnp.concatenate([self.stack, sent])
        steps.leave(self.stack)
        self.bit //= 2
        if self.bit:
            self.sent = flip_narrow(self.stack, self.bit, self.narrow)

    def finish(self, steps):
        while self.bit:
            self.middle(steps)
        return self.stack

    def halves(self, steps):
        while self.bit > 1:
            self.middle(steps)
        sent = steps.enter(self.sent)
        steps.leave(sent)
        return self.stack, sent


class Gather:
    def __init__(self, wide, first=2, second=4, direct=False, split=False, halves=False):
        self.wide, self.bits, self.direct = wide, (first, second), direct
        self.split, self.halves = split, halves

    def add(self, array, chip, split=False):
        self.pieces.append((array, 0, chip, 0))
        half = array.shape[0] // 2
        for low in (0, half) if split else (0,):
            part = array[low : low + half] if split else array
            self.crossed.append((flip_wide(part, 1, self.wide), 1, chip, low))

    def plane(self, steps, column):
        column = steps.enter(column)
        steps.leave(column)
        self.near = [flip_wide(column, bit, self.wide) for bit in self.bits]
        if self.direct:
            self.far = [flip_wide(column, 6, self.wide)]
        self.pieces, self.crossed = [], []
        self.add(column, 0)

    def settle(self, steps, at):
        self.near[at] = steps.enter(self.near[at])
        steps.leave(self.near[at])

    def forward(self, steps):
        near, other = steps.enter(*self.near)
        steps.leave(near)
        if not self.direct:
            half = near.shape[0] // 2
            parts = [near[:half], near[half:]] if self.halves else [near]
            self.far = [flip_wide(part, self.bits[1], self.wide) for part in parts]
        self.add(near, self.bits[0] // 2)
        self.add(other, self.bits[1] // 2)

    def cross(self, steps):
        arrays = steps.enter(*[p[0] for p in self.crossed])
        steps.leave(arrays[-1])
        self.crossed = [(a,) + p[1:] for a, p in zip(arrays, self.crossed)]

    def arrive(self, steps):
        if self.halves:
            low = 0
            for far in steps.enter(*self.far):
                steps.leave(far)
                self.pieces.append((far, 0, 3, low))
                self.crossed.append((flip_wide(far, 1, self.wide), 1, 3, low))
                low += far.shape[0]
        else:
            far = steps.enter(self.far[0])
            steps.leave(far)
            self.add(far, 3, self.split)

    def finish(self, steps):
        arrays = steps.enter(*[p[0] for p in self.crossed])
        steps.leave(arrays[-1])
        return self.pieces + [(a,) + p[1:] for a, p in zip(arrays, self.crossed)]


class PlaneFirst:
    def __init__(self, narrow, wide, x):
        self.narrow, self.wide, self.x = narrow, wide, x

    def start(self, steps):
        x = steps.enter(self.x)
        self.x = x
        self.near = [flip_wide(x, bit, self.wide) for bit in (2, 4)]

    def forward(self, steps):
        self.near = steps.enter(*self.near)
        steps.leave(self.near[0])
        self.far = flip_wide(self.near[0], 4, self.wide)

    def arrive(self, steps):
        far = steps.enter(self.far)
        blocks = [self.x, *self.near, far]
        self.columns = [Columns(self.narrow, jnp.stack(blocks))]
        steps.leave(*[c.stack for c in self.columns])

    def columns_start(self, steps):
        for column in self.columns:
            column.start(steps)

    def columns_middle(self, steps):
        for column in self.columns:
            column.middle(steps)

    def cores(self, steps):
        halves = [column.halves(steps) for column in self.columns]
        self.pieces = [
            (part, 0, 2 * n, low) for n, pair in enumerate(halves)
            for part, low in zip(pair, (0, self.narrow // 2))
        ]
        self.crossed = [flip_wide(p[0], 1, self.wide) for p in self.pieces]

    def finish(self, steps):
        crossed = steps.enter(*self.crossed)
        steps.leave(*crossed)
        return self.pieces + [(a, 1) + p[2:] for a, p in zip(crossed, self.pieces)]


class PlainDown(Gather):
    def __init__(self, narrow, wide, x):
        self.column, self.inner = Columns(narrow, x), PlainGather(wide)

    def start(self, steps):
        self.column.start(steps)

    def forward(self, steps):
        pass

    def arrive(self, steps):
        pass

    def columns_start(self, steps):
        pass

    def columns_middle(self, steps):
        pass

    def cores(self, steps):
        self.inner.plane(steps, self.column.finish(steps))
        self.inner.arrive(steps)

    def finish(self, steps):
        return self.inner.finish(steps)


class SmallGather:
    def __init__(self, narrow, wide, x):
        self.narrow, self.wide, self.stack, self.bits = narrow, wide, x[None], []
        bit = 1
        while bit < narrow:
            self.bits.append((flip_narrow, bit, narrow))
            bit *= 2
        bit = 2
        while bit < wide:
            self.bits.append((flip_wide, bit, wide))
            bit *= 2

    def start(self, steps):
        self.stack = steps.enter(self.stack)
        self.send()

    def send(self):
        if self.bits:
            flip, bit, count = self.bits.pop(0)
            self.sent = flip(self.stack, bit, count)
        else:
            self.sent = None

    def middle(self, steps):
        self.stack = jnp.concatenate([self.stack, steps.enter(self.sent)])
        steps.leave(self.stack)
        self.send()
        if self.sent is None:
            self.crossed = flip_wide(self.stack, 1, self.wide)

    def finish(self, steps):
        while self.sent is not None:
            self.middle(steps)
        crossed = steps.enter(self.crossed)
        steps.leave(crossed)
        return [self.stack, crossed]


class PlainGather(Gather):
    def plane(self, steps, column):
        column = steps.enter(column)
        steps.leave(column)
        found = {0: column}
        bit = 2
        while bit < self.wide:
            for at in list(found):
                found[at ^ bit] = flip_wide(found[at], bit, self.wide)
            bit *= 2
        self.pieces, self.crossed = [], []
        for at, array in found.items():
            self.add(array, at // 2)

    def settle(self, steps, at):
        pass

    def cross(self, steps):
        pass

    def forward(self, steps):
        pass

    def arrive(self, steps):
        pass


def ordered(pieces, narrow, wide):
    table = [None] * wide
    for array, core, chip, _ in pieces:
        table[2 * chip + core] = array
    order = jnp.arange(wide) ^ lax.axis_index("wide")
    place = np.argsort(narrow_order(narrow))
    shift = jnp.asarray(place)[jnp.arange(narrow) ^ lax.axis_index("narrow")]
    full = jnp.stack(table, axis=1)[shift[:, None], order[None]]
    return full.reshape((narrow * wide,) + full.shape[2:])


class Scatter:
    def __init__(self, narrow, wide, keep, send, first=2, second=4, joined=False):
        self.narrow, self.wide, self.keep, self.bits = narrow, wide, keep, (first, second)
        self.joined = joined
        self.sent = flip_wide(send, 1, wide)

    def plane(self, steps):
        self.sent = steps.enter(self.sent)
        second = self.bits[1]
        mine = [self.chip(n).astype(bf16) for n in (3, second // 2)]
        if self.joined:
            mine = [jnp.stack(mine)]
        steps.leave(*mine)
        self.away = [flip_wide(part, second, self.wide) for part in mine]

    def chip(self, n):
        return self.keep[n].astype(f32) + self.sent[n].astype(f32)

    def settle(self, steps):
        self.away[1] = steps.enter(self.away[1])
        steps.leave(self.away[1])

    def forward(self, steps):
        if self.joined:
            self.away = list(steps.enter(self.away[0]))
        else:
            self.away[0] = steps.enter(self.away[0])
        first = self.bits[0]
        both = (self.chip(first // 2) + self.away[0].astype(f32)).astype(bf16)
        steps.leave(both)
        self.near = flip_wide(both, first, self.wide)

    def column(self, steps):
        if self.joined:
            near, straight = steps.enter(self.near), self.away[1]
        else:
            near, straight = steps.enter(self.near, self.away[1])
        total = self.chip(0) + straight.astype(f32) + near.astype(f32)
        total = total.astype(bf16)
        steps.leave(total)
        return total


class DirectScatter(Scatter):
    def plane(self, steps):
        sent = steps.enter(self.sent)
        mine = (self.keep.astype(f32) + sent.astype(f32)).astype(bf16)
        steps.leave(mine)
        self.mine = mine
        self.other = [flip_wide(mine[n], 2 * n, self.wide) for n in range(1, self.wide // 2)]

    def column(self, steps):
        other = steps.enter(*self.other)
        total = self.mine[0].astype(f32)
        for part in other:
            total = total + part.astype(f32)
        total = total.astype(bf16)
        steps.leave(total)
        return total


class Rows:
    def __init__(self, steps, narrow, mine):
        self.narrow, self.bit = narrow, 1
        z = lax.axis_index("narrow")
        self.mine = [lax.dynamic_index_in_dim(mine, z ^ n, 0, False) for n in range(narrow)]
        self.send()

    def send(self):
        away = jnp.stack([part for n, part in enumerate(self.mine) if n & 1])
        self.mine = [part for n, part in enumerate(self.mine) if not n & 1]
        self.sent = flip_narrow(away, self.bit, self.narrow)

    def middle(self, steps):
        sent = steps.enter(self.sent)
        self.mine = [part.astype(f32) + sent[n].astype(f32) for n, part in enumerate(self.mine)]
        self.bit *= 2
        if self.bit < self.narrow:
            self.mine = [part.astype(bf16) for part in self.mine]
            steps.leave(*self.mine)
            self.send()
        else:
            steps.leave(self.mine[0])

    def finish(self, steps):
        while self.bit < self.narrow:
            self.middle(steps)
        return self.mine[0]


class DirectRows:
    def __init__(self, steps, narrow, mine):
        z = lax.axis_index("narrow")
        parts = [lax.dynamic_index_in_dim(mine, z ^ n, 0, False) for n in range(narrow)]
        self.own = parts[0]
        self.sent = [flip_narrow(parts[n], n, narrow) for n in range(1, narrow)]

    def middle(self, steps):
        pass

    def finish(self, steps):
        sent = steps.enter(*self.sent)
        total = self.own.astype(f32)
        for part in sent:
            total = total + part.astype(f32)
        steps.leave(total)
        return total


class PlainScatter(Scatter):
    def plane(self, steps):
        sent = steps.enter(self.sent)
        mine = self.keep.astype(f32) + sent.astype(f32)
        bit = self.wide // 2
        while bit > 1:
            half = mine.shape[0] // 2
            low = mine.astype(bf16)
            mine = low[:half].astype(f32) + flip_wide(low[half:], bit, self.wide).astype(f32)
            bit //= 2
        self.total = mine[0].astype(bf16)

    def settle(self, steps):
        pass

    def forward(self, steps):
        pass

    def column(self, steps):
        return self.total


def piece_arrays(pieces):
    return [p[0] for p in pieces]


def piece_places(pieces):
    return [p[1:] for p in pieces]


def load_rows(where, sources, places, index, rows, dst, sem, narrow, wide):
    if places is None:
        pltpu.make_async_copy(sources[0].at[index], dst, sem).start()
        return
    for src, (core, chip, low) in zip(sources, places):
        w = jnp.bitwise_xor(where[1], 2 * chip + core)
        for n, flip in enumerate(narrow_order(narrow)[low : low + src.shape[0]]):
            z = jnp.bitwise_xor(where[0], flip)
            row = pl.multiple_of((z * wide + w) * rows, rows)
            pltpu.make_async_copy(
                src.at[n, pl.ds(index * rows, rows)], dst.at[pl.ds(row, rows), :], sem
            ).start()


def load_pairs(where, sources, places, dst, sem, narrow, wide):
    if places is None:
        pltpu.make_async_copy(sources[0].at[0], dst, sem).start()
        return
    for src, (core, chip, low) in zip(sources, places):
        rows, lanes = src.shape[2:]
        lane = pl.multiple_of(jnp.bitwise_xor(jnp.bitwise_and(where[1], 1), core) * lanes, lanes)
        for n, flip in enumerate(narrow_order(narrow)[low : low + src.shape[0]]):
            z = jnp.bitwise_xor(where[0], flip)
            for flip in range(src.shape[1]):
                c = jnp.bitwise_xor(lax.shift_right_logical(where[1], 1), chip + flip)
                row = pl.multiple_of((z * (wide // 2) + c) * rows, rows)
                pltpu.make_async_copy(
                    src.at[n, flip], dst.at[pl.ds(row, rows), pl.ds(lane, lanes)], sem
                ).start()


def wait_all(ref, sem):
    pltpu.make_async_copy(ref, ref, sem).wait()


def store_rows(where, src, out, index, rows, sem, narrow, wide):
    if len(out) == 1:
        pltpu.make_async_copy(src, out[0].at[index], sem).start()
        return
    core = jnp.bitwise_and(where[1], 1)
    chip = lax.shift_right_logical(where[1], 1)
    for z in range(narrow):
        for c in range(wide // 2):
            flip = jnp.bitwise_xor(chip, c)
            for dst, side in zip(out, (core, 1 - core)):
                row = pl.multiple_of((z * wide + 2 * c + side) * rows, rows)
                pltpu.make_async_copy(
                    src.at[pl.ds(row, rows), :], dst.at[flip, z, pl.ds(index * rows, rows)], sem
                ).start()


def store_pairs(where, src, out, sem, narrow, wide):
    if len(out) == 1:
        pltpu.make_async_copy(src, out[0].at[0], sem).start()
        return
    core = jnp.bitwise_and(where[1], 1)
    chip = lax.shift_right_logical(where[1], 1)
    rows, lanes = out[0].shape[2:]
    for z in range(narrow):
        for c in range(wide // 2):
            flip = jnp.bitwise_xor(chip, c)
            for dst, side in zip(out, (core, 1 - core)):
                lane = pl.multiple_of(side * lanes, lanes)
                pltpu.make_async_copy(
                    src.at[pl.ds((z * (wide // 2) + c) * rows, rows), pl.ds(lane, lanes)],
                    dst.at[flip, z],
                    sem,
                ).start()


def prepare_kernel(hidden_ref, segment_ref, rel_ref, lay_ref, pick_ref, rel_out, lay_out):
    count = hidden_ref.shape[1]
    keys = pick_ref.shape[0]
    seen = hidden_ref[...] == 0
    before = lax.broadcasted_iota(jnp.int32, (count, count), 0)
    after = lax.broadcasted_iota(jnp.int32, (count, count), 1)
    upper = jnp.where(before <= after, 1.0, 0.0).astype(bf16)
    seen_rows = jnp.broadcast_to(jnp.where(seen, 1.0, 0.0), (16, count)).astype(bf16)
    rank = dot(seen_rows, upper)[0:1].astype(jnp.int32) - 1
    rank = jnp.where(seen, rank, -1)
    number = lax.broadcasted_iota(jnp.int32, (keys, count), 0)
    pick = jnp.where(number == rank, 1.0, 0.0).astype(bf16)
    pick_ref[...] = pick
    segment = jnp.broadcast_to(segment_ref[...].astype(f32), (16, count)).astype(bf16)
    key_segment = dot(pick, segment, NT)[:, 0:1]
    valid = key_segment == segment_ref[...].astype(f32)
    rel = dot(pick, rel_ref[...].astype(f32).astype(bf16), NT).astype(jnp.int32)
    lay = dot(pick, lay_ref[...].astype(f32).astype(bf16), NT).astype(jnp.int32)
    rel_out[...] = jnp.where(valid, rel, NB)
    lay_out[...] = lay + NB_REL


def bias_kernel(low, table_ref, rel_ref, lay_ref, *refs):
    out_ref = refs[-1]
    keys, count = rel_ref.shape
    groups = keys // 8
    pair = pl.program_id(0) + low
    tables = [
        jnp.broadcast_to(table_ref[pl.ds(2 * pair + side, 1), :], (keys, 128)) for side in range(2)
    ]
    for c in range(count // 128):
        lanes = slice(c * 128, c * 128 + 128)
        for side in range(2):
            found = jnp.take_along_axis(tables[side], rel_ref[:, lanes], axis=1)
            found = found + jnp.take_along_axis(tables[side], lay_ref[:, lanes], axis=1)
            out_ref[0, :, side * 8 : side * 8 + 8, lanes] = found.reshape(groups, 8, 128)


def embed(tokens_ref, hidden_ref, vectors_ref):
    return jnp.where(hidden_ref[...] == 1.0, vectors_ref[2:3, :], tokens_ref[...].astype(f32))


def inverse_rms(v):
    return lax.rsqrt(jnp.mean(v * v, axis=-1, keepdims=True) + eps_norm)


def pack_kernel(where, wide, lengths, *refs):
    query, key, value, out, gate, up, down, smalls = refs[:8]
    attn_ref, small_ref, first_ref, second_ref = refs[8:12]
    rows = query.shape[0]
    for n, ref in enumerate((query, key, value, out)):
        attn_ref[n * rows : (n + 1) * rows, :] = ref[...].astype(bf16)
    own = where[0] * wide + where[1]
    dims = (8, smalls.shape[1])
    row = lax.broadcasted_iota(jnp.int32, dims, 0)
    lane = lax.broadcasted_iota(jnp.int32, dims, 1)
    spread = jnp.broadcast_to(smalls[...], dims)
    placed = jnp.zeros(dims, f32)
    at = 0
    for n, length in enumerate(lengths):
        part = jnp.where((row == n) & (lane >= at) & (lane < at + length), spread, 0.0)
        placed = placed + pltpu.roll(part, own * length + (dims[1] - at), 1)
        at += length
    small_ref[...] = placed.astype(bf16)
    size = first_ref.shape[1]
    for n, ref in enumerate((gate, up)):
        first_ref[n * rows : (n + 1) * rows, :] = ref[:, 0:size].astype(bf16)
        second_ref[n * rows : (n + 1) * rows, :] = ref[:, size:].astype(bf16)
    if len(refs) == 13:
        refs[12][...] = down[...].astype(bf16)
    else:
        half = down.shape[1] // 2
        core = jnp.bitwise_and(where[1], 1)
        for n, side in enumerate((core, 1 - core)):
            lanes = pl.ds(pl.multiple_of(side * half, half), half)
            refs[12 + n][...] = down[:, lanes].astype(bf16)


def unpack_kernel(left_ref, right_ref, vectors_ref, table_ref):
    width = vectors_ref.shape[1]
    vectors = jnp.sum(left_ref[...].astype(f32), axis=0) + jnp.sum(right_ref[...].astype(f32), axis=0)
    vectors_ref[...] = vectors
    lane = lax.broadcasted_iota(jnp.int32, (H, width), 1)
    head = lax.broadcasted_iota(jnp.int32, (H, width), 0)
    entry = lax.broadcasted_iota(jnp.int32, (width, 128), 0) // H
    bucket = lax.broadcasted_iota(jnp.int32, (width, 128), 1)
    end = lax.broadcasted_iota(jnp.int32, (H, 128), 1)
    table = jnp.where(end >= NB, neg_large, 0.0)
    for n, first in ((3, 0), (4, NB_REL)):
        split = jnp.where(lane % H == head, vectors[n : n + 1], 0.0).astype(bf16)
        spot = jnp.where(entry + first == bucket, 1.0, 0.0).astype(bf16)
        table = table + dot(split, spot)
    table_ref[...] = table


def project_kernel(narrow, wide, places, where, tokens_ref, hidden_ref, pick_ref, vectors_ref, *refs):
    sources = refs[:-6]
    input_ref, query_ref, key_ref, value_ref, weights, sems = refs[-6:]
    width = tokens_ref.shape[1]
    rows = width // (narrow * wide)
    for n in range(3):
        load_rows(where, sources, places, n, rows, weights.at[n], sems.at[n], narrow, wide)
    embedded = embed(tokens_ref, hidden_ref, vectors_ref)
    attn_input = (embedded * inverse_rms(embedded) * vectors_ref[0:1, :]).astype(bf16)
    input_ref[...] = attn_input
    seen = dot(pick_ref[...], attn_input).astype(bf16)
    wait_all(weights.at[0], sems.at[0])
    query_ref[...] = dot(attn_input, weights[0]).astype(bf16)
    wait_all(weights.at[1], sems.at[1])
    key_ref[...] = dot(seen, weights[1]).astype(bf16)
    wait_all(weights.at[2], sems.at[2])
    value_ref[...] = dot(seen, weights[2]).astype(bf16)


def by_side(x):
    keys = x.shape[0]
    wide = x.astype(f32).reshape(keys // 8, 8, 128)
    left = lax.broadcasted_iota(jnp.int32, wide.shape, 2) < HD
    both = jnp.concatenate([jnp.where(left, wide, 0.0), jnp.where(left, 0.0, wide)], axis=1)
    return both.astype(bf16).reshape(keys * 2, 128)


def own_side(x):
    x = x.reshape(x.shape[0] // 16, 16, 128)
    left = lax.broadcasted_iota(jnp.int32, (x.shape[0], 8, 128), 2) < HD
    return jnp.where(left, x[:, 0:8], x[:, 8:16]).reshape(x.shape[0] * 8, 128)


def per_side(x, fold, spread):
    return jnp.concatenate(
        [
            jnp.broadcast_to(fold(x[side * 8 : side * 8 + 8], axis=0, keepdims=True), (8, spread))
            for side in range(2)
        ],
        axis=0,
    )[None]


def attend_kernel(query_ref, key_ref, value_ref, bias_ref, attended_ref, probs_ref):
    count = query_ref.shape[0]
    keys = key_ref.shape[0]
    for n in range(bias_ref.shape[0]):
        lanes = slice(n * 128, n * 128 + 128)
        scores = dot(by_side(key_ref[:, lanes]), query_ref[:, lanes], NT).reshape(keys // 8, 16, count)
        scores = scores + bias_ref[n]
        top = per_side(jnp.max(scores, axis=0), jnp.max, count)
        exponent = jnp.exp(scores - top)
        total = per_side(jnp.sum(exponent, axis=0), jnp.sum, count)
        probs = (exponent * (1.0 / total)).astype(bf16)
        probs_ref[n] = probs
        attended = dot(by_side(value_ref[:, lanes]), probs.reshape(keys * 2, count), TN)
        attended_ref[lanes, :] = attended.astype(bf16)


def residual_kernel(
    narrow, wide, places, where, attended_ref, tokens_ref, hidden_ref, vectors_ref, *refs
):
    sources = refs[:-4]
    residual_ref, input_ref, weight, sem = refs[-4:]
    rows = weight.shape[0] // (narrow * wide)
    load_rows(where, sources, places, 3, rows, weight, sem, narrow, wide)
    embedded = embed(tokens_ref, hidden_ref, vectors_ref)
    wait_all(weight, sem)
    residual = embedded + dot(attended_ref[...], weight[...], TN)
    residual_ref[...] = residual
    input_ref[...] = (residual * inverse_rms(residual) * vectors_ref[1:2, :]).astype(bf16)


def gelu_parts(v):
    scale = math.sqrt(2.0 / math.pi)
    square = v * v
    bend = jnp.tanh(scale * v * (1.0 + 0.044715 * square))
    half = 0.5 * (1.0 + bend)
    slope = half + 0.5 * v * (1.0 - bend * bend) * (scale * (1.0 + 3 * 0.044715 * square))
    return v * half, slope


def ffn_kernel(narrow, wide, low, counts, places, down_places, where, input_ref, cot_ref, *refs):
    sources, refs = refs[: counts[0]], refs[counts[0] :]
    down_sources, refs = refs[: counts[1]], refs[counts[1] :]
    acc_in, refs = (None, refs) if low == 0 else (refs[0], refs[1:])
    out, refs = refs[: counts[2]], refs[counts[2] :]
    active_ref, acc_ref, weights, down_ref, grads, turned, sems = refs
    width = input_ref.shape[1]
    rows = width // (narrow * wide)
    size = active_ref.shape[1]
    for n in range(2):
        load_rows(where, sources, places, n, rows, weights.at[n], sems.at[n], narrow, wide)
    load_pairs(where, down_sources, down_places, down_ref, sems.at[2], narrow, wide)
    x = input_ref[...]
    turned[...] = x.T
    steps = [slice(at, min(at + FF_STEP, size)) for at in range(0, size, FF_STEP)]
    acc = None if acc_in is None else acc_in[...]
    for at, lanes in enumerate(steps):
        if at == 0:
            wait_all(weights.at[0], sems.at[0])
        gate = dot(x, weights[0, :, lanes])
        gelu, slope = gelu_parts(gate)
        if at == 0:
            wait_all(weights.at[1], sems.at[1])
        up = dot(x, weights[1, :, lanes])
        active_ref[:, lanes] = (gelu * up).astype(bf16)
        if at == 0:
            wait_all(down_ref, sems.at[2])
        act_grad = dot(cot_ref[...], down_ref[low + lanes.start : low + lanes.stop, :], NT)
        up_back = (act_grad * gelu).astype(bf16)
        gate_back = (act_grad * up * slope).astype(bf16)
        last = at == len(steps) - 1
        for n, back in ((1, up_back), (0, gate_back)):
            grads[n, :, lanes] = dot(turned[...], back).astype(bf16)
            if last:
                store_rows(where, grads.at[n], out, n, rows, sems.at[n], narrow, wide)
        for n, back in ((1, up_back), (0, gate_back)):
            term = dot(back, weights[n, :, lanes], NT)
            acc = term if acc is None else acc + term
    acc_ref[...] = acc
    for n in range(2):
        wait_all(grads.at[n], sems.at[n])


def turn_kernel(narrow, wide, places, down_places, counts, where, *refs):
    residual_ref, ffn_ref, cot_ref, attended_ref, vectors_ref = refs[:5]
    actives, refs = refs[5 : 5 + len(PARTS)], refs[5 + len(PARTS) :]
    sources, down_sources, refs = refs[: counts[0]], refs[counts[0] : counts[0] + counts[1]], refs[sum(counts) :]
    grad_ref, head_ref, gain_out, output_ref = refs[:4]
    weight, grads, down, down_grads, sems = refs[-5:]
    out, down_out = refs[4:-5][: len(refs[4:-5]) // 2], refs[4:-5][len(refs[4:-5]) // 2 :]
    rows = weight.shape[0] // (narrow * wide)
    load_rows(where, sources, places, 3, rows, weight, sems.at[0], narrow, wide)
    load_pairs(where, down_sources, down_places, down, sems.at[2], narrow, wide)
    cot = cot_ref[...]
    residual = residual_ref[...]
    inverse = inverse_rms(residual)
    normed = residual * inverse
    ffn_grad = ffn_ref[...]
    gain_out[...] = jnp.sum(ffn_grad * normed, axis=0, keepdims=True)
    scaled = ffn_grad * vectors_ref[1:2, :]
    center = jnp.mean(scaled * normed, axis=-1, keepdims=True)
    grad = cot.astype(f32) + (scaled - normed * center) * inverse
    grad_ref[...] = grad
    low = grad.astype(bf16)
    grads[...] = dot(attended_ref[...], low).astype(bf16)
    store_rows(where, grads, out, 0, rows, sems.at[1], narrow, wide)
    at = 0
    for ref in actives:
        down_grads[at : at + ref.shape[1], :] = dot(ref[...], cot, TN).astype(bf16)
        at += ref.shape[1]
    store_pairs(where, down_grads, down_out, sems.at[3], narrow, wide)
    wait_all(weight, sems.at[0])
    head_ref[...] = dot(weight[...], low, NT).astype(bf16)
    wait_all(down, sems.at[2])
    total = residual
    at = 0
    for ref in actives:
        total = total + dot(ref[...], down[at : at + ref.shape[1], :])
        at += ref.shape[1]
    output_ref[...] = total.astype(bf16)
    wait_all(grads, sems.at[1])
    wait_all(down_grads, sems.at[3])


def attend_back_kernel(
    query_ref, key_ref, value_ref, head_ref, probs_ref, query_out, key_out, value_out, scores_ref
):
    count = query_ref.shape[0]
    keys = key_ref.shape[0]
    for n in range(probs_ref.shape[0]):
        lanes = slice(n * 128, n * 128 + 128)
        low = probs_ref[n]
        head = head_ref[lanes, :]
        probs = low.astype(f32)
        prob_grad = dot(by_side(value_ref[:, lanes]), head).reshape(keys // 8, 16, count)
        center = per_side(jnp.sum(probs * prob_grad, axis=0), jnp.sum, count)
        score_grad = (probs * (prob_grad - center)).astype(bf16)
        scores_ref[n] = score_grad
        score_grad = score_grad.reshape(keys * 2, count)
        query_grad = dot(by_side(key_ref[:, lanes]), score_grad, TN)
        query_out[:, lanes] = query_grad.T.astype(bf16)
        key_out[:, lanes] = own_side(dot(score_grad, query_ref[:, lanes])).astype(bf16)
        value_out[:, lanes] = own_side(dot(low.reshape(keys * 2, count), head, NT)).astype(bf16)


def table_kernel(scores_ref, rel_ref, lay_ref, out_ref, total):
    keys, count = rel_ref.shape
    total[...] = jnp.zeros_like(total)

    def step(g, _):
        rows = pl.ds(pl.multiple_of(g * 8, 8), 8)
        hot = []
        for ids, low, high in ((rel_ref[rows, :], 0, NB_REL), (lay_ref[rows, :], NB_REL, NB)):
            for b in range(low, high, 2):
                pair = [jnp.where(ids == b + n, 1.0, 0.0) for n in range(2)]
                hot.append(jnp.concatenate(pair, axis=0).astype(bf16))
        hot = jnp.concatenate(hot, axis=0)
        grads = scores_ref[:, pl.ds(g, 1)].reshape(H * 8, count)
        total[...] += dot(hot, grads, NT)
        return 0

    lax.fori_loop(0, keys // 8, step, 0, unroll=4)
    row = lax.broadcasted_iota(jnp.int32, total.shape, 0) % 8
    lane = lax.broadcasted_iota(jnp.int32, total.shape, 1) % 8
    own = jnp.where(row == lane, total[...], 0.0)
    own = jnp.sum(own.reshape(NB, 8, H * 8), axis=1)
    fold = lax.broadcasted_iota(jnp.int32, (H * 8, 128), 0) // 8
    fold = jnp.where(fold == lax.broadcasted_iota(jnp.int32, (H * 8, 128), 1), 1.0, 0.0)
    out_ref[...] = jnp.dot(own, fold, precision=lax.Precision.HIGHEST, preferred_element_type=f32)


def spread_rows(pick_ref, ref):
    return dot(pick_ref[...], ref[...], TN).astype(bf16)


def project_grads_kernel(
    narrow, wide, where, input_ref, pick_ref, query_ref, key_ref, value_ref, key_out, value_out, *refs
):
    out, (grads, turned, sems) = refs[:-3], refs[-3:]
    rows = turned.shape[0] // (narrow * wide)
    turned[...] = input_ref[...].T
    key_out[...] = spread_rows(pick_ref, key_ref)
    value_out[...] = spread_rows(pick_ref, value_ref)
    for n, ref in enumerate((query_ref, key_out, value_out)):
        grads[n] = dot(turned[...], ref[...]).astype(bf16)
        store_rows(where, grads.at[n], out, n, rows, sems.at[n], narrow, wide)
    for n in range(3):
        wait_all(grads.at[n], sems.at[n])


def project_back_kernel(
    narrow, wide, places, count, where, query_ref, key_ref, value_ref, tokens_ref, hidden_ref,
    vectors_ref, residual_ref, *refs
):
    sources, refs = refs[:count], refs[count:]
    tokens_out, gain_out, embed_out, weights, sems = refs
    rows = weights.shape[1] // (narrow * wide)
    for n in range(3):
        load_rows(where, sources, places, n, rows, weights.at[n], sems.at[n], narrow, wide)
    embedded = embed(tokens_ref, hidden_ref, vectors_ref)
    inverse = inverse_rms(embedded)
    normed = embedded * inverse
    attn_grad = None
    for n, ref in enumerate((query_ref, key_ref, value_ref)):
        wait_all(weights.at[n], sems.at[n])
        term = dot(ref[...], weights[n], NT)
        attn_grad = term if n == 0 else attn_grad + term
    gain_out[...] = jnp.sum(attn_grad * normed, axis=0, keepdims=True)
    scaled = attn_grad * vectors_ref[0:1, :]
    center = jnp.mean(scaled * normed, axis=-1, keepdims=True)
    grad = residual_ref[...] + (scaled - normed * center) * inverse
    concealed = hidden_ref[...] == 1.0
    tokens_out[...] = jnp.where(concealed, 0.0, grad)
    embed_out[...] = jnp.sum(jnp.where(concealed, grad, 0.0), axis=0, keepdims=True)


def shape(dims, kind):
    return jax.ShapeDtypeStruct(tuple(dims), kind)


def local(
    tokens, hidden_patch, segment_ids, rel_ids, layout_ids, w_query, w_key, w_value, w_out, w_gate,
    w_up, w_down, gain_attn, gain_ffn, mask_embed, rel_table, layout_table, cotangent,
):
    narrow, wide = lax.axis_size("narrow"), lax.axis_size("wide")
    devices = narrow * wide
    count, width = tokens.shape
    keys = count - HIDE
    ff = w_gate.shape[1]
    rows = w_query.shape[0]
    where = jnp.stack([lax.axis_index("narrow"), lax.axis_index("wide")]).astype(jnp.int32)
    core = lax.axis_index("wide") % 2

    fine = narrow % 2 == 0 and wide == 8 and rows % 16 == 0 and w_down.shape[0] % 8 == 0
    gather, scatter = (Gather, Scatter) if fine else (PlainGather, PlainScatter)
    steps = Steps()

    def sources_of(pieces, low_rows):
        if fine:
            return piece_arrays(pieces), piece_places(pieces)
        full = ordered(pieces, narrow, wide)
        full = full.reshape((devices, full.shape[1] // low_rows, -1) + full.shape[2:])
        return [jnp.swapaxes(full, 0, 1).reshape(full.shape[1], -1, full.shape[-1])], None

    chip_flip, z_index = jnp.meshgrid(jnp.arange(wide // 2), jnp.arange(narrow), indexing="ij")

    def sides(parts):
        flip = (chip_flip * 2) ^ lax.axis_index("wide")
        return [parts[z_index * wide + (flip ^ side)] for side in range(2)]

    def blocks_of(grads, number):
        if fine:
            return grads
        parts = grads[0].reshape(number, devices, -1, grads[0].shape[-1])
        return sides(jnp.swapaxes(parts, 0, 1).reshape(devices, -1, parts.shape[-1]))

    def block_shapes(number, block_rows, lanes):
        if fine:
            return [shape((wide // 2, narrow, number * block_rows, lanes), bf16)] * 2
        return [shape((number, devices * block_rows, lanes), bf16)]

    def call(kernel, in_specs, outs, scratch, us, *args, mib=56):
        return pl.pallas_call(
            kernel,
            in_specs=in_specs,
            out_specs=[o[0] for o in outs],
            out_shape=[o[1] for o in outs],
            scratch_shapes=scratch,
            compiler_params=params(mib),
            cost_estimate=cost(us),
        )(*args)

    def vm(dims, kind):
        return (VM, shape(dims, kind))

    def anys(shapes):
        return [(ANY, x) for x in shapes]

    smalls = (gain_attn, gain_ffn, mask_embed, rel_table, layout_table)
    lengths = tuple(p.shape[0] for p in smalls)
    small = jnp.concatenate(smalls + (jnp.zeros(width - sum(lengths), f32),))[None]
    bounds = [0, PARTS[0], ff]
    half = width // 2
    down_shapes = [(w_down.shape[0], half)] * 2 if fine else [w_down.shape]
    attn_low, small_low, first_low, second_low, *down_low = pl.pallas_call(
        lambda where_ref, *refs: pack_kernel(where_ref, wide, lengths, *refs),
        in_specs=[SM] + [VM] * 8,
        out_shape=[
            shape(dims, bf16)
            for dims in [(4 * rows, width), (8, width), (2 * rows, PARTS[0]), (2 * rows, PARTS[1])] + down_shapes
        ],
        compiler_params=params(),
        cost_estimate=cost(0),
    )(where, w_query, w_key, w_value, w_out, w_gate, w_up, w_down, small)
    smalls_gather = SmallGather(narrow, wide, small_low)
    attn_column = Columns(narrow, attn_low)
    attn = gather(wide, split=True)
    gu_columns = [Columns(narrow, jnp.concatenate([first_low, second_low], axis=1))]
    gu = [gather(wide, 4, 2, halves=True), gather(wide, direct=True)]
    if fine:
        mine, other = down_low
        other = flip_wide(other, 1, wide)
        down_low = jnp.where(
            core == 0, jnp.concatenate([mine, other]), jnp.concatenate([other, mine])
        )
    else:
        down_low = down_low[0]
    down = (PlaneFirst if fine else PlainDown)(narrow, wide, down_low)

    hidden_column = hidden_patch.astype(f32)[:, None]
    smalls_gather.start(steps)
    attn_column.start(steps)
    steps.leave(attn_low)
    hidden_row = steps.enter(hidden_patch[None])
    pick, rel_index, lay_index = pl.pallas_call(
        prepare_kernel,
        out_shape=(
            shape((keys, count), bf16), shape((keys, count), jnp.int32), shape((keys, count), jnp.int32),
        ),
        compiler_params=params(),
        cost_estimate=cost(0),
    )(hidden_row, segment_ids[None], rel_ids, layout_ids)
    steps.leave(pick)

    groups = keys // 8
    whole = pl.BlockSpec((keys, count), lambda p: (0, 0))

    def bias_half(part, table, *given):
        low = part * (PAIRS // 2)
        out = pl.pallas_call(
            functools.partial(bias_kernel, low),
            grid=(PAIRS // 2,),
            in_specs=[pl.BlockSpec((H, 128), lambda p: (0, 0)), whole, whole] + [ANY] * len(given),
            out_specs=pl.BlockSpec((1, groups, 16, count), lambda p: (p + low, 0, 0, 0)),
            out_shape=shape((PAIRS, groups, 16, count), f32),
            input_output_aliases={3: 0} if given else {},
            compiler_params=params(),
            cost_estimate=cost(0),
        )(table, rel_index, lay_index, *given)
        steps.leave(out)
        return out

    smalls_gather.middle(steps)
    down.start(steps)
    down.forward(steps)
    smalls_gather.middle(steps)
    attn_column.middle(steps)
    down.arrive(steps)
    smalls_gather.middle(steps)
    attn.plane(steps, attn_column.finish(steps))
    vectors, table = pl.pallas_call(
        unpack_kernel,
        out_shape=(shape((8, width), f32), shape((H, 128), f32)),
        compiler_params=params(),
        cost_estimate=cost(0),
    )(*smalls_gather.finish(steps))
    gu_columns[0].start(steps)
    bias = bias_half(0, steps.enter(table))
    gu_columns[0].middle(steps)
    bias = bias_half(1, steps.enter(table), bias)
    attn.forward(steps)
    down.columns_start(steps)
    gu_stack = gu_columns[0].finish(steps)
    gu_stack = [gu_stack[:, :, : PARTS[0]], gu_stack[:, :, PARTS[0] :]]
    gu[0].plane(steps, gu_stack[0])
    attn.cross(steps)
    gu[0].settle(steps, 1)
    down.columns_middle(steps)
    attn.arrive(steps)
    attn_pieces = attn.finish(steps)
    attn_sources, attn_places = sources_of(attn_pieces, rows)
    place = steps.enter(where)
    attn_input, query, key, value = call(
        functools.partial(project_kernel, narrow, wide, attn_places),
        [SM] + [VM] * 4 + [ANY] * len(attn_sources),
        [vm((count, width), bf16), vm((count, width), bf16), vm((keys, width), bf16), vm((keys, width), bf16)],
        [pltpu.VMEM((3, width, width), bf16), pltpu.SemaphoreType.DMA((3,))],
        0, place, tokens, hidden_column, pick, vectors, *attn_sources,
    )
    steps.leave(query)
    gu[0].forward(steps)

    row_block = pl.BlockSpec((count, 256), lambda p: (0, p))
    key_block = pl.BlockSpec((keys, 256), lambda p: (0, p))
    turn_block = pl.BlockSpec((256, count), lambda p: (p, 0))
    score_block = pl.BlockSpec((2, groups, 16, count), lambda p: (p, 0, 0, 0))
    query_here = steps.enter(query)
    attended, probs = pl.pallas_call(
        attend_kernel,
        grid=(PAIRS // 2,),
        in_specs=[row_block, key_block, key_block, score_block],
        out_specs=[turn_block, score_block],
        out_shape=(shape((width, count), bf16), shape((PAIRS, groups, 16, count), bf16)),
        compiler_params=params(),
        cost_estimate=cost(0),
    )(query_here, key, value, bias)
    steps.leave(attended)
    place = steps.enter(where)
    residual, ffn_input = call(
        functools.partial(residual_kernel, narrow, wide, attn_places),
        [SM] + [VM] * 4 + [ANY] * len(attn_sources),
        [vm((count, width), f32), vm((count, width), bf16)],
        [pltpu.VMEM((width, width), bf16), pltpu.SemaphoreType.DMA],
        0, place, attended, tokens, hidden_column, vectors, *attn_sources,
    )
    steps.leave(residual)
    down.cores(steps)
    gu[0].arrive(steps)
    gu[1].plane(steps, gu_stack[1])
    down_sources, down_places = sources_of(down.finish(steps), w_down.shape[0])

    acc, active, gu_sums = None, [], []

    def ffn(part, acc, sources, places):
        size = PARTS[part]
        shapes = block_shapes(2, rows, size)
        place = steps.enter(where)
        extra = () if part == 0 else (acc,)
        results = call(
            functools.partial(
                ffn_kernel, narrow, wide, bounds[part],
                (len(sources), len(down_sources), len(shapes)), places, down_places,
            ),
            [SM, VM, VM] + [ANY] * (len(sources) + len(down_sources)) + [VM] * len(extra),
            anys(shapes) + [vm((count, size), bf16), vm((count, width), f32)],
            [
                pltpu.VMEM((2, width, size), bf16), pltpu.VMEM((ff, width), bf16),
                pltpu.VMEM((2, width, size), bf16), pltpu.VMEM((width, count), bf16),
                pltpu.SemaphoreType.DMA((3,)),
            ],
            FFN_COST[part], place, ffn_input, cotangent, *sources, *down_sources, *extra, mib=60,
        )
        act, acc = results[-2:]
        active.append(act)
        steps.leave(acc)
        turn = ((2, 4), (4, 2, True))[part]
        gu_sums.append(scatter(narrow, wide, *blocks_of(results[:-2], 2), *turn))
        return acc

    gu_pieces = [None, None]
    gu_pieces[0] = gu[0].finish(steps)
    acc = ffn(0, acc, *sources_of(gu_pieces[0], rows))
    gu[1].forward(steps)
    gu[1].arrive(steps)
    gu_pieces[1] = gu[1].finish(steps)
    acc = ffn(1, acc, *sources_of(gu_pieces[1], rows))
    gu_sums[0].plane(steps)
    gu_sums[1].plane(steps)

    shapes = block_shapes(1, rows, width)
    if fine:
        down_grad_shapes = [shape((wide // 2, narrow, 2 * w_down.shape[0], half), bf16)] * 2
    else:
        down_grad_shapes = [shape((1, ff, width), bf16)]
    place = steps.enter(where)
    residual_grad, head, ffn_gain_part, output, *grads = call(
        functools.partial(
            turn_kernel, narrow, wide, attn_places, down_places, (len(attn_sources), len(down_sources))
        ),
        [SM] + [VM] * (5 + len(PARTS)) + [ANY] * (len(attn_sources) + len(down_sources)),
        [
            vm((count, width), f32), vm((width, count), bf16), vm((1, width), f32),
            vm((count, width), bf16),
        ] + anys(shapes + down_grad_shapes),
        [
            pltpu.VMEM((width, width), bf16), pltpu.VMEM((width, width), bf16),
            pltpu.VMEM((ff, width), bf16), pltpu.VMEM((ff, width), bf16),
            pltpu.SemaphoreType.DMA((4,)),
        ],
        100, place, residual, acc, cotangent, attended, vectors, *active, *attn_sources, *down_sources,
        mib=60,
    )
    steps.leave(head)
    out_grads, down_grads = grads[: len(shapes)], grads[len(shapes) :]
    out_sum = scatter(narrow, wide, *blocks_of(out_grads, 1), 4, 2, True)
    down_sum = scatter(narrow, wide, *blocks_of(down_grads, 1), joined=True)
    gu_sums[1].forward(steps)
    gu_sums[0].forward(steps)

    query_here = steps.enter(query)
    query_grad, key_grad, value_grad, score_grads = pl.pallas_call(
        attend_back_kernel,
        grid=(PAIRS // 2,),
        in_specs=[row_block, key_block, key_block, turn_block, score_block],
        out_specs=[row_block, key_block, key_block, score_block],
        out_shape=(
            shape((count, width), bf16), shape((keys, width), bf16), shape((keys, width), bf16),
            shape((PAIRS, groups, 16, count), bf16),
        ),
        compiler_params=params(),
        cost_estimate=cost(100),
    )(query_here, key, value, head, probs)
    steps.leave(query_grad)
    out_sum.plane(steps)
    down_sum.plane(steps)

    shapes = block_shapes(3, rows, width)
    place = steps.enter(where)
    key_wide, value_wide, *qkv_grads = call(
        functools.partial(project_grads_kernel, narrow, wide),
        [SM] + [VM] * 5,
        [vm((count, width), bf16), vm((count, width), bf16)] + anys(shapes),
        [
            pltpu.VMEM((3, width, width), bf16), pltpu.VMEM((width, count), bf16),
            pltpu.SemaphoreType.DMA((3,)),
        ],
        100, place, attn_input, pick, query_grad, key_grad, value_grad,
    )
    steps.leave(key_wide)
    qkv_sum = scatter(narrow, wide, *blocks_of(qkv_grads, 3))
    gu_totals = [part.column(steps) for part in reversed(gu_sums)][::-1]
    gu_rows = Rows(steps, narrow, jnp.concatenate(gu_totals, axis=2))
    out_sum.forward(steps)

    place = steps.enter(where)
    tokens_grad, attn_gain_part, embed_part = call(
        functools.partial(project_back_kernel, narrow, wide, attn_places, len(attn_sources)),
        [SM] + [VM] * 7 + [ANY] * len(attn_sources),
        [vm((count, width), f32), vm((1, width), f32), vm((1, width), f32)],
        [pltpu.VMEM((3, width, width), bf16), pltpu.SemaphoreType.DMA((3,))],
        100, place, query_grad, key_wide, value_wide, tokens, hidden_column, vectors, residual_grad,
        *attn_sources,
    )
    steps.leave(tokens_grad)
    qkv_sum.plane(steps)
    down_sum.forward(steps)
    out_rows = Rows(steps, narrow, out_sum.column(steps))
    gu_rows.middle(steps)

    scores_here = steps.enter(score_grads)
    table_grads = pl.pallas_call(
        table_kernel,
        out_shape=shape((NB, 128), f32),
        scratch_shapes=[pltpu.VMEM((NB * 8, H * 8), f32)],
        compiler_params=params(),
        cost_estimate=cost(100),
    )(scores_here, rel_index, lay_index)
    steps.leave(table_grads)
    gu_total = gu_rows.finish(steps)
    out_rows.middle(steps)
    qkv_sum.forward(steps)
    down_rows = Rows(steps, narrow, down_sum.column(steps))
    qkv_sum.settle(steps)
    table_grads = steps.enter(table_grads)[:, :H]
    parts = (attn_gain_part, ffn_gain_part, embed_part, table_grads[:NB_REL], table_grads[NB_REL:])
    parts = jnp.concatenate([v.reshape(devices, -1) for v in parts], axis=1).astype(bf16)
    small_sum = DirectScatter(narrow, wide, *sides(parts[:, None]))
    down_rows.middle(steps)
    qkv_rows = Rows(steps, narrow, qkv_sum.column(steps))
    small_sum.plane(steps)
    small_rows = DirectRows(steps, narrow, small_sum.column(steps))
    qkv_rows.middle(steps)
    small_rows.middle(steps)
    out_total = out_rows.finish(steps)
    down_total = down_rows.finish(steps)
    if fine:
        rows_here = w_down.shape[0]
        mine = lax.dynamic_slice_in_dim(down_total, core * rows_here, rows_here, 0)
        other = lax.dynamic_slice_in_dim(down_total, (1 - core) * rows_here, rows_here, 0)
        other = flip_wide(other, 1, wide)
        down_total = jnp.where(
            core == 0, jnp.concatenate([mine, other], 1), jnp.concatenate([other, mine], 1)
        )
    qkv_total = qkv_rows.finish(steps)
    small_total = small_rows.finish(steps)[0]
    small_out, at = [], 0
    for p in smalls:
        small_out.append(small_total[at : at + p.shape[0]])
        at += p.shape[0]
    return (
        output, tokens_grad, qkv_total[:rows], qkv_total[rows : 2 * rows], qkv_total[2 * rows :],
        out_total, gu_total[:rows], gu_total[rows:], down_total, *small_out,
    )


def solution(mesh):
    both = P(("narrow", "wide"))
    table = P(("narrow", "wide"), None)
    return jax.shard_map(
        local,
        mesh=mesh,
        in_specs=(table, both, both) + (table,) * 9 + (both,) * 5 + (table,),
        out_specs=(table,) * 9 + (both,) * 5,
        check_vma=False,
    )
```

```python
import functools
import math

import jax
import jax.numpy as jnp
import numpy as np
from jax import lax
from jax.experimental import pallas as pl
from jax.experimental.pallas import tpu as pltpu
from jax.sharding import PartitionSpec as P

H = 16
HD = 64
PAIRS = H // 2
NB_REL = 32
NB_LAY = 64
NB = NB_REL + NB_LAY
HIDE = 192
PARTS = (2048, 768)
FFN_COST = (0, 100)
FF_STEP = 1024

eps_norm = 1e-06
neg_large = -1e30
f32 = jnp.float32
bf16 = jnp.bfloat16

NN = (((1,), (0,)), ((), ()))
NT = (((1,), (1,)), ((), ()))
TN = (((0,), (0,)), ((), ()))


def dot(a, b, dims=NN):
    return lax.dot_general(a, b, dims, preferred_element_type=f32)


def params(mib=56):
    return pltpu.CompilerParams(vmem_limit_bytes=mib * 1024 * 1024)


def cost(us):
    return pl.CostEstimate(flops=int(us * 1.5e9), bytes_accessed=0, transcendentals=0)


VM = pl.BlockSpec(memory_space=pltpu.VMEM)
SM = pl.BlockSpec(memory_space=pltpu.SMEM)
ANY = pl.BlockSpec(memory_space=pl.ANY)


def flip_narrow(x, bits, count):
    return lax.ppermute(x, "narrow", [(i, i ^ bits) for i in range(count)])


def narrow_order(count):
    order, bit = [0], count // 2
    while bit:
        order += [at ^ bit for at in order]
        bit //= 2
    return order


def flip_wide(x, bits, count):
    return lax.ppermute(x, "wide", [(i, i ^ bits) for i in range(count)])


class Steps:
    def __init__(self):
        self.last = ()

    def enter(self, *values):
        out = lax.optimization_barrier(tuple(values) + self.last)
        return out[: len(values)] if len(values) > 1 else out[0]

    def leave(self, *values):
        self.last = tuple(values)


class Columns:
    def __init__(self, narrow, x):
        self.narrow, self.stack, self.bit = narrow, x[None], narrow // 2

    def start(self, steps):
        stack = steps.enter(self.stack)
        self.stack, self.sent = stack, flip_narrow(stack, self.bit, self.narrow)

    def middle(self, steps):
        sent = steps.enter(self.sent)
        self.stack = jnp.concatenate([self.stack, sent])
        steps.leave(self.stack)
        self.bit //= 2
        if self.bit:
            self.sent = flip_narrow(self.stack, self.bit, self.narrow)

    def finish(self, steps):
        while self.bit:
            self.middle(steps)
        return self.stack

    def halves(self, steps):
        while self.bit > 1:
            self.middle(steps)
        sent = steps.enter(self.sent)
        steps.leave(sent)
        return self.stack, sent


class Gather:
    def __init__(self, wide, first=2, second=4, direct=False, split=False, halves=False):
        self.wide, self.bits, self.direct = wide, (first, second), direct
        self.split, self.halves = split, halves

    def add(self, array, chip, split=False):
        self.pieces.append((array, 0, chip, 0))
        half = array.shape[0] // 2
        for low in (0, half) if split else (0,):
            part = array[low : low + half] if split else array
            self.crossed.append((flip_wide(part, 1, self.wide), 1, chip, low))

    def plane(self, steps, column):
        column = steps.enter(column)
        steps.leave(column)
        self.near = [flip_wide(column, bit, self.wide) for bit in self.bits]
        if self.direct:
            self.far = [flip_wide(column, 6, self.wide)]
        self.pieces, self.crossed = [], []
        self.add(column, 0)

    def settle(self, steps, at):
        self.near[at] = steps.enter(self.near[at])
        steps.leave(self.near[at])

    def forward(self, steps):
        near, other = steps.enter(*self.near)
        steps.leave(near)
        if not self.direct:
            half = near.shape[0] // 2
            parts = [near[:half], near[half:]] if self.halves else [near]
            self.far = [flip_wide(part, self.bits[1], self.wide) for part in parts]
        self.add(near, self.bits[0] // 2)
        self.add(other, self.bits[1] // 2)

    def cross(self, steps):
        arrays = steps.enter(*[p[0] for p in self.crossed])
        steps.leave(arrays[-1])
        self.crossed = [(a,) + p[1:] for a, p in zip(arrays, self.crossed)]

    def arrive(self, steps):
        if self.halves:
            low = 0
            for far in steps.enter(*self.far):
                steps.leave(far)
                self.pieces.append((far, 0, 3, low))
                self.crossed.append((flip_wide(far, 1, self.wide), 1, 3, low))
                low += far.shape[0]
        else:
            far = steps.enter(self.far[0])
            steps.leave(far)
            self.add(far, 3, self.split)

    def finish(self, steps):
        arrays = steps.enter(*[p[0] for p in self.crossed])
        steps.leave(arrays[-1])
        return self.pieces + [(a,) + p[1:] for a, p in zip(arrays, self.crossed)]


class PlaneFirst:
    def __init__(self, narrow, wide, x):
        self.narrow, self.wide, self.x = narrow, wide, x

    def start(self, steps):
        x = steps.enter(self.x)
        self.x = x
        self.near = [flip_wide(x, bit, self.wide) for bit in (2, 4)]

    def forward(self, steps):
        self.near = steps.enter(*self.near)
        steps.leave(self.near[0])
        self.far = flip_wide(self.near[0], 4, self.wide)

    def arrive(self, steps):
        far = steps.enter(self.far)
        blocks = [self.x, *self.near, far]
        self.columns = [Columns(self.narrow, jnp.stack(blocks))]
        steps.leave(*[c.stack for c in self.columns])

    def columns_start(self, steps):
        for column in self.columns:
            column.start(steps)

    def columns_middle(self, steps):
        for column in self.columns:
            column.middle(steps)

    def cores(self, steps):
        halves = [column.halves(steps) for column in self.columns]
        self.pieces = [
            (part, 0, 2 * n, low) for n, pair in enumerate(halves)
            for part, low in zip(pair, (0, self.narrow // 2))
        ]
        self.crossed = [flip_wide(p[0], 1, self.wide) for p in self.pieces]

    def finish(self, steps):
        crossed = steps.enter(*self.crossed)
        steps.leave(*crossed)
        return self.pieces + [(a, 1) + p[2:] for a, p in zip(crossed, self.pieces)]


class PlainDown(Gather):
    def __init__(self, narrow, wide, x):
        self.column, self.inner = Columns(narrow, x), PlainGather(wide)

    def start(self, steps):
        self.column.start(steps)

    def forward(self, steps):
        pass

    def arrive(self, steps):
        pass

    def columns_start(self, steps):
        pass

    def columns_middle(self, steps):
        pass

    def cores(self, steps):
        self.inner.plane(steps, self.column.finish(steps))
        self.inner.arrive(steps)

    def finish(self, steps):
        return self.inner.finish(steps)


class SmallGather:
    def __init__(self, narrow, wide, x):
        self.narrow, self.wide, self.stack, self.bits = narrow, wide, x[None], []
        bit = 1
        while bit < narrow:
            self.bits.append((flip_narrow, bit, narrow))
            bit *= 2
        bit = 2
        while bit < wide:
            self.bits.append((flip_wide, bit, wide))
            bit *= 2

    def start(self, steps):
        self.stack = steps.enter(self.stack)
        self.send()

    def send(self):
        if self.bits:
            flip, bit, count = self.bits.pop(0)
            self.sent = flip(self.stack, bit, count)
        else:
            self.sent = None

    def middle(self, steps):
        self.stack = jnp.concatenate([self.stack, steps.enter(self.sent)])
        steps.leave(self.stack)
        self.send()
        if self.sent is None:
            self.crossed = flip_wide(self.stack, 1, self.wide)

    def finish(self, steps):
        while self.sent is not None:
            self.middle(steps)
        crossed = steps.enter(self.crossed)
        steps.leave(crossed)
        return [self.stack, crossed]


class PlainGather(Gather):
    def plane(self, steps, column):
        column = steps.enter(column)
        steps.leave(column)
        found = {0: column}
        bit = 2
        while bit < self.wide:
            for at in list(found):
                found[at ^ bit] = flip_wide(found[at], bit, self.wide)
            bit *= 2
        self.pieces, self.crossed = [], []
        for at, array in found.items():
            self.add(array, at // 2)

    def settle(self, steps, at):
        pass

    def cross(self, steps):
        pass

    def forward(self, steps):
        pass

    def arrive(self, steps):
        pass


def ordered(pieces, narrow, wide):
    table = [None] * wide
    for array, core, chip, _ in pieces:
        table[2 * chip + core] = array
    order = jnp.arange(wide) ^ lax.axis_index("wide")
    place = np.argsort(narrow_order(narrow))
    shift = jnp.asarray(place)[jnp.arange(narrow) ^ lax.axis_index("narrow")]
    full = jnp.stack(table, axis=1)[shift[:, None], order[None]]
    return full.reshape((narrow * wide,) + full.shape[2:])


class Scatter:
    def __init__(self, narrow, wide, keep, send, first=2, second=4, joined=False):
        self.narrow, self.wide, self.keep, self.bits = narrow, wide, keep, (first, second)
        self.joined = joined
        self.sent = flip_wide(send, 1, wide)

    def plane(self, steps):
        self.sent = steps.enter(self.sent)
        second = self.bits[1]
        mine = [self.chip(n).astype(bf16) for n in (3, second // 2)]
        if self.joined:
            mine = [jnp.stack(mine)]
        steps.leave(*mine)
        self.away = [flip_wide(part, second, self.wide) for part in mine]

    def chip(self, n):
        return self.keep[n].astype(f32) + self.sent[n].astype(f32)

    def settle(self, steps):
        self.away[1] = steps.enter(self.away[1])
        steps.leave(self.away[1])

    def forward(self, steps):
        if self.joined:
            self.away = list(steps.enter(self.away[0]))
        else:
            self.away[0] = steps.enter(self.away[0])
        first = self.bits[0]
        both = (self.chip(first // 2) + self.away[0].astype(f32)).astype(bf16)
        steps.leave(both)
        self.near = flip_wide(both, first, self.wide)

    def column(self, steps):
        if self.joined:
            near, straight = steps.enter(self.near), self.away[1]
        else:
            near, straight = steps.enter(self.near, self.away[1])
        total = self.chip(0) + straight.astype(f32) + near.astype(f32)
        total = total.astype(bf16)
        steps.leave(total)
        return total


class DirectScatter(Scatter):
    def plane(self, steps):
        sent = steps.enter(self.sent)
        mine = (self.keep.astype(f32) + sent.astype(f32)).astype(bf16)
        steps.leave(mine)
        self.mine = mine
        self.other = [flip_wide(mine[n], 2 * n, self.wide) for n in range(1, self.wide // 2)]

    def column(self, steps):
        other = steps.enter(*self.other)
        total = self.mine[0].astype(f32)
        for part in other:
            total = total + part.astype(f32)
        total = total.astype(bf16)
        steps.leave(total)
        return total


class Rows:
    def __init__(self, steps, narrow, mine):
        self.narrow, self.bit = narrow, 1
        z = lax.axis_index("narrow")
        self.mine = [lax.dynamic_index_in_dim(mine, z ^ n, 0, False) for n in range(narrow)]
        self.send()

    def send(self):
        away = jnp.stack([part for n, part in enumerate(self.mine) if n & 1])
        self.mine = [part for n, part in enumerate(self.mine) if not n & 1]
        self.sent = flip_narrow(away, self.bit, self.narrow)

    def middle(self, steps):
        sent = steps.enter(self.sent)
        self.mine = [part.astype(f32) + sent[n].astype(f32) for n, part in enumerate(self.mine)]
        self.bit *= 2
        if self.bit < self.narrow:
            self.mine = [part.astype(bf16) for part in self.mine]
            steps.leave(*self.mine)
            self.send()
        else:
            steps.leave(self.mine[0])

    def finish(self, steps):
        while self.bit < self.narrow:
            self.middle(steps)
        return self.mine[0]


class DirectRows:
    def __init__(self, steps, narrow, mine):
        z = lax.axis_index("narrow")
        parts = [lax.dynamic_index_in_dim(mine, z ^ n, 0, False) for n in range(narrow)]
        self.own = parts[0]
        self.sent = [flip_narrow(parts[n], n, narrow) for n in range(1, narrow)]

    def middle(self, steps):
        pass

    def finish(self, steps):
        sent = steps.enter(*self.sent)
        total = self.own.astype(f32)
        for part in sent:
            total = total + part.astype(f32)
        steps.leave(total)
        return total


class PlainScatter(Scatter):
    def plane(self, steps):
        sent = steps.enter(self.sent)
        mine = self.keep.astype(f32) + sent.astype(f32)
        bit = self.wide // 2
        while bit > 1:
            half = mine.shape[0] // 2
            low = mine.astype(bf16)
            mine = low[:half].astype(f32) + flip_wide(low[half:], bit, self.wide).astype(f32)
            bit //= 2
        self.total = mine[0].astype(bf16)

    def settle(self, steps):
        pass

    def forward(self, steps):
        pass

    def column(self, steps):
        return self.total


def piece_arrays(pieces):
    return [p[0] for p in pieces]


def piece_places(pieces):
    return [p[1:] for p in pieces]


def load_rows(where, sources, places, index, rows, dst, sem, narrow, wide):
    if places is None:
        pltpu.make_async_copy(sources[0].at[index], dst, sem).start()
        return
    for src, (core, chip, low) in zip(sources, places):
        w = jnp.bitwise_xor(where[1], 2 * chip + core)
        for n, flip in enumerate(narrow_order(narrow)[low : low + src.shape[0]]):
            z = jnp.bitwise_xor(where[0], flip)
            row = pl.multiple_of((z * wide + w) * rows, rows)
            pltpu.make_async_copy(
                src.at[n, pl.ds(index * rows, rows)], dst.at[pl.ds(row, rows), :], sem
            ).start()


def load_pairs(where, sources, places, dst, sem, narrow, wide):
    if places is None:
        pltpu.make_async_copy(sources[0].at[0], dst, sem).start()
        return
    for src, (core, chip, low) in zip(sources, places):
        rows, lanes = src.shape[2:]
        lane = pl.multiple_of(jnp.bitwise_xor(jnp.bitwise_and(where[1], 1), core) * lanes, lanes)
        for n, flip in enumerate(narrow_order(narrow)[low : low + src.shape[0]]):
            z = jnp.bitwise_xor(where[0], flip)
            for flip in range(src.shape[1]):
                c = jnp.bitwise_xor(lax.shift_right_logical(where[1], 1), chip + flip)
                row = pl.multiple_of((z * (wide // 2) + c) * rows, rows)
                pltpu.make_async_copy(
                    src.at[n, flip], dst.at[pl.ds(row, rows), pl.ds(lane, lanes)], sem
                ).start()


def wait_all(ref, sem):
    pltpu.make_async_copy(ref, ref, sem).wait()


def store_rows(where, src, out, index, rows, sem, narrow, wide):
    if len(out) == 1:
        pltpu.make_async_copy(src, out[0].at[index], sem).start()
        return
    core = jnp.bitwise_and(where[1], 1)
    chip = lax.shift_right_logical(where[1], 1)
    for z in range(narrow):
        for c in range(wide // 2):
            flip = jnp.bitwise_xor(chip, c)
            for dst, side in zip(out, (core, 1 - core)):
                row = pl.multiple_of((z * wide + 2 * c + side) * rows, rows)
                pltpu.make_async_copy(
                    src.at[pl.ds(row, rows), :], dst.at[flip, z, pl.ds(index * rows, rows)], sem
                ).start()


def store_pairs(where, src, out, sem, narrow, wide):
    if len(out) == 1:
        pltpu.make_async_copy(src, out[0].at[0], sem).start()
        return
    core = jnp.bitwise_and(where[1], 1)
    chip = lax.shift_right_logical(where[1], 1)
    rows, lanes = out[0].shape[2:]
    for z in range(narrow):
        for c in range(wide // 2):
            flip = jnp.bitwise_xor(chip, c)
            for dst, side in zip(out, (core, 1 - core)):
                lane = pl.multiple_of(side * lanes, lanes)
                pltpu.make_async_copy(
                    src.at[pl.ds((z * (wide // 2) + c) * rows, rows), pl.ds(lane, lanes)],
                    dst.at[flip, z],
                    sem,
                ).start()


def prepare_kernel(hidden_ref, segment_ref, rel_ref, lay_ref, pick_ref, rel_out, lay_out):
    count = hidden_ref.shape[1]
    keys = pick_ref.shape[0]
    seen = hidden_ref[...] == 0
    before = lax.broadcasted_iota(jnp.int32, (count, count), 0)
    after = lax.broadcasted_iota(jnp.int32, (count, count), 1)
    upper = jnp.where(before <= after, 1.0, 0.0).astype(bf16)
    seen_rows = jnp.broadcast_to(jnp.where(seen, 1.0, 0.0), (16, count)).astype(bf16)
    rank = dot(seen_rows, upper)[0:1].astype(jnp.int32) - 1
    rank = jnp.where(seen, rank, -1)
    number = lax.broadcasted_iota(jnp.int32, (keys, count), 0)
    pick = jnp.where(number == rank, 1.0, 0.0).astype(bf16)
    pick_ref[...] = pick
    segment = jnp.broadcast_to(segment_ref[...].astype(f32), (16, count)).astype(bf16)
    key_segment = dot(pick, segment, NT)[:, 0:1]
    valid = key_segment == segment_ref[...].astype(f32)
    rel = dot(pick, rel_ref[...].astype(f32).astype(bf16), NT).astype(jnp.int32)
    lay = dot(pick, lay_ref[...].astype(f32).astype(bf16), NT).astype(jnp.int32)
    rel_out[...] = jnp.where(valid, rel, NB)
    lay_out[...] = lay + NB_REL


def bias_kernel(low, table_ref, rel_ref, lay_ref, *refs):
    out_ref = refs[-1]
    keys, count = rel_ref.shape
    groups = keys // 8
    pair = pl.program_id(0) + low
    tables = [
        jnp.broadcast_to(table_ref[pl.ds(2 * pair + side, 1), :], (keys, 128)) for side in range(2)
    ]
    for c in range(count // 128):
        lanes = slice(c * 128, c * 128 + 128)
        for side in range(2):
            found = jnp.take_along_axis(tables[side], rel_ref[:, lanes], axis=1)
            found = found + jnp.take_along_axis(tables[side], lay_ref[:, lanes], axis=1)
            out_ref[0, :, side * 8 : side * 8 + 8, lanes] = found.reshape(groups, 8, 128)


def embed(tokens_ref, hidden_ref, vectors_ref):
    return jnp.where(hidden_ref[...] == 1.0, vectors_ref[2:3, :], tokens_ref[...].astype(f32))


def inverse_rms(v):
    return lax.rsqrt(jnp.mean(v * v, axis=-1, keepdims=True) + eps_norm)


def pack_kernel(where, wide, lengths, *refs):
    query, key, value, out, gate, up, down, smalls = refs[:8]
    attn_ref, small_ref, first_ref, second_ref = refs[8:12]
    rows = query.shape[0]
    for n, ref in enumerate((query, key, value, out)):
        attn_ref[n * rows : (n + 1) * rows, :] = ref[...].astype(bf16)
    own = where[0] * wide + where[1]
    dims = (8, smalls.shape[1])
    row = lax.broadcasted_iota(jnp.int32, dims, 0)
    lane = lax.broadcasted_iota(jnp.int32, dims, 1)
    spread = jnp.broadcast_to(smalls[...], dims)
    placed = jnp.zeros(dims, f32)
    at = 0
    for n, length in enumerate(lengths):
        part = jnp.where((row == n) & (lane >= at) & (lane < at + length), spread, 0.0)
        placed = placed + pltpu.roll(part, own * length + (dims[1] - at), 1)
        at += length
    small_ref[...] = placed.astype(bf16)
    size = first_ref.shape[1]
    for n, ref in enumerate((gate, up)):
        first_ref[n * rows : (n + 1) * rows, :] = ref[:, 0:size].astype(bf16)
        second_ref[n * rows : (n + 1) * rows, :] = ref[:, size:].astype(bf16)
    if len(refs) == 13:
        refs[12][...] = down[...].astype(bf16)
    else:
        half = down.shape[1] // 2
        core = jnp.bitwise_and(where[1], 1)
        for n, side in enumerate((core, 1 - core)):
            lanes = pl.ds(pl.multiple_of(side * half, half), half)
            refs[12 + n][...] = down[:, lanes].astype(bf16)


def unpack_kernel(left_ref, right_ref, vectors_ref, table_ref):
    width = vectors_ref.shape[1]
    vectors = jnp.sum(left_ref[...].astype(f32), axis=0) + jnp.sum(right_ref[...].astype(f32), axis=0)
    vectors_ref[...] = vectors
    lane = lax.broadcasted_iota(jnp.int32, (H, width), 1)
    head = lax.broadcasted_iota(jnp.int32, (H, width), 0)
    entry = lax.broadcasted_iota(jnp.int32, (width, 128), 0) // H
    bucket = lax.broadcasted_iota(jnp.int32, (width, 128), 1)
    end = lax.broadcasted_iota(jnp.int32, (H, 128), 1)
    table = jnp.where(end >= NB, neg_large, 0.0)
    for n, first in ((3, 0), (4, NB_REL)):
        split = jnp.where(lane % H == head, vectors[n : n + 1], 0.0).astype(bf16)
        spot = jnp.where(entry + first == bucket, 1.0, 0.0).astype(bf16)
        table = table + dot(split, spot)
    table_ref[...] = table


def project_kernel(narrow, wide, places, where, tokens_ref, hidden_ref, pick_ref, vectors_ref, *refs):
    sources = refs[:-6]
    input_ref, query_ref, key_ref, value_ref, weights, sems = refs[-6:]
    width = tokens_ref.shape[1]
    rows = width // (narrow * wide)
    for n in range(3):
        load_rows(where, sources, places, n, rows, weights.at[n], sems.at[n], narrow, wide)
    embedded = embed(tokens_ref, hidden_ref, vectors_ref)
    attn_input = (embedded * inverse_rms(embedded) * vectors_ref[0:1, :]).astype(bf16)
    input_ref[...] = attn_input
    seen = dot(pick_ref[...], attn_input).astype(bf16)
    wait_all(weights.at[0], sems.at[0])
    query_ref[...] = dot(attn_input, weights[0]).astype(bf16)
    wait_all(weights.at[1], sems.at[1])
    key_ref[...] = dot(seen, weights[1]).astype(bf16)
    wait_all(weights.at[2], sems.at[2])
    value_ref[...] = dot(seen, weights[2]).astype(bf16)


def by_side(x):
    keys = x.shape[0]
    wide = x.astype(f32).reshape(keys // 8, 8, 128)
    left = lax.broadcasted_iota(jnp.int32, wide.shape, 2) < HD
    both = jnp.concatenate([jnp.where(left, wide, 0.0), jnp.where(left, 0.0, wide)], axis=1)
    return both.astype(bf16).reshape(keys * 2, 128)


def own_side(x):
    x = x.reshape(x.shape[0] // 16, 16, 128)
    left = lax.broadcasted_iota(jnp.int32, (x.shape[0], 8, 128), 2) < HD
    return jnp.where(left, x[:, 0:8], x[:, 8:16]).reshape(x.shape[0] * 8, 128)


def per_side(x, fold, spread):
    return jnp.concatenate(
        [
            jnp.broadcast_to(fold(x[side * 8 : side * 8 + 8], axis=0, keepdims=True), (8, spread))
            for side in range(2)
        ],
        axis=0,
    )[None]


def attend_kernel(query_ref, key_ref, value_ref, bias_ref, attended_ref, probs_ref):
    count = query_ref.shape[0]
    keys = key_ref.shape[0]
    for n in range(bias_ref.shape[0]):
        lanes = slice(n * 128, n * 128 + 128)
        scores = dot(by_side(key_ref[:, lanes]), query_ref[:, lanes], NT).reshape(keys // 8, 16, count)
        scores = scores + bias_ref[n]
        top = per_side(jnp.max(scores, axis=0), jnp.max, count)
        exponent = jnp.exp(scores - top)
        total = per_side(jnp.sum(exponent, axis=0), jnp.sum, count)
        probs = (exponent * (1.0 / total)).astype(bf16)
        probs_ref[n] = probs
        attended = dot(by_side(value_ref[:, lanes]), probs.reshape(keys * 2, count), TN)
        attended_ref[lanes, :] = attended.astype(bf16)


def residual_kernel(
    narrow, wide, places, where, attended_ref, tokens_ref, hidden_ref, vectors_ref, *refs
):
    sources = refs[:-4]
    residual_ref, input_ref, weight, sem = refs[-4:]
    rows = weight.shape[0] // (narrow * wide)
    load_rows(where, sources, places, 3, rows, weight, sem, narrow, wide)
    embedded = embed(tokens_ref, hidden_ref, vectors_ref)
    wait_all(weight, sem)
    residual = embedded + dot(attended_ref[...], weight[...], TN)
    residual_ref[...] = residual
    input_ref[...] = (residual * inverse_rms(residual) * vectors_ref[1:2, :]).astype(bf16)


def gelu_parts(v):
    scale = math.sqrt(2.0 / math.pi)
    square = v * v
    bend = jnp.tanh(scale * v * (1.0 + 0.044715 * square))
    half = 0.5 * (1.0 + bend)
    slope = half + 0.5 * v * (1.0 - bend * bend) * (scale * (1.0 + 3 * 0.044715 * square))
    return v * half, slope


def ffn_kernel(narrow, wide, low, counts, places, down_places, where, input_ref, cot_ref, *refs):
    sources, refs = refs[: counts[0]], refs[counts[0] :]
    down_sources, refs = refs[: counts[1]], refs[counts[1] :]
    acc_in, refs = (None, refs) if low == 0 else (refs[0], refs[1:])
    out, refs = refs[: counts[2]], refs[counts[2] :]
    active_ref, acc_ref, weights, down_ref, grads, turned, sems = refs
    width = input_ref.shape[1]
    rows = width // (narrow * wide)
    size = active_ref.shape[1]
    for n in range(2):
        load_rows(where, sources, places, n, rows, weights.at[n], sems.at[n], narrow, wide)
    load_pairs(where, down_sources, down_places, down_ref, sems.at[2], narrow, wide)
    x = input_ref[...]
    turned[...] = x.T
    steps = [slice(at, min(at + FF_STEP, size)) for at in range(0, size, FF_STEP)]
    acc = None if acc_in is None else acc_in[...]
    for at, lanes in enumerate(steps):
        if at == 0:
            wait_all(weights.at[0], sems.at[0])
        gate = dot(x, weights[0, :, lanes])
        gelu, slope = gelu_parts(gate)
        if at == 0:
            wait_all(weights.at[1], sems.at[1])
        up = dot(x, weights[1, :, lanes])
        active_ref[:, lanes] = (gelu * up).astype(bf16)
        if at == 0:
            wait_all(down_ref, sems.at[2])
        act_grad = dot(cot_ref[...], down_ref[low + lanes.start : low + lanes.stop, :], NT)
        up_back = (act_grad * gelu).astype(bf16)
        gate_back = (act_grad * up * slope).astype(bf16)
        last = at == len(steps) - 1
        for n, back in ((1, up_back), (0, gate_back)):
            grads[n, :, lanes] = dot(turned[...], back).astype(bf16)
            if last:
                store_rows(where, grads.at[n], out, n, rows, sems.at[n], narrow, wide)
        for n, back in ((1, up_back), (0, gate_back)):
            term = dot(back, weights[n, :, lanes], NT)
            acc = term if acc is None else acc + term
    acc_ref[...] = acc
    for n in range(2):
        wait_all(grads.at[n], sems.at[n])


def turn_kernel(narrow, wide, places, down_places, counts, where, *refs):
    residual_ref, ffn_ref, cot_ref, attended_ref, vectors_ref = refs[:5]
    actives, refs = refs[5 : 5 + len(PARTS)], refs[5 + len(PARTS) :]
    sources, down_sources, refs = refs[: counts[0]], refs[counts[0] : counts[0] + counts[1]], refs[sum(counts) :]
    grad_ref, head_ref, gain_out, output_ref = refs[:4]
    weight, grads, down, down_grads, sems = refs[-5:]
    out, down_out = refs[4:-5][: len(refs[4:-5]) // 2], refs[4:-5][len(refs[4:-5]) // 2 :]
    rows = weight.shape[0] // (narrow * wide)
    load_rows(where, sources, places, 3, rows, weight, sems.at[0], narrow, wide)
    load_pairs(where, down_sources, down_places, down, sems.at[2], narrow, wide)
    cot = cot_ref[...]
    residual = residual_ref[...]
    inverse = inverse_rms(residual)
    normed = residual * inverse
    ffn_grad = ffn_ref[...]
    gain_out[...] = jnp.sum(ffn_grad * normed, axis=0, keepdims=True)
    scaled = ffn_grad * vectors_ref[1:2, :]
    center = jnp.mean(scaled * normed, axis=-1, keepdims=True)
    grad = cot.astype(f32) + (scaled - normed * center) * inverse
    grad_ref[...] = grad
    low = grad.astype(bf16)
    grads[...] = dot(attended_ref[...], low).astype(bf16)
    store_rows(where, grads, out, 0, rows, sems.at[1], narrow, wide)
    at = 0
    for ref in actives:
        down_grads[at : at + ref.shape[1], :] = dot(ref[...], cot, TN).astype(bf16)
        at += ref.shape[1]
    store_pairs(where, down_grads, down_out, sems.at[3], narrow, wide)
    wait_all(weight, sems.at[0])
    head_ref[...] = dot(weight[...], low, NT).astype(bf16)
    wait_all(down, sems.at[2])
    total = residual
    at = 0
    for ref in actives:
        total = total + dot(ref[...], down[at : at + ref.shape[1], :])
        at += ref.shape[1]
    output_ref[...] = total.astype(bf16)
    wait_all(grads, sems.at[1])
    wait_all(down_grads, sems.at[3])


def attend_back_kernel(
    query_ref, key_ref, value_ref, head_ref, probs_ref, query_out, key_out, value_out, scores_ref
):
    count = query_ref.shape[0]
    keys = key_ref.shape[0]
    for n in range(probs_ref.shape[0]):
        lanes = slice(n * 128, n * 128 + 128)
        low = probs_ref[n]
        head = head_ref[lanes, :]
        probs = low.astype(f32)
        prob_grad = dot(by_side(value_ref[:, lanes]), head).reshape(keys // 8, 16, count)
        center = per_side(jnp.sum(probs * prob_grad, axis=0), jnp.sum, count)
        score_grad = (probs * (prob_grad - center)).astype(bf16)
        scores_ref[n] = score_grad
        score_grad = score_grad.reshape(keys * 2, count)
        query_grad = dot(by_side(key_ref[:, lanes]), score_grad, TN)
        query_out[:, lanes] = query_grad.T.astype(bf16)
        key_out[:, lanes] = own_side(dot(score_grad, query_ref[:, lanes])).astype(bf16)
        value_out[:, lanes] = own_side(dot(low.reshape(keys * 2, count), head, NT)).astype(bf16)


def table_kernel(scores_ref, rel_ref, lay_ref, out_ref, total):
    keys, count = rel_ref.shape
    total[...] = jnp.zeros_like(total)

    def step(g, _):
        rows = pl.ds(pl.multiple_of(g * 8, 8), 8)
        hot = []
        for ids, low, high in ((rel_ref[rows, :], 0, NB_REL), (lay_ref[rows, :], NB_REL, NB)):
            for b in range(low, high, 2):
                pair = [jnp.where(ids == b + n, 1.0, 0.0) for n in range(2)]
                hot.append(jnp.concatenate(pair, axis=0).astype(bf16))
        hot = jnp.concatenate(hot, axis=0)
        grads = scores_ref[:, pl.ds(g, 1)].reshape(H * 8, count)
        total[...] += dot(hot, grads, NT)
        return 0

    lax.fori_loop(0, keys // 8, step, 0, unroll=4)
    row = lax.broadcasted_iota(jnp.int32, total.shape, 0) % 8
    lane = lax.broadcasted_iota(jnp.int32, total.shape, 1) % 8
    own = jnp.where(row == lane, total[...], 0.0)
    own = jnp.sum(own.reshape(NB, 8, H * 8), axis=1)
    fold = lax.broadcasted_iota(jnp.int32, (H * 8, 128), 0) // 8
    fold = jnp.where(fold == lax.broadcasted_iota(jnp.int32, (H * 8, 128), 1), 1.0, 0.0)
    out_ref[...] = jnp.dot(own, fold, precision=lax.Precision.HIGHEST, preferred_element_type=f32)


def spread_rows(pick_ref, ref):
    return dot(pick_ref[...], ref[...], TN).astype(bf16)


def project_grads_kernel(
    narrow, wide, where, input_ref, pick_ref, query_ref, key_ref, value_ref, key_out, value_out, *refs
):
    out, (grads, turned, sems) = refs[:-3], refs[-3:]
    rows = turned.shape[0] // (narrow * wide)
    turned[...] = input_ref[...].T
    key_out[...] = spread_rows(pick_ref, key_ref)
    value_out[...] = spread_rows(pick_ref, value_ref)
    for n, ref in enumerate((query_ref, key_out, value_out)):
        grads[n] = dot(turned[...], ref[...]).astype(bf16)
        store_rows(where, grads.at[n], out, n, rows, sems.at[n], narrow, wide)
    for n in range(3):
        wait_all(grads.at[n], sems.at[n])


def project_back_kernel(
    narrow, wide, places, count, where, query_ref, key_ref, value_ref, tokens_ref, hidden_ref,
    vectors_ref, residual_ref, *refs
):
    sources, refs = refs[:count], refs[count:]
    tokens_out, gain_out, embed_out, weights, sems = refs
    rows = weights.shape[1] // (narrow * wide)
    for n in range(3):
        load_rows(where, sources, places, n, rows, weights.at[n], sems.at[n], narrow, wide)
    embedded = embed(tokens_ref, hidden_ref, vectors_ref)
    inverse = inverse_rms(embedded)
    normed = embedded * inverse
    attn_grad = None
    for n, ref in enumerate((query_ref, key_ref, value_ref)):
        wait_all(weights.at[n], sems.at[n])
        term = dot(ref[...], weights[n], NT)
        attn_grad = term if n == 0 else attn_grad + term
    gain_out[...] = jnp.sum(attn_grad * normed, axis=0, keepdims=True)
    scaled = attn_grad * vectors_ref[0:1, :]
    center = jnp.mean(scaled * normed, axis=-1, keepdims=True)
    grad = residual_ref[...] + (scaled - normed * center) * inverse
    concealed = hidden_ref[...] == 1.0
    tokens_out[...] = jnp.where(concealed, 0.0, grad)
    embed_out[...] = jnp.sum(jnp.where(concealed, grad, 0.0), axis=0, keepdims=True)


def shape(dims, kind):
    return jax.ShapeDtypeStruct(tuple(dims), kind)


def local(
    tokens, hidden_patch, segment_ids, rel_ids, layout_ids, w_query, w_key, w_value, w_out, w_gate,
    w_up, w_down, gain_attn, gain_ffn, mask_embed, rel_table, layout_table, cotangent,
):
    narrow, wide = lax.axis_size("narrow"), lax.axis_size("wide")
    devices = narrow * wide
    count, width = tokens.shape
    keys = count - HIDE
    ff = w_gate.shape[1]
    rows = w_query.shape[0]
    where = jnp.stack([lax.axis_index("narrow"), lax.axis_index("wide")]).astype(jnp.int32)
    core = lax.axis_index("wide") % 2

    fine = narrow % 2 == 0 and wide == 8 and rows % 16 == 0 and w_down.shape[0] % 8 == 0
    gather, scatter = (Gather, Scatter) if fine else (PlainGather, PlainScatter)
    steps = Steps()

    def sources_of(pieces, low_rows):
        if fine:
            return piece_arrays(pieces), piece_places(pieces)
        full = ordered(pieces, narrow, wide)
        full = full.reshape((devices, full.shape[1] // low_rows, -1) + full.shape[2:])
        return [jnp.swapaxes(full, 0, 1).reshape(full.shape[1], -1, full.shape[-1])], None

    chip_flip, z_index = jnp.meshgrid(jnp.arange(wide // 2), jnp.arange(narrow), indexing="ij")

    def sides(parts):
        flip = (chip_flip * 2) ^ lax.axis_index("wide")
        return [parts[z_index * wide + (flip ^ side)] for side in range(2)]

    def blocks_of(grads, number):
        if fine:
            return grads
        parts = grads[0].reshape(number, devices, -1, grads[0].shape[-1])
        return sides(jnp.swapaxes(parts, 0, 1).reshape(devices, -1, parts.shape[-1]))

    def block_shapes(number, block_rows, lanes):
        if fine:
            return [shape((wide // 2, narrow, number * block_rows, lanes), bf16)] * 2
        return [shape((number, devices * block_rows, lanes), bf16)]

    def call(kernel, in_specs, outs, scratch, us, *args, mib=56):
        return pl.pallas_call(
            kernel,
            in_specs=in_specs,
            out_specs=[o[0] for o in outs],
            out_shape=[o[1] for o in outs],
            scratch_shapes=scratch,
            compiler_params=params(mib),
            cost_estimate=cost(us),
        )(*args)

    def vm(dims, kind):
        return (VM, shape(dims, kind))

    def anys(shapes):
        return [(ANY, x) for x in shapes]

    smalls = (gain_attn, gain_ffn, mask_embed, rel_table, layout_table)
    lengths = tuple(p.shape[0] for p in smalls)
    small = jnp.concatenate(smalls + (jnp.zeros(width - sum(lengths), f32),))[None]
    bounds = [0, PARTS[0], ff]
    half = width // 2
    down_shapes = [(w_down.shape[0], half)] * 2 if fine else [w_down.shape]
    attn_low, small_low, first_low, second_low, *down_low = pl.pallas_call(
        lambda where_ref, *refs: pack_kernel(where_ref, wide, lengths, *refs),
        in_specs=[SM] + [VM] * 8,
        out_shape=[
            shape(dims, bf16)
            for dims in [(4 * rows, width), (8, width), (2 * rows, PARTS[0]), (2 * rows, PARTS[1])] + down_shapes
        ],
        compiler_params=params(),
        cost_estimate=cost(0),
    )(where, w_query, w_key, w_value, w_out, w_gate, w_up, w_down, small)
    smalls_gather = SmallGather(narrow, wide, small_low)
    attn_column = Columns(narrow, attn_low)
    attn = gather(wide, split=True)
    gu_columns = [Columns(narrow, jnp.concatenate([first_low, second_low], axis=1))]
    gu = [gather(wide, 4, 2, halves=True), gather(wide, direct=True)]
    if fine:
        mine, other = down_low
        other = flip_wide(other, 1, wide)
        down_low = jnp.where(
            core == 0, jnp.concatenate([mine, other]), jnp.concatenate([other, mine])
        )
    else:
        down_low = down_low[0]
    down = (PlaneFirst if fine else PlainDown)(narrow, wide, down_low)

    hidden_column = hidden_patch.astype(f32)[:, None]
    smalls_gather.start(steps)
    attn_column.start(steps)
    steps.leave(attn_low)
    hidden_row = steps.enter(hidden_patch[None])
    pick, rel_index, lay_index = pl.pallas_call(
        prepare_kernel,
        out_shape=(
            shape((keys, count), bf16), shape((keys, count), jnp.int32), shape((keys, count), jnp.int32),
        ),
        compiler_params=params(),
        cost_estimate=cost(0),
    )(hidden_row, segment_ids[None], rel_ids, layout_ids)
    steps.leave(pick)

    groups = keys // 8
    whole = pl.BlockSpec((keys, count), lambda p: (0, 0))

    def bias_half(part, table, *given):
        low = part * (PAIRS // 2)
        out = pl.pallas_call(
            functools.partial(bias_kernel, low),
            grid=(PAIRS // 2,),
            in_specs=[pl.BlockSpec((H, 128), lambda p: (0, 0)), whole, whole] + [ANY] * len(given),
            out_specs=pl.BlockSpec((1, groups, 16, count), lambda p: (p + low, 0, 0, 0)),
            out_shape=shape((PAIRS, groups, 16, count), f32),
            input_output_aliases={3: 0} if given else {},
            compiler_params=params(),
            cost_estimate=cost(0),
        )(table, rel_index, lay_index, *given)
        steps.leave(out)
        return out

    smalls_gather.middle(steps)
    down.start(steps)
    down.forward(steps)
    smalls_gather.middle(steps)
    attn_column.middle(steps)
    down.arrive(steps)
    smalls_gather.middle(steps)
    attn.plane(steps, attn_column.finish(steps))
    vectors, table = pl.pallas_call(
        unpack_kernel,
        out_shape=(shape((8, width), f32), shape((H, 128), f32)),
        compiler_params=params(),
        cost_estimate=cost(0),
    )(*smalls_gather.finish(steps))
    gu_columns[0].start(steps)
    bias = bias_half(0, steps.enter(table))
    gu_columns[0].middle(steps)
    bias = bias_half(1, steps.enter(table), bias)
    attn.forward(steps)
    down.columns_start(steps)
    gu_stack = gu_columns[0].finish(steps)
    gu_stack = [gu_stack[:, :, : PARTS[0]], gu_stack[:, :, PARTS[0] :]]
    steps.leave(*gu_stack)
    gu[0].plane(steps, gu_stack[0])
    attn.cross(steps)
    gu[0].settle(steps, 1)
    down.columns_middle(steps)
    attn.arrive(steps)
    attn_pieces = attn.finish(steps)
    attn_sources, attn_places = sources_of(attn_pieces, rows)
    place = steps.enter(where)
    attn_input, query, key, value = call(
        functools.partial(project_kernel, narrow, wide, attn_places),
        [SM] + [VM] * 4 + [ANY] * len(attn_sources),
        [vm((count, width), bf16), vm((count, width), bf16), vm((keys, width), bf16), vm((keys, width), bf16)],
        [pltpu.VMEM((3, width, width), bf16), pltpu.SemaphoreType.DMA((3,))],
        0, place, tokens, hidden_column, pick, vectors, *attn_sources,
    )
    steps.leave(query)
    gu[0].forward(steps)

    row_block = pl.BlockSpec((count, 256), lambda p: (0, p))
    key_block = pl.BlockSpec((keys, 256), lambda p: (0, p))
    turn_block = pl.BlockSpec((256, count), lambda p: (p, 0))
    score_block = pl.BlockSpec((2, groups, 16, count), lambda p: (p, 0, 0, 0))
    query_here = steps.enter(query)
    attended, probs = pl.pallas_call(
        attend_kernel,
        grid=(PAIRS // 2,),
        in_specs=[row_block, key_block, key_block, score_block],
        out_specs=[turn_block, score_block],
        out_shape=(shape((width, count), bf16), shape((PAIRS, groups, 16, count), bf16)),
        compiler_params=params(),
        cost_estimate=cost(0),
    )(query_here, key, value, bias)
    steps.leave(attended)
    place = steps.enter(where)
    residual, ffn_input = call(
        functools.partial(residual_kernel, narrow, wide, attn_places),
        [SM] + [VM] * 4 + [ANY] * len(attn_sources),
        [vm((count, width), f32), vm((count, width), bf16)],
        [pltpu.VMEM((width, width), bf16), pltpu.SemaphoreType.DMA],
        0, place, attended, tokens, hidden_column, vectors, *attn_sources,
    )
    steps.leave(residual)
    down.cores(steps)
    gu[0].arrive(steps)
    gu[1].plane(steps, gu_stack[1])
    down_sources, down_places = sources_of(down.finish(steps), w_down.shape[0])

    acc, active, gu_sums = None, [], []

    def ffn(part, acc, sources, places):
        size = PARTS[part]
        shapes = block_shapes(2, rows, size)
        place = steps.enter(where)
        extra = () if part == 0 else (acc,)
        results = call(
            functools.partial(
                ffn_kernel, narrow, wide, bounds[part],
                (len(sources), len(down_sources), len(shapes)), places, down_places,
            ),
            [SM, VM, VM] + [ANY] * (len(sources) + len(down_sources)) + [VM] * len(extra),
            anys(shapes) + [vm((count, size), bf16), vm((count, width), f32)],
            [
                pltpu.VMEM((2, width, size), bf16), pltpu.VMEM((ff, width), bf16),
                pltpu.VMEM((2, width, size), bf16), pltpu.VMEM((width, count), bf16),
                pltpu.SemaphoreType.DMA((3,)),
            ],
            FFN_COST[part], place, ffn_input, cotangent, *sources, *down_sources, *extra, mib=60,
        )
        act, acc = results[-2:]
        active.append(act)
        steps.leave(acc)
        turn = ((2, 4), (4, 2, True))[part]
        gu_sums.append(scatter(narrow, wide, *blocks_of(results[:-2], 2), *turn))
        return acc

    gu_pieces = [None, None]
    gu_pieces[0] = gu[0].finish(steps)
    acc = ffn(0, acc, *sources_of(gu_pieces[0], rows))
    gu[1].forward(steps)
    gu[1].arrive(steps)
    gu_pieces[1] = gu[1].finish(steps)
    acc = ffn(1, acc, *sources_of(gu_pieces[1], rows))
    gu_sums[0].plane(steps)
    gu_sums[1].plane(steps)

    shapes = block_shapes(1, rows, width)
    if fine:
        down_grad_shapes = [shape((wide // 2, narrow, 2 * w_down.shape[0], half), bf16)] * 2
    else:
        down_grad_shapes = [shape((1, ff, width), bf16)]
    place = steps.enter(where)
    residual_grad, head, ffn_gain_part, output, *grads = call(
        functools.partial(
            turn_kernel, narrow, wide, attn_places, down_places, (len(attn_sources), len(down_sources))
        ),
        [SM] + [VM] * (5 + len(PARTS)) + [ANY] * (len(attn_sources) + len(down_sources)),
        [
            vm((count, width), f32), vm((width, count), bf16), vm((1, width), f32),
            vm((count, width), bf16),
        ] + anys(shapes + down_grad_shapes),
        [
            pltpu.VMEM((width, width), bf16), pltpu.VMEM((width, width), bf16),
            pltpu.VMEM((ff, width), bf16), pltpu.VMEM((ff, width), bf16),
            pltpu.SemaphoreType.DMA((4,)),
        ],
        100, place, residual, acc, cotangent, attended, vectors, *active, *attn_sources, *down_sources,
        mib=60,
    )
    steps.leave(head)
    out_grads, down_grads = grads[: len(shapes)], grads[len(shapes) :]
    out_sum = scatter(narrow, wide, *blocks_of(out_grads, 1), 4, 2, True)
    down_sum = scatter(narrow, wide, *blocks_of(down_grads, 1), joined=True)
    gu_sums[1].forward(steps)
    gu_sums[0].forward(steps)

    query_here = steps.enter(query)
    query_grad, key_grad, value_grad, score_grads = pl.pallas_call(
        attend_back_kernel,
        grid=(PAIRS // 2,),
        in_specs=[row_block, key_block, key_block, turn_block, score_block],
        out_specs=[row_block, key_block, key_block, score_block],
        out_shape=(
            shape((count, width), bf16), shape((keys, width), bf16), shape((keys, width), bf16),
            shape((PAIRS, groups, 16, count), bf16),
        ),
        compiler_params=params(),
        cost_estimate=cost(100),
    )(query_here, key, value, head, probs)
    steps.leave(query_grad)
    out_sum.plane(steps)
    down_sum.plane(steps)

    shapes = block_shapes(3, rows, width)
    place = steps.enter(where)
    key_wide, value_wide, *qkv_grads = call(
        functools.partial(project_grads_kernel, narrow, wide),
        [SM] + [VM] * 5,
        [vm((count, width), bf16), vm((count, width), bf16)] + anys(shapes),
        [
            pltpu.VMEM((3, width, width), bf16), pltpu.VMEM((width, count), bf16),
            pltpu.SemaphoreType.DMA((3,)),
        ],
        100, place, attn_input, pick, query_grad, key_grad, value_grad,
    )
    steps.leave(key_wide)
    qkv_sum = scatter(narrow, wide, *blocks_of(qkv_grads, 3))
    gu_totals = [part.column(steps) for part in reversed(gu_sums)][::-1]
    gu_rows = Rows(steps, narrow, jnp.concatenate(gu_totals, axis=2))
    out_sum.forward(steps)

    place = steps.enter(where)
    tokens_grad, attn_gain_part, embed_part = call(
        functools.partial(project_back_kernel, narrow, wide, attn_places, len(attn_sources)),
        [SM] + [VM] * 7 + [ANY] * len(attn_sources),
        [vm((count, width), f32), vm((1, width), f32), vm((1, width), f32)],
        [pltpu.VMEM((3, width, width), bf16), pltpu.SemaphoreType.DMA((3,))],
        100, place, query_grad, key_wide, value_wide, tokens, hidden_column, vectors, residual_grad,
        *attn_sources,
    )
    steps.leave(tokens_grad)
    qkv_sum.plane(steps)
    down_sum.forward(steps)
    out_rows = Rows(steps, narrow, out_sum.column(steps))
    gu_rows.middle(steps)

    scores_here = steps.enter(score_grads)
    table_grads = pl.pallas_call(
        table_kernel,
        out_shape=shape((NB, 128), f32),
        scratch_shapes=[pltpu.VMEM((NB * 8, H * 8), f32)],
        compiler_params=params(),
        cost_estimate=cost(100),
    )(scores_here, rel_index, lay_index)
    steps.leave(table_grads)
    gu_total = gu_rows.finish(steps)
    out_rows.middle(steps)
    qkv_sum.forward(steps)
    down_rows = Rows(steps, narrow, down_sum.column(steps))
    qkv_sum.settle(steps)
    table_grads = steps.enter(table_grads)[:, :H]
    parts = (attn_gain_part, ffn_gain_part, embed_part, table_grads[:NB_REL], table_grads[NB_REL:])
    parts = jnp.concatenate([v.reshape(devices, -1) for v in parts], axis=1).astype(bf16)
    small_sum = DirectScatter(narrow, wide, *sides(parts[:, None]))
    down_rows.middle(steps)
    qkv_rows = Rows(steps, narrow, qkv_sum.column(steps))
    small_sum.plane(steps)
    small_rows = DirectRows(steps, narrow, small_sum.column(steps))
    qkv_rows.middle(steps)
    small_rows.middle(steps)
    down_total = down_rows.finish(steps)
    out_total = out_rows.finish(steps)
    if fine:
        rows_here = w_down.shape[0]
        mine = lax.dynamic_slice_in_dim(down_total, core * rows_here, rows_here, 0)
        other = lax.dynamic_slice_in_dim(down_total, (1 - core) * rows_here, rows_here, 0)
        other = flip_wide(other, 1, wide)
        down_total = jnp.where(
            core == 0, jnp.concatenate([mine, other], 1), jnp.concatenate([other, mine], 1)
        )
    qkv_total = qkv_rows.finish(steps)
    small_total = small_rows.finish(steps)[0]
    small_out, at = [], 0
    for p in smalls:
        small_out.append(small_total[at : at + p.shape[0]])
        at += p.shape[0]
    return (
        output, tokens_grad, qkv_total[:rows], qkv_total[rows : 2 * rows], qkv_total[2 * rows :],
        out_total, gu_total[:rows], gu_total[rows:], down_total, *small_out,
    )


def solution(mesh):
    both = P(("narrow", "wide"))
    table = P(("narrow", "wide"), None)
    return jax.shard_map(
        local,
        mesh=mesh,
        in_specs=(table, both, both) + (table,) * 9 + (both,) * 5 + (table,),
        out_specs=(table,) * 9 + (both,) * 5,
        check_vma=False,
    )
```

```python
import functools
import math

import jax
import jax.numpy as jnp
import numpy as np
from jax import lax
from jax.experimental import pallas as pl
from jax.experimental.pallas import tpu as pltpu
from jax.sharding import PartitionSpec as P

H = 16
HD = 64
PAIRS = H // 2
NB_REL = 32
NB_LAY = 64
NB = NB_REL + NB_LAY
HIDE = 192
PARTS = (2048, 768)
FFN_COST = (0, 100)
FF_STEP = 1024

eps_norm = 1e-06
neg_large = -1e30
f32 = jnp.float32
bf16 = jnp.bfloat16

NN = (((1,), (0,)), ((), ()))
NT = (((1,), (1,)), ((), ()))
TN = (((0,), (0,)), ((), ()))


def dot(a, b, dims=NN):
    return lax.dot_general(a, b, dims, preferred_element_type=f32)


def params(mib=56):
    return pltpu.CompilerParams(vmem_limit_bytes=mib * 1024 * 1024)


def cost(us):
    return pl.CostEstimate(flops=int(us * 1.5e9), bytes_accessed=0, transcendentals=0)


VM = pl.BlockSpec(memory_space=pltpu.VMEM)
SM = pl.BlockSpec(memory_space=pltpu.SMEM)
ANY = pl.BlockSpec(memory_space=pl.ANY)


def flip_narrow(x, bits, count):
    return lax.ppermute(x, "narrow", [(i, i ^ bits) for i in range(count)])


def narrow_order(count):
    order, bit = [0], count // 2
    while bit:
        order += [at ^ bit for at in order]
        bit //= 2
    return order


def flip_wide(x, bits, count):
    return lax.ppermute(x, "wide", [(i, i ^ bits) for i in range(count)])


class Steps:
    def __init__(self):
        self.last = ()

    def enter(self, *values):
        out = lax.optimization_barrier(tuple(values) + self.last)
        return out[: len(values)] if len(values) > 1 else out[0]

    def leave(self, *values):
        self.last = tuple(values)


class Columns:
    def __init__(self, narrow, x):
        self.narrow, self.stack, self.bit = narrow, x[None], narrow // 2

    def start(self, steps):
        stack = steps.enter(self.stack)
        self.stack, self.sent = stack, flip_narrow(stack, self.bit, self.narrow)

    def middle(self, steps):
        sent = steps.enter(self.sent)
        self.stack = jnp.concatenate([self.stack, sent])
        steps.leave(self.stack)
        self.bit //= 2
        if self.bit:
            self.sent = flip_narrow(self.stack, self.bit, self.narrow)

    def finish(self, steps):
        while self.bit:
            self.middle(steps)
        return self.stack

    def halves(self, steps):
        while self.bit > 1:
            self.middle(steps)
        sent = steps.enter(self.sent)
        steps.leave(sent)
        return self.stack, sent


class Gather:
    def __init__(self, wide, first=2, second=4, direct=False, split=False, halves=False):
        self.wide, self.bits, self.direct = wide, (first, second), direct
        self.split, self.halves = split, halves

    def add(self, array, chip, split=False):
        self.pieces.append((array, 0, chip, 0))
        half = array.shape[0] // 2
        for low in (0, half) if split else (0,):
            part = array[low : low + half] if split else array
            self.crossed.append((flip_wide(part, 1, self.wide), 1, chip, low))

    def plane(self, steps, column):
        column = steps.enter(column)
        steps.leave(column)
        self.near = [flip_wide(column, bit, self.wide) for bit in self.bits]
        if self.direct:
            self.far = [flip_wide(column, 6, self.wide)]
        self.pieces, self.crossed = [], []
        self.add(column, 0)

    def settle(self, steps, at):
        self.near[at] = steps.enter(self.near[at])
        steps.leave(self.near[at])

    def forward(self, steps):
        near, other = steps.enter(*self.near)
        steps.leave(near)
        if not self.direct:
            half = near.shape[0] // 2
            parts = [near[:half], near[half:]] if self.halves else [near]
            self.far = [flip_wide(part, self.bits[1], self.wide) for part in parts]
        self.add(near, self.bits[0] // 2)
        self.add(other, self.bits[1] // 2)

    def cross(self, steps):
        arrays = steps.enter(*[p[0] for p in self.crossed])
        steps.leave(arrays[-1])
        self.crossed = [(a,) + p[1:] for a, p in zip(arrays, self.crossed)]

    def arrive(self, steps):
        if self.halves:
            low = 0
            for far in steps.enter(*self.far):
                steps.leave(far)
                self.pieces.append((far, 0, 3, low))
                self.crossed.append((flip_wide(far, 1, self.wide), 1, 3, low))
                low += far.shape[0]
        else:
            far = steps.enter(self.far[0])
            steps.leave(far)
            self.add(far, 3, self.split)

    def finish(self, steps):
        arrays = steps.enter(*[p[0] for p in self.crossed])
        steps.leave(arrays[-1])
        return self.pieces + [(a,) + p[1:] for a, p in zip(arrays, self.crossed)]


class PlaneFirst:
    def __init__(self, narrow, wide, x):
        self.narrow, self.wide, self.x = narrow, wide, x

    def start(self, steps):
        x = steps.enter(self.x)
        self.x = x
        self.near = [flip_wide(x, bit, self.wide) for bit in (2, 4)]

    def forward(self, steps):
        self.near = steps.enter(*self.near)
        steps.leave(self.near[0])
        self.far = flip_wide(self.near[0], 4, self.wide)

    def arrive(self, steps):
        far = steps.enter(self.far)
        blocks = [self.x, *self.near, far]
        self.columns = [Columns(self.narrow, jnp.stack(blocks))]
        steps.leave(*[c.stack for c in self.columns])

    def columns_start(self, steps):
        for column in self.columns:
            column.start(steps)

    def columns_middle(self, steps):
        for column in self.columns:
            column.middle(steps)

    def cores(self, steps):
        halves = [column.halves(steps) for column in self.columns]
        self.pieces = [
            (part, 0, 2 * n, low) for n, pair in enumerate(halves)
            for part, low in zip(pair, (0, self.narrow // 2))
        ]
        self.crossed = [flip_wide(p[0], 1, self.wide) for p in self.pieces]

    def finish(self, steps):
        crossed = steps.enter(*self.crossed)
        steps.leave(*crossed)
        return self.pieces + [(a, 1) + p[2:] for a, p in zip(crossed, self.pieces)]


class PlainDown(Gather):
    def __init__(self, narrow, wide, x):
        self.column, self.inner = Columns(narrow, x), PlainGather(wide)

    def start(self, steps):
        self.column.start(steps)

    def forward(self, steps):
        pass

    def arrive(self, steps):
        pass

    def columns_start(self, steps):
        pass

    def columns_middle(self, steps):
        pass

    def cores(self, steps):
        self.inner.plane(steps, self.column.finish(steps))
        self.inner.arrive(steps)

    def finish(self, steps):
        return self.inner.finish(steps)


class SmallGather:
    def __init__(self, narrow, wide, x):
        self.narrow, self.wide, self.stack, self.bits = narrow, wide, x[None], []
        bit = 1
        while bit < narrow:
            self.bits.append((flip_narrow, bit, narrow))
            bit *= 2
        bit = 2
        while bit < wide:
            self.bits.append((flip_wide, bit, wide))
            bit *= 2

    def start(self, steps):
        self.stack = steps.enter(self.stack)
        self.send()

    def send(self):
        if self.bits:
            flip, bit, count = self.bits.pop(0)
            self.sent = flip(self.stack, bit, count)
        else:
            self.sent = None

    def middle(self, steps):
        self.stack = jnp.concatenate([self.stack, steps.enter(self.sent)])
        steps.leave(self.stack)
        self.send()
        if self.sent is None:
            self.crossed = flip_wide(self.stack, 1, self.wide)

    def finish(self, steps):
        while self.sent is not None:
            self.middle(steps)
        crossed = steps.enter(self.crossed)
        steps.leave(crossed)
        return [self.stack, crossed]


class PlainGather(Gather):
    def plane(self, steps, column):
        column = steps.enter(column)
        steps.leave(column)
        found = {0: column}
        bit = 2
        while bit < self.wide:
            for at in list(found):
                found[at ^ bit] = flip_wide(found[at], bit, self.wide)
            bit *= 2
        self.pieces, self.crossed = [], []
        for at, array in found.items():
            self.add(array, at // 2)

    def settle(self, steps, at):
        pass

    def cross(self, steps):
        pass

    def forward(self, steps):
        pass

    def arrive(self, steps):
        pass


def ordered(pieces, narrow, wide):
    table = [None] * wide
    for array, core, chip, _ in pieces:
        table[2 * chip + core] = array
    order = jnp.arange(wide) ^ lax.axis_index("wide")
    place = np.argsort(narrow_order(narrow))
    shift = jnp.asarray(place)[jnp.arange(narrow) ^ lax.axis_index("narrow")]
    full = jnp.stack(table, axis=1)[shift[:, None], order[None]]
    return full.reshape((narrow * wide,) + full.shape[2:])


class Scatter:
    def __init__(self, narrow, wide, keep, send, first=2, second=4, joined=False):
        self.narrow, self.wide, self.keep, self.bits = narrow, wide, keep, (first, second)
        self.joined = joined
        self.sent = flip_wide(send, 1, wide)

    def plane(self, steps):
        self.sent = steps.enter(self.sent)
        second = self.bits[1]
        mine = [self.chip(n).astype(bf16) for n in (3, second // 2)]
        if self.joined:
            mine = [jnp.stack(mine)]
        steps.leave(*mine)
        self.away = [flip_wide(part, second, self.wide) for part in mine]

    def chip(self, n):
        return self.keep[n].astype(f32) + self.sent[n].astype(f32)

    def settle(self, steps):
        self.away[1] = steps.enter(self.away[1])
        steps.leave(self.away[1])

    def forward(self, steps):
        if self.joined:
            self.away = list(steps.enter(self.away[0]))
        else:
            self.away[0] = steps.enter(self.away[0])
        first = self.bits[0]
        both = (self.chip(first // 2) + self.away[0].astype(f32)).astype(bf16)
        steps.leave(both)
        self.near = flip_wide(both, first, self.wide)

    def column(self, steps):
        if self.joined:
            near, straight = steps.enter(self.near), self.away[1]
        else:
            near, straight = steps.enter(self.near, self.away[1])
        total = self.chip(0) + straight.astype(f32) + near.astype(f32)
        total = total.astype(bf16)
        steps.leave(total)
        return total


class DirectScatter(Scatter):
    def plane(self, steps):
        sent = steps.enter(self.sent)
        mine = (self.keep.astype(f32) + sent.astype(f32)).astype(bf16)
        steps.leave(mine)
        self.mine = mine
        self.other = [flip_wide(mine[n], 2 * n, self.wide) for n in range(1, self.wide // 2)]

    def column(self, steps):
        other = steps.enter(*self.other)
        total = self.mine[0].astype(f32)
        for part in other:
            total = total + part.astype(f32)
        total = total.astype(bf16)
        steps.leave(total)
        return total


class Rows:
    def __init__(self, steps, narrow, mine):
        self.narrow, self.bit = narrow, 1
        z = lax.axis_index("narrow")
        self.mine = [lax.dynamic_index_in_dim(mine, z ^ n, 0, False) for n in range(narrow)]
        self.send()

    def send(self):
        away = jnp.stack([part for n, part in enumerate(self.mine) if n & 1])
        self.mine = [part for n, part in enumerate(self.mine) if not n & 1]
        self.sent = flip_narrow(away, self.bit, self.narrow)

    def middle(self, steps):
        sent = steps.enter(self.sent)
        self.mine = [part.astype(f32) + sent[n].astype(f32) for n, part in enumerate(self.mine)]
        self.bit *= 2
        if self.bit < self.narrow:
            self.mine = [part.astype(bf16) for part in self.mine]
            steps.leave(*self.mine)
            self.send()
        else:
            steps.leave(self.mine[0])

    def finish(self, steps):
        while self.bit < self.narrow:
            self.middle(steps)
        return self.mine[0]


class DirectRows:
    def __init__(self, steps, narrow, mine):
        z = lax.axis_index("narrow")
        parts = [lax.dynamic_index_in_dim(mine, z ^ n, 0, False) for n in range(narrow)]
        self.own = parts[0]
        self.sent = [flip_narrow(parts[n], n, narrow) for n in range(1, narrow)]

    def middle(self, steps):
        pass

    def finish(self, steps):
        sent = steps.enter(*self.sent)
        total = self.own.astype(f32)
        for part in sent:
            total = total + part.astype(f32)
        steps.leave(total)
        return total


class PlainScatter(Scatter):
    def plane(self, steps):
        sent = steps.enter(self.sent)
        mine = self.keep.astype(f32) + sent.astype(f32)
        bit = self.wide // 2
        while bit > 1:
            half = mine.shape[0] // 2
            low = mine.astype(bf16)
            mine = low[:half].astype(f32) + flip_wide(low[half:], bit, self.wide).astype(f32)
            bit //= 2
        self.total = mine[0].astype(bf16)

    def settle(self, steps):
        pass

    def forward(self, steps):
        pass

    def column(self, steps):
        return self.total


def piece_arrays(pieces):
    return [p[0] for p in pieces]


def piece_places(pieces):
    return [p[1:] for p in pieces]


def load_rows(where, sources, places, index, rows, dst, sem, narrow, wide):
    if places is None:
        pltpu.make_async_copy(sources[0].at[index], dst, sem).start()
        return
    for src, (core, chip, low) in zip(sources, places):
        w = jnp.bitwise_xor(where[1], 2 * chip + core)
        for n, flip in enumerate(narrow_order(narrow)[low : low + src.shape[0]]):
            z = jnp.bitwise_xor(where[0], flip)
            row = pl.multiple_of((z * wide + w) * rows, rows)
            pltpu.make_async_copy(
                src.at[n, pl.ds(index * rows, rows)], dst.at[pl.ds(row, rows), :], sem
            ).start()


def load_pairs(where, sources, places, dst, sem, narrow, wide):
    if places is None:
        pltpu.make_async_copy(sources[0].at[0], dst, sem).start()
        return
    for src, (core, chip, low) in zip(sources, places):
        rows, lanes = src.shape[2:]
        lane = pl.multiple_of(jnp.bitwise_xor(jnp.bitwise_and(where[1], 1), core) * lanes, lanes)
        for n, flip in enumerate(narrow_order(narrow)[low : low + src.shape[0]]):
            z = jnp.bitwise_xor(where[0], flip)
            for flip in range(src.shape[1]):
                c = jnp.bitwise_xor(lax.shift_right_logical(where[1], 1), chip + flip)
                row = pl.multiple_of((z * (wide // 2) + c) * rows, rows)
                pltpu.make_async_copy(
                    src.at[n, flip], dst.at[pl.ds(row, rows), pl.ds(lane, lanes)], sem
                ).start()


def wait_all(ref, sem):
    pltpu.make_async_copy(ref, ref, sem).wait()


def store_rows(where, src, out, index, rows, sem, narrow, wide, lanes=slice(None)):
    if len(out) == 1:
        pltpu.make_async_copy(src.at[:, lanes], out[0].at[index, :, lanes], sem).start()
        return
    core = jnp.bitwise_and(where[1], 1)
    chip = lax.shift_right_logical(where[1], 1)
    for z in range(narrow):
        for c in range(wide // 2):
            flip = jnp.bitwise_xor(chip, c)
            for dst, side in zip(out, (core, 1 - core)):
                row = pl.multiple_of((z * wide + 2 * c + side) * rows, rows)
                pltpu.make_async_copy(
                    src.at[pl.ds(row, rows), lanes],
                    dst.at[flip, z, pl.ds(index * rows, rows), lanes],
                    sem,
                ).start()


def store_pairs(where, src, out, sem, narrow, wide):
    if len(out) == 1:
        pltpu.make_async_copy(src, out[0].at[0], sem).start()
        return
    core = jnp.bitwise_and(where[1], 1)
    chip = lax.shift_right_logical(where[1], 1)
    rows, lanes = out[0].shape[2:]
    for z in range(narrow):
        for c in range(wide // 2):
            flip = jnp.bitwise_xor(chip, c)
            for dst, side in zip(out, (core, 1 - core)):
                lane = pl.multiple_of(side * lanes, lanes)
                pltpu.make_async_copy(
                    src.at[pl.ds((z * (wide // 2) + c) * rows, rows), pl.ds(lane, lanes)],
                    dst.at[flip, z],
                    sem,
                ).start()


def prepare_kernel(hidden_ref, segment_ref, rel_ref, lay_ref, pick_ref, rel_out, lay_out):
    count = hidden_ref.shape[1]
    keys = pick_ref.shape[0]
    seen = hidden_ref[...] == 0
    before = lax.broadcasted_iota(jnp.int32, (count, count), 0)
    after = lax.broadcasted_iota(jnp.int32, (count, count), 1)
    upper = jnp.where(before <= after, 1.0, 0.0).astype(bf16)
    seen_rows = jnp.broadcast_to(jnp.where(seen, 1.0, 0.0), (16, count)).astype(bf16)
    rank = dot(seen_rows, upper)[0:1].astype(jnp.int32) - 1
    rank = jnp.where(seen, rank, -1)
    number = lax.broadcasted_iota(jnp.int32, (keys, count), 0)
    pick = jnp.where(number == rank, 1.0, 0.0).astype(bf16)
    pick_ref[...] = pick
    segment = jnp.broadcast_to(segment_ref[...].astype(f32), (16, count)).astype(bf16)
    key_segment = dot(pick, segment, NT)[:, 0:1]
    valid = key_segment == segment_ref[...].astype(f32)
    rel = dot(pick, rel_ref[...].astype(f32).astype(bf16), NT).astype(jnp.int32)
    lay = dot(pick, lay_ref[...].astype(f32).astype(bf16), NT).astype(jnp.int32)
    rel_out[...] = jnp.where(valid, rel, NB)
    lay_out[...] = lay + NB_REL


def bias_kernel(low, table_ref, rel_ref, lay_ref, *refs):
    out_ref = refs[-1]
    keys, count = rel_ref.shape
    groups = keys // 8
    pair = pl.program_id(0) + low
    tables = [
        jnp.broadcast_to(table_ref[pl.ds(2 * pair + side, 1), :], (keys, 128)) for side in range(2)
    ]
    for c in range(count // 128):
        lanes = slice(c * 128, c * 128 + 128)
        for side in range(2):
            found = jnp.take_along_axis(tables[side], rel_ref[:, lanes], axis=1)
            found = found + jnp.take_along_axis(tables[side], lay_ref[:, lanes], axis=1)
            out_ref[0, :, side * 8 : side * 8 + 8, lanes] = found.reshape(groups, 8, 128)


def embed(tokens_ref, hidden_ref, vectors_ref):
    return jnp.where(hidden_ref[...] == 1.0, vectors_ref[2:3, :], tokens_ref[...].astype(f32))


def inverse_rms(v):
    return lax.rsqrt(jnp.mean(v * v, axis=-1, keepdims=True) + eps_norm)


def pack_kernel(where, wide, lengths, *refs):
    query, key, value, out, gate, up, down, smalls = refs[:8]
    attn_ref, small_ref, first_ref, second_ref = refs[8:12]
    rows = query.shape[0]
    for n, ref in enumerate((query, key, value, out)):
        attn_ref[n * rows : (n + 1) * rows, :] = ref[...].astype(bf16)
    own = where[0] * wide + where[1]
    dims = (8, smalls.shape[1])
    row = lax.broadcasted_iota(jnp.int32, dims, 0)
    lane = lax.broadcasted_iota(jnp.int32, dims, 1)
    spread = jnp.broadcast_to(smalls[...], dims)
    placed = jnp.zeros(dims, f32)
    at = 0
    for n, length in enumerate(lengths):
        part = jnp.where((row == n) & (lane >= at) & (lane < at + length), spread, 0.0)
        placed = placed + pltpu.roll(part, own * length + (dims[1] - at), 1)
        at += length
    small_ref[...] = placed.astype(bf16)
    size = first_ref.shape[1]
    for n, ref in enumerate((gate, up)):
        first_ref[n * rows : (n + 1) * rows, :] = ref[:, 0:size].astype(bf16)
        second_ref[n * rows : (n + 1) * rows, :] = ref[:, size:].astype(bf16)
    if len(refs) == 13:
        refs[12][...] = down[...].astype(bf16)
    else:
        half = down.shape[1] // 2
        core = jnp.bitwise_and(where[1], 1)
        for n, side in enumerate((core, 1 - core)):
            lanes = pl.ds(pl.multiple_of(side * half, half), half)
            refs[12 + n][...] = down[:, lanes].astype(bf16)


def unpack_kernel(left_ref, right_ref, vectors_ref, table_ref):
    width = vectors_ref.shape[1]
    vectors = jnp.sum(left_ref[...].astype(f32), axis=0) + jnp.sum(right_ref[...].astype(f32), axis=0)
    vectors_ref[...] = vectors
    lane = lax.broadcasted_iota(jnp.int32, (H, width), 1)
    head = lax.broadcasted_iota(jnp.int32, (H, width), 0)
    entry = lax.broadcasted_iota(jnp.int32, (width, 128), 0) // H
    bucket = lax.broadcasted_iota(jnp.int32, (width, 128), 1)
    end = lax.broadcasted_iota(jnp.int32, (H, 128), 1)
    table = jnp.where(end >= NB, neg_large, 0.0)
    for n, first in ((3, 0), (4, NB_REL)):
        split = jnp.where(lane % H == head, vectors[n : n + 1], 0.0).astype(bf16)
        spot = jnp.where(entry + first == bucket, 1.0, 0.0).astype(bf16)
        table = table + dot(split, spot)
    table_ref[...] = table


def project_kernel(narrow, wide, places, where, tokens_ref, hidden_ref, pick_ref, vectors_ref, *refs):
    sources = refs[:-6]
    input_ref, query_ref, key_ref, value_ref, weights, sems = refs[-6:]
    width = tokens_ref.shape[1]
    rows = width // (narrow * wide)
    for n in range(3):
        load_rows(where, sources, places, n, rows, weights.at[n], sems.at[n], narrow, wide)
    embedded = embed(tokens_ref, hidden_ref, vectors_ref)
    attn_input = (embedded * inverse_rms(embedded) * vectors_ref[0:1, :]).astype(bf16)
    input_ref[...] = attn_input
    seen = dot(pick_ref[...], attn_input).astype(bf16)
    wait_all(weights.at[0], sems.at[0])
    query_ref[...] = dot(attn_input, weights[0]).astype(bf16)
    wait_all(weights.at[1], sems.at[1])
    key_ref[...] = dot(seen, weights[1]).astype(bf16)
    wait_all(weights.at[2], sems.at[2])
    value_ref[...] = dot(seen, weights[2]).astype(bf16)


def by_side(x):
    keys = x.shape[0]
    wide = x.astype(f32).reshape(keys // 8, 8, 128)
    left = lax.broadcasted_iota(jnp.int32, wide.shape, 2) < HD
    both = jnp.concatenate([jnp.where(left, wide, 0.0), jnp.where(left, 0.0, wide)], axis=1)
    return both.astype(bf16).reshape(keys * 2, 128)


def own_side(x):
    x = x.reshape(x.shape[0] // 16, 16, 128)
    left = lax.broadcasted_iota(jnp.int32, (x.shape[0], 8, 128), 2) < HD
    return jnp.where(left, x[:, 0:8], x[:, 8:16]).reshape(x.shape[0] * 8, 128)


def per_side(x, fold, spread):
    return jnp.concatenate(
        [
            jnp.broadcast_to(fold(x[side * 8 : side * 8 + 8], axis=0, keepdims=True), (8, spread))
            for side in range(2)
        ],
        axis=0,
    )[None]


def attend_kernel(query_ref, key_ref, value_ref, bias_ref, attended_ref, probs_ref):
    count = query_ref.shape[0]
    keys = key_ref.shape[0]
    for n in range(bias_ref.shape[0]):
        lanes = slice(n * 128, n * 128 + 128)
        scores = dot(by_side(key_ref[:, lanes]), query_ref[:, lanes], NT).reshape(keys // 8, 16, count)
        scores = scores + bias_ref[n]
        top = per_side(jnp.max(scores, axis=0), jnp.max, count)
        exponent = jnp.exp(scores - top)
        total = per_side(jnp.sum(exponent, axis=0), jnp.sum, count)
        probs = (exponent * (1.0 / total)).astype(bf16)
        probs_ref[n] = probs
        attended = dot(by_side(value_ref[:, lanes]), probs.reshape(keys * 2, count), TN)
        attended_ref[lanes, :] = attended.astype(bf16)


def residual_kernel(
    narrow, wide, places, where, attended_ref, tokens_ref, hidden_ref, vectors_ref, *refs
):
    sources = refs[:-4]
    residual_ref, input_ref, weight, sem = refs[-4:]
    rows = weight.shape[0] // (narrow * wide)
    load_rows(where, sources, places, 3, rows, weight, sem, narrow, wide)
    embedded = embed(tokens_ref, hidden_ref, vectors_ref)
    wait_all(weight, sem)
    residual = embedded + dot(attended_ref[...], weight[...], TN)
    residual_ref[...] = residual
    input_ref[...] = (residual * inverse_rms(residual) * vectors_ref[1:2, :]).astype(bf16)


def gelu_parts(v):
    scale = math.sqrt(2.0 / math.pi)
    square = v * v
    bend = jnp.tanh(scale * v * (1.0 + 0.044715 * square))
    half = 0.5 * (1.0 + bend)
    slope = half + 0.5 * v * (1.0 - bend * bend) * (scale * (1.0 + 3 * 0.044715 * square))
    return v * half, slope


def ffn_kernel(narrow, wide, low, counts, places, down_places, where, input_ref, cot_ref, *refs):
    sources, refs = refs[: counts[0]], refs[counts[0] :]
    down_sources, refs = refs[: counts[1]], refs[counts[1] :]
    acc_in, refs = (None, refs) if low == 0 else (refs[0], refs[1:])
    out, refs = refs[: counts[2]], refs[counts[2] :]
    active_ref, acc_ref, weights, down_ref, grads, turned, sems = refs
    width = input_ref.shape[1]
    rows = width // (narrow * wide)
    size = active_ref.shape[1]
    for n in range(2):
        load_rows(where, sources, places, n, rows, weights.at[n], sems.at[n], narrow, wide)
    load_pairs(where, down_sources, down_places, down_ref, sems.at[2], narrow, wide)
    x = input_ref[...]
    turned[...] = x.T
    steps = [slice(at, min(at + FF_STEP, size)) for at in range(0, size, FF_STEP)]
    acc = None if acc_in is None else acc_in[...]
    for at, lanes in enumerate(steps):
        if at == 0:
            wait_all(weights.at[0], sems.at[0])
        gate = dot(x, weights[0, :, lanes])
        gelu, slope = gelu_parts(gate)
        if at == 0:
            wait_all(weights.at[1], sems.at[1])
        up = dot(x, weights[1, :, lanes])
        active_ref[:, lanes] = (gelu * up).astype(bf16)
        if at == 0:
            wait_all(down_ref, sems.at[2])
        act_grad = dot(cot_ref[...], down_ref[low + lanes.start : low + lanes.stop, :], NT)
        up_back = (act_grad * gelu).astype(bf16)
        gate_back = (act_grad * up * slope).astype(bf16)
        for n, back in ((1, up_back), (0, gate_back)):
            grads[n, :, lanes] = dot(turned[...], back).astype(bf16)
            store_rows(where, grads.at[n], out, n, rows, sems.at[n], narrow, wide, lanes)
        for n, back in ((1, up_back), (0, gate_back)):
            term = dot(back, weights[n, :, lanes], NT)
            acc = term if acc is None else acc + term
    acc_ref[...] = acc
    for n in range(2):
        wait_all(grads.at[n], sems.at[n])


def turn_kernel(narrow, wide, places, down_places, counts, where, *refs):
    residual_ref, ffn_ref, cot_ref, attended_ref, vectors_ref = refs[:5]
    actives, refs = refs[5 : 5 + len(PARTS)], refs[5 + len(PARTS) :]
    sources, down_sources, refs = refs[: counts[0]], refs[counts[0] : counts[0] + counts[1]], refs[sum(counts) :]
    grad_ref, head_ref, gain_out, output_ref = refs[:4]
    weight, grads, down, down_grads, sems = refs[-5:]
    out, down_out = refs[4:-5][: len(refs[4:-5]) // 2], refs[4:-5][len(refs[4:-5]) // 2 :]
    rows = weight.shape[0] // (narrow * wide)
    load_rows(where, sources, places, 3, rows, weight, sems.at[0], narrow, wide)
    load_pairs(where, down_sources, down_places, down, sems.at[2], narrow, wide)
    cot = cot_ref[...]
    residual = residual_ref[...]
    inverse = inverse_rms(residual)
    normed = residual * inverse
    ffn_grad = ffn_ref[...]
    gain_out[...] = jnp.sum(ffn_grad * normed, axis=0, keepdims=True)
    scaled = ffn_grad * vectors_ref[1:2, :]
    center = jnp.mean(scaled * normed, axis=-1, keepdims=True)
    grad = cot.astype(f32) + (scaled - normed * center) * inverse
    grad_ref[...] = grad
    low = grad.astype(bf16)
    grads[...] = dot(attended_ref[...], low).astype(bf16)
    store_rows(where, grads, out, 0, rows, sems.at[1], narrow, wide)
    at = 0
    for ref in actives:
        down_grads[at : at + ref.shape[1], :] = dot(ref[...], cot, TN).astype(bf16)
        at += ref.shape[1]
    store_pairs(where, down_grads, down_out, sems.at[3], narrow, wide)
    wait_all(weight, sems.at[0])
    head_ref[...] = dot(weight[...], low, NT).astype(bf16)
    wait_all(down, sems.at[2])
    total = residual
    at = 0
    for ref in actives:
        total = total + dot(ref[...], down[at : at + ref.shape[1], :])
        at += ref.shape[1]
    output_ref[...] = total.astype(bf16)
    wait_all(grads, sems.at[1])
    wait_all(down_grads, sems.at[3])


def attend_back_kernel(
    query_ref, key_ref, value_ref, head_ref, probs_ref, query_out, key_out, value_out, scores_ref
):
    count = query_ref.shape[0]
    keys = key_ref.shape[0]
    for n in range(probs_ref.shape[0]):
        lanes = slice(n * 128, n * 128 + 128)
        low = probs_ref[n]
        head = head_ref[lanes, :]
        probs = low.astype(f32)
        prob_grad = dot(by_side(value_ref[:, lanes]), head).reshape(keys // 8, 16, count)
        center = per_side(jnp.sum(probs * prob_grad, axis=0), jnp.sum, count)
        score_grad = (probs * (prob_grad - center)).astype(bf16)
        scores_ref[n] = score_grad
        score_grad = score_grad.reshape(keys * 2, count)
        query_grad = dot(by_side(key_ref[:, lanes]), score_grad, TN)
        query_out[:, lanes] = query_grad.T.astype(bf16)
        key_out[:, lanes] = own_side(dot(score_grad, query_ref[:, lanes])).astype(bf16)
        value_out[:, lanes] = own_side(dot(low.reshape(keys * 2, count), head, NT)).astype(bf16)


def table_kernel(scores_ref, rel_ref, lay_ref, out_ref, total):
    keys, count = rel_ref.shape
    total[...] = jnp.zeros_like(total)

    def step(g, _):
        rows = pl.ds(pl.multiple_of(g * 8, 8), 8)
        hot = []
        for ids, low, high in ((rel_ref[rows, :], 0, NB_REL), (lay_ref[rows, :], NB_REL, NB)):
            for b in range(low, high, 2):
                pair = [jnp.where(ids == b + n, 1.0, 0.0) for n in range(2)]
                hot.append(jnp.concatenate(pair, axis=0).astype(bf16))
        hot = jnp.concatenate(hot, axis=0)
        grads = scores_ref[:, pl.ds(g, 1)].reshape(H * 8, count)
        total[...] += dot(hot, grads, NT)
        return 0

    lax.fori_loop(0, keys // 8, step, 0, unroll=4)
    row = lax.broadcasted_iota(jnp.int32, total.shape, 0) % 8
    lane = lax.broadcasted_iota(jnp.int32, total.shape, 1) % 8
    own = jnp.where(row == lane, total[...], 0.0)
    own = jnp.sum(own.reshape(NB, 8, H * 8), axis=1)
    fold = lax.broadcasted_iota(jnp.int32, (H * 8, 128), 0) // 8
    fold = jnp.where(fold == lax.broadcasted_iota(jnp.int32, (H * 8, 128), 1), 1.0, 0.0)
    out_ref[...] = jnp.dot(own, fold, precision=lax.Precision.HIGHEST, preferred_element_type=f32)


def spread_rows(pick_ref, ref):
    return dot(pick_ref[...], ref[...], TN).astype(bf16)


def project_grads_kernel(
    narrow, wide, where, input_ref, pick_ref, query_ref, key_ref, value_ref, key_out, value_out, *refs
):
    out, (grads, turned, sems) = refs[:-3], refs[-3:]
    rows = turned.shape[0] // (narrow * wide)
    turned[...] = input_ref[...].T
    key_out[...] = spread_rows(pick_ref, key_ref)
    value_out[...] = spread_rows(pick_ref, value_ref)
    for n, ref in enumerate((query_ref, key_out, value_out)):
        grads[n] = dot(turned[...], ref[...]).astype(bf16)
        store_rows(where, grads.at[n], out, n, rows, sems.at[n], narrow, wide)
    for n in range(3):
        wait_all(grads.at[n], sems.at[n])


def project_back_kernel(
    narrow, wide, places, count, where, query_ref, key_ref, value_ref, tokens_ref, hidden_ref,
    vectors_ref, residual_ref, *refs
):
    sources, refs = refs[:count], refs[count:]
    tokens_out, gain_out, embed_out, weights, sems = refs
    rows = weights.shape[1] // (narrow * wide)
    for n in range(3):
        load_rows(where, sources, places, n, rows, weights.at[n], sems.at[n], narrow, wide)
    embedded = embed(tokens_ref, hidden_ref, vectors_ref)
    inverse = inverse_rms(embedded)
    normed = embedded * inverse
    attn_grad = None
    for n, ref in enumerate((query_ref, key_ref, value_ref)):
        wait_all(weights.at[n], sems.at[n])
        term = dot(ref[...], weights[n], NT)
        attn_grad = term if n == 0 else attn_grad + term
    gain_out[...] = jnp.sum(attn_grad * normed, axis=0, keepdims=True)
    scaled = attn_grad * vectors_ref[0:1, :]
    center = jnp.mean(scaled * normed, axis=-1, keepdims=True)
    grad = residual_ref[...] + (scaled - normed * center) * inverse
    concealed = hidden_ref[...] == 1.0
    tokens_out[...] = jnp.where(concealed, 0.0, grad)
    embed_out[...] = jnp.sum(jnp.where(concealed, grad, 0.0), axis=0, keepdims=True)


def shape(dims, kind):
    return jax.ShapeDtypeStruct(tuple(dims), kind)


def local(
    tokens, hidden_patch, segment_ids, rel_ids, layout_ids, w_query, w_key, w_value, w_out, w_gate,
    w_up, w_down, gain_attn, gain_ffn, mask_embed, rel_table, layout_table, cotangent,
):
    narrow, wide = lax.axis_size("narrow"), lax.axis_size("wide")
    devices = narrow * wide
    count, width = tokens.shape
    keys = count - HIDE
    ff = w_gate.shape[1]
    rows = w_query.shape[0]
    where = jnp.stack([lax.axis_index("narrow"), lax.axis_index("wide")]).astype(jnp.int32)
    core = lax.axis_index("wide") % 2

    fine = narrow % 2 == 0 and wide == 8 and rows % 16 == 0 and w_down.shape[0] % 8 == 0
    gather, scatter = (Gather, Scatter) if fine else (PlainGather, PlainScatter)
    steps = Steps()

    def sources_of(pieces, low_rows):
        if fine:
            return piece_arrays(pieces), piece_places(pieces)
        full = ordered(pieces, narrow, wide)
        full = full.reshape((devices, full.shape[1] // low_rows, -1) + full.shape[2:])
        return [jnp.swapaxes(full, 0, 1).reshape(full.shape[1], -1, full.shape[-1])], None

    chip_flip, z_index = jnp.meshgrid(jnp.arange(wide // 2), jnp.arange(narrow), indexing="ij")

    def sides(parts):
        flip = (chip_flip * 2) ^ lax.axis_index("wide")
        return [parts[z_index * wide + (flip ^ side)] for side in range(2)]

    def blocks_of(grads, number):
        if fine:
            return grads
        parts = grads[0].reshape(number, devices, -1, grads[0].shape[-1])
        return sides(jnp.swapaxes(parts, 0, 1).reshape(devices, -1, parts.shape[-1]))

    def block_shapes(number, block_rows, lanes):
        if fine:
            return [shape((wide // 2, narrow, number * block_rows, lanes), bf16)] * 2
        return [shape((number, devices * block_rows, lanes), bf16)]

    def call(kernel, in_specs, outs, scratch, us, *args, mib=56):
        return pl.pallas_call(
            kernel,
            in_specs=in_specs,
            out_specs=[o[0] for o in outs],
            out_shape=[o[1] for o in outs],
            scratch_shapes=scratch,
            compiler_params=params(mib),
            cost_estimate=cost(us),
        )(*args)

    def vm(dims, kind):
        return (VM, shape(dims, kind))

    def anys(shapes):
        return [(ANY, x) for x in shapes]

    smalls = (gain_attn, gain_ffn, mask_embed, rel_table, layout_table)
    lengths = tuple(p.shape[0] for p in smalls)
    small = jnp.concatenate(smalls + (jnp.zeros(width - sum(lengths), f32),))[None]
    bounds = [0, PARTS[0], ff]
    half = width // 2
    down_shapes = [(w_down.shape[0], half)] * 2 if fine else [w_down.shape]
    attn_low, small_low, first_low, second_low, *down_low = pl.pallas_call(
        lambda where_ref, *refs: pack_kernel(where_ref, wide, lengths, *refs),
        in_specs=[SM] + [VM] * 8,
        out_shape=[
            shape(dims, bf16)
            for dims in [(4 * rows, width), (8, width), (2 * rows, PARTS[0]), (2 * rows, PARTS[1])] + down_shapes
        ],
        compiler_params=params(),
        cost_estimate=cost(0),
    )(where, w_query, w_key, w_value, w_out, w_gate, w_up, w_down, small)
    smalls_gather = SmallGather(narrow, wide, small_low)
    attn_column = Columns(narrow, attn_low)
    attn = gather(wide, split=True)
    gu_columns = [Columns(narrow, jnp.concatenate([first_low, second_low], axis=1))]
    gu = [gather(wide, 4, 2, halves=True), gather(wide, direct=True)]
    if fine:
        mine, other = down_low
        other = flip_wide(other, 1, wide)
        down_low = jnp.where(
            core == 0, jnp.concatenate([mine, other]), jnp.concatenate([other, mine])
        )
    else:
        down_low = down_low[0]
    down = (PlaneFirst if fine else PlainDown)(narrow, wide, down_low)

    hidden_column = hidden_patch.astype(f32)[:, None]
    smalls_gather.start(steps)
    attn_column.start(steps)
    steps.leave(attn_low)
    hidden_row = steps.enter(hidden_patch[None])
    pick, rel_index, lay_index = pl.pallas_call(
        prepare_kernel,
        out_shape=(
            shape((keys, count), bf16), shape((keys, count), jnp.int32), shape((keys, count), jnp.int32),
        ),
        compiler_params=params(),
        cost_estimate=cost(0),
    )(hidden_row, segment_ids[None], rel_ids, layout_ids)
    steps.leave(pick)

    groups = keys // 8
    whole = pl.BlockSpec((keys, count), lambda p: (0, 0))

    def bias_half(part, table, *given):
        low = part * (PAIRS // 2)
        out = pl.pallas_call(
            functools.partial(bias_kernel, low),
            grid=(PAIRS // 2,),
            in_specs=[pl.BlockSpec((H, 128), lambda p: (0, 0)), whole, whole] + [ANY] * len(given),
            out_specs=pl.BlockSpec((1, groups, 16, count), lambda p: (p + low, 0, 0, 0)),
            out_shape=shape((PAIRS, groups, 16, count), f32),
            input_output_aliases={3: 0} if given else {},
            compiler_params=params(),
            cost_estimate=cost(0),
        )(table, rel_index, lay_index, *given)
        steps.leave(out)
        return out

    smalls_gather.middle(steps)
    down.start(steps)
    down.forward(steps)
    smalls_gather.middle(steps)
    attn_column.middle(steps)
    down.arrive(steps)
    smalls_gather.middle(steps)
    attn.plane(steps, attn_column.finish(steps))
    vectors, table = pl.pallas_call(
        unpack_kernel,
        out_shape=(shape((8, width), f32), shape((H, 128), f32)),
        compiler_params=params(),
        cost_estimate=cost(0),
    )(*smalls_gather.finish(steps))
    gu_columns[0].start(steps)
    bias = bias_half(0, steps.enter(table))
    gu_columns[0].middle(steps)
    bias = bias_half(1, steps.enter(table), bias)
    attn.forward(steps)
    down.columns_start(steps)
    gu_stack = gu_columns[0].finish(steps)
    gu_stack = [gu_stack[:, :, : PARTS[0]], gu_stack[:, :, PARTS[0] :]]
    steps.leave(*gu_stack)
    gu[0].plane(steps, gu_stack[0])
    attn.cross(steps)
    gu[0].settle(steps, 1)
    down.columns_middle(steps)
    attn.arrive(steps)
    attn_pieces = attn.finish(steps)
    attn_sources, attn_places = sources_of(attn_pieces, rows)
    place = steps.enter(where)
    attn_input, query, key, value = call(
        functools.partial(project_kernel, narrow, wide, attn_places),
        [SM] + [VM] * 4 + [ANY] * len(attn_sources),
        [vm((count, width), bf16), vm((count, width), bf16), vm((keys, width), bf16), vm((keys, width), bf16)],
        [pltpu.VMEM((3, width, width), bf16), pltpu.SemaphoreType.DMA((3,))],
        0, place, tokens, hidden_column, pick, vectors, *attn_sources,
    )
    steps.leave(query)
    gu[0].forward(steps)

    row_block = pl.BlockSpec((count, 512), lambda p: (0, p))
    key_block = pl.BlockSpec((keys, 512), lambda p: (0, p))
    turn_block = pl.BlockSpec((512, count), lambda p: (p, 0))
    score_block = pl.BlockSpec((4, groups, 16, count), lambda p: (p, 0, 0, 0))
    query_here = steps.enter(query)
    attended, probs = pl.pallas_call(
        attend_kernel,
        grid=(PAIRS // 4,),
        in_specs=[row_block, key_block, key_block, score_block],
        out_specs=[turn_block, score_block],
        out_shape=(shape((width, count), bf16), shape((PAIRS, groups, 16, count), bf16)),
        compiler_params=params(),
        cost_estimate=cost(0),
    )(query_here, key, value, bias)
    steps.leave(attended)
    place = steps.enter(where)
    residual, ffn_input = call(
        functools.partial(residual_kernel, narrow, wide, attn_places),
        [SM] + [VM] * 4 + [ANY] * len(attn_sources),
        [vm((count, width), f32), vm((count, width), bf16)],
        [pltpu.VMEM((width, width), bf16), pltpu.SemaphoreType.DMA],
        0, place, attended, tokens, hidden_column, vectors, *attn_sources,
    )
    steps.leave(residual)
    down.cores(steps)
    gu[0].arrive(steps)
    gu[1].plane(steps, gu_stack[1])
    down_sources, down_places = sources_of(down.finish(steps), w_down.shape[0])

    acc, active, gu_sums = None, [], []

    def ffn(part, acc, sources, places):
        size = PARTS[part]
        shapes = block_shapes(2, rows, size)
        place = steps.enter(where)
        extra = () if part == 0 else (acc,)
        results = call(
            functools.partial(
                ffn_kernel, narrow, wide, bounds[part],
                (len(sources), len(down_sources), len(shapes)), places, down_places,
            ),
            [SM, VM, VM] + [ANY] * (len(sources) + len(down_sources)) + [VM] * len(extra),
            anys(shapes) + [vm((count, size), bf16), vm((count, width), f32)],
            [
                pltpu.VMEM((2, width, size), bf16), pltpu.VMEM((ff, width), bf16),
                pltpu.VMEM((2, width, size), bf16), pltpu.VMEM((width, count), bf16),
                pltpu.SemaphoreType.DMA((3,)),
            ],
            FFN_COST[part], place, ffn_input, cotangent, *sources, *down_sources, *extra, mib=60,
        )
        act, acc = results[-2:]
        active.append(act)
        steps.leave(acc)
        turn = ((2, 4), (4, 2, True))[part]
        gu_sums.append(scatter(narrow, wide, *blocks_of(results[:-2], 2), *turn))
        return acc

    gu_pieces = [None, None]
    gu_pieces[0] = gu[0].finish(steps)
    acc = ffn(0, acc, *sources_of(gu_pieces[0], rows))
    gu[1].forward(steps)
    gu[1].arrive(steps)
    gu_pieces[1] = gu[1].finish(steps)
    acc = ffn(1, acc, *sources_of(gu_pieces[1], rows))
    gu_sums[0].plane(steps)
    gu_sums[1].plane(steps)

    shapes = block_shapes(1, rows, width)
    if fine:
        down_grad_shapes = [shape((wide // 2, narrow, 2 * w_down.shape[0], half), bf16)] * 2
    else:
        down_grad_shapes = [shape((1, ff, width), bf16)]
    place = steps.enter(where)
    residual_grad, head, ffn_gain_part, output, *grads = call(
        functools.partial(
            turn_kernel, narrow, wide, attn_places, down_places, (len(attn_sources), len(down_sources))
        ),
        [SM] + [VM] * (5 + len(PARTS)) + [ANY] * (len(attn_sources) + len(down_sources)),
        [
            vm((count, width), f32), vm((width, count), bf16), vm((1, width), f32),
            vm((count, width), bf16),
        ] + anys(shapes + down_grad_shapes),
        [
            pltpu.VMEM((width, width), bf16), pltpu.VMEM((width, width), bf16),
            pltpu.VMEM((ff, width), bf16), pltpu.VMEM((ff, width), bf16),
            pltpu.SemaphoreType.DMA((4,)),
        ],
        100, place, residual, acc, cotangent, attended, vectors, *active, *attn_sources, *down_sources,
        mib=60,
    )
    steps.leave(head)
    out_grads, down_grads = grads[: len(shapes)], grads[len(shapes) :]
    out_sum = scatter(narrow, wide, *blocks_of(out_grads, 1), 4, 2, True)
    down_sum = scatter(narrow, wide, *blocks_of(down_grads, 1), joined=True)
    gu_sums[1].forward(steps)
    gu_sums[0].forward(steps)

    query_here = steps.enter(query)
    query_grad, key_grad, value_grad, score_grads = pl.pallas_call(
        attend_back_kernel,
        grid=(PAIRS // 4,),
        in_specs=[row_block, key_block, key_block, turn_block, score_block],
        out_specs=[row_block, key_block, key_block, score_block],
        out_shape=(
            shape((count, width), bf16), shape((keys, width), bf16), shape((keys, width), bf16),
            shape((PAIRS, groups, 16, count), bf16),
        ),
        compiler_params=params(),
        cost_estimate=cost(100),
    )(query_here, key, value, head, probs)
    steps.leave(query_grad)
    out_sum.plane(steps)
    down_sum.plane(steps)

    shapes = block_shapes(3, rows, width)
    place = steps.enter(where)
    key_wide, value_wide, *qkv_grads = call(
        functools.partial(project_grads_kernel, narrow, wide),
        [SM] + [VM] * 5,
        [vm((count, width), bf16), vm((count, width), bf16)] + anys(shapes),
        [
            pltpu.VMEM((3, width, width), bf16), pltpu.VMEM((width, count), bf16),
            pltpu.SemaphoreType.DMA((3,)),
        ],
        100, place, attn_input, pick, query_grad, key_grad, value_grad,
    )
    steps.leave(key_wide)
    qkv_sum = scatter(narrow, wide, *blocks_of(qkv_grads, 3))
    gu_totals = [part.column(steps) for part in reversed(gu_sums)][::-1]
    gu_rows = Rows(steps, narrow, jnp.concatenate(gu_totals, axis=2))
    out_sum.forward(steps)

    place = steps.enter(where)
    tokens_grad, attn_gain_part, embed_part = call(
        functools.partial(project_back_kernel, narrow, wide, attn_places, len(attn_sources)),
        [SM] + [VM] * 7 + [ANY] * len(attn_sources),
        [vm((count, width), f32), vm((1, width), f32), vm((1, width), f32)],
        [pltpu.VMEM((3, width, width), bf16), pltpu.SemaphoreType.DMA((3,))],
        100, place, query_grad, key_wide, value_wide, tokens, hidden_column, vectors, residual_grad,
        *attn_sources,
    )
    steps.leave(tokens_grad)
    qkv_sum.plane(steps)
    down_sum.forward(steps)
    out_rows = Rows(steps, narrow, out_sum.column(steps))
    gu_rows.middle(steps)

    scores_here = steps.enter(score_grads)
    table_grads = pl.pallas_call(
        table_kernel,
        out_shape=shape((NB, 128), f32),
        scratch_shapes=[pltpu.VMEM((NB * 8, H * 8), f32)],
        compiler_params=params(),
        cost_estimate=cost(100),
    )(scores_here, rel_index, lay_index)
    steps.leave(table_grads)
    gu_total = gu_rows.finish(steps)
    out_rows.middle(steps)
    qkv_sum.forward(steps)
    down_rows = Rows(steps, narrow, down_sum.column(steps))
    qkv_sum.settle(steps)
    table_grads = steps.enter(table_grads)[:, :H]
    parts = (attn_gain_part, ffn_gain_part, embed_part, table_grads[:NB_REL], table_grads[NB_REL:])
    parts = jnp.concatenate([v.reshape(devices, -1) for v in parts], axis=1).astype(bf16)
    small_sum = DirectScatter(narrow, wide, *sides(parts[:, None]))
    down_rows.middle(steps)
    qkv_rows = Rows(steps, narrow, qkv_sum.column(steps))
    small_sum.plane(steps)
    small_rows = DirectRows(steps, narrow, small_sum.column(steps))
    qkv_rows.middle(steps)
    small_rows.middle(steps)
    down_total = down_rows.finish(steps)
    out_total = out_rows.finish(steps)
    if fine:
        rows_here = w_down.shape[0]
        mine = lax.dynamic_slice_in_dim(down_total, core * rows_here, rows_here, 0)
        other = lax.dynamic_slice_in_dim(down_total, (1 - core) * rows_here, rows_here, 0)
        other = flip_wide(other, 1, wide)
        down_total = jnp.where(
            core == 0, jnp.concatenate([mine, other], 1), jnp.concatenate([other, mine], 1)
        )
    qkv_total = qkv_rows.finish(steps)
    small_total = small_rows.finish(steps)[0]
    small_out, at = [], 0
    for p in smalls:
        small_out.append(small_total[at : at + p.shape[0]])
        at += p.shape[0]
    return (
        output, tokens_grad, qkv_total[:rows], qkv_total[rows : 2 * rows], qkv_total[2 * rows :],
        out_total, gu_total[:rows], gu_total[rows:], down_total, *small_out,
    )


def solution(mesh):
    both = P(("narrow", "wide"))
    table = P(("narrow", "wide"), None)
    return jax.shard_map(
        local,
        mesh=mesh,
        in_specs=(table, both, both) + (table,) * 9 + (both,) * 5 + (table,),
        out_specs=(table,) * 9 + (both,) * 5,
        check_vma=False,
    )
```
